256 devices in a mesh: gx: 8 (over z_hi, x), gz: 32 (over z_lo, y, core).
Axes of the slice: x: 4, y: 4, z: 8 (z_hi: 2, z_lo: 4; z = z_hi * 4 + z_lo), core: 2. Of those that a mesh axis runs over, the one named last changes fastest.
Arguments:
- tokens: bfloat16 [64, 8, 256, 768], P('gx', None, 'gz'), may hold values from -6 to 6
- body_mask: int32 [64, 8, 256], P('gx', None, 'gz'), may hold values 0 or 1
- cotangent: bfloat16 [64, 8, 256, 768], P('gx', None, 'gz'), may hold values from -6 to 6
- input_proj: bfloat16 [768, 1152], replicated, may hold values from -2 to 6
- output_proj: bfloat16 [384, 768], replicated, may hold values from -0.3125 to 0.3125
- coarse_proj: bfloat16 [768, 768], replicated, may hold values from -0.21875 to 0.21875
Outputs:
- block_out: bfloat16 [64, 8, 256, 768], P('gx', None, 'gz')
- token_grad: bfloat16 [64, 8, 256, 768], P('gx', None, 'gz')
- input_grad: float32 [768, 1152], P(('gx', 'gz'))
- output_grad: float32 [384, 768], P(None, ('gx', 'gz'))
- coarse_grad: float32 [768, 768], P(('gx', 'gz'))
The draws below stay inside these ranges and needn't reach their ends.
All inputs are finite; a program needn't handle non-finite values. No bound on the sum of `body_mask` on one device may be relied on, other than what follows from the above.
Results may differ from the reference program's by a relative error of at most 0.015.
The reference program's roundings to bfloat16 on the way count: a program that leaves them out, or rounds other values in their place, can miss the bound.
Values may be sent and summed in bfloat16 or wider, within the bound.
No kernel may reach another device: no remote copies, remote signals or barrier semaphores. Data moves between devices by JAX's collectives and lax.ppermute only.
A program may use at most 128 MiB of HBM per device.

```python
import math
import jax
import jax.numpy as jnp
from jax import lax

D = 768
HEADS = 6
HEAD = 64
INNER = 384
WIN = 8
SHIFT = 4
POOL = 8
NX = 64
NY = 8
NZ = 256
COARSE = 32


def draw_input_proj(key, part):
    inner = HEADS * HEAD
    base = jax.random.normal(key, (D, 3 * inner), jnp.float32) / math.sqrt(D)
    return base.astype(jnp.bfloat16)


def touch_ends(values, rng, low, top_value):
    spot = [jax.random.randint(jax.random.fold_in(rng, axis), (), 0, length) for axis, length in enumerate(values.shape)]
    widest = values.shape.index(max(values.shape))
    next_to = spot[:widest] + [(spot[widest] + 1) % values.shape[widest]] + spot[widest + 1:]
    return values.at[tuple(spot)].set(low).at[tuple(next_to)].set(top_value)


def shard_levels(stream_key, extent, cuts, least, largest):
    def one(position, blocks):
        steps = jax.random.uniform(jax.random.fold_in(jax.random.fold_in(stream_key, 6), position), (blocks,), jnp.float32, least / len(cuts), largest / len(cuts))
        return jnp.repeat(jnp.exp(steps), extent[position] // blocks).reshape((-1,) + (1,) * (len(extent) - position - 1))

    loudness = one(*cuts[0])
    for cut in cuts[1:]:
        loudness = loudness * one(*cut)
    return loudness


def gaussian(stream_key, shape, width, reach, pieces=(), held_as=jnp.bfloat16):
    result = width * jax.random.normal(stream_key, shape, jnp.float32)
    if pieces:
        result = result * shard_levels(stream_key, shape, pieces, -0.22, 0.18)
    return jnp.clip(result, -reach, reach).astype(held_as)


def setup_inputs(seed: int = 0) -> dict:
    keys = jax.random.split(jax.random.key(seed), 7)
    return {
        "tokens": gaussian(keys[0], (NX, NY, NZ, D), 1.0, 6.0, ((0, 8), (2, 32))),
        "body_mask": touch_ends((jax.random.randint(keys[1], (NX, NY, NZ), 0, 4) < 3).astype(jnp.int32), jax.random.fold_in(keys[1], 1), 0, 1),
        "cotangent": gaussian(keys[2], (NX, NY, NZ, D), 1.0, 6.0, ((0, 8), (2, 32))),
        "input_proj": draw_input_proj(jax.random.fold_in(keys[6], 71), 0),
        "output_proj": gaussian(keys[4], (INNER, D), INNER ** -0.5, 0.3125),
        "coarse_proj": gaussian(keys[5], (D, 2 * INNER), D ** -0.5, 0.21875),
    }


def product(form, left, right):
    return jnp.einsum(form, left.astype(jnp.float32), right.astype(jnp.float32))

def normalize(values):
    centre = values - lax.optimization_barrier(jnp.mean(values, axis=-1, keepdims=True))
    inv_std = lax.rsqrt(lax.optimization_barrier(jnp.mean(centre * centre, axis=-1, keepdims=True)) + 1e-05)
    return (centre * inv_std, inv_std)

def norm_backward(normed, inv_std, grad_normed):
    first = lax.optimization_barrier(jnp.mean(grad_normed, axis=-1, keepdims=True))
    second = lax.optimization_barrier(jnp.mean(grad_normed * normed, axis=-1, keepdims=True))
    return inv_std * (grad_normed - first - normed * second)

def window_math(win_tokens, win_mask, coarse_kv, input_proj, output_proj, win_cot):
    windows, length, features = win_tokens.shape
    inner = input_proj.shape[1] // 3
    heads = inner // HEAD
    coarse = coarse_kv.shape[0]
    scaling = 1.0 / math.sqrt(HEAD)
    packed = product('bnd,de->bne', win_tokens, input_proj).astype(jnp.bfloat16)
    packed = packed.reshape(windows, length, 3, heads, HEAD)
    query = packed[:, :, 0]
    keys_win = packed[:, :, 1]
    values_win = packed[:, :, 2]
    keys_far = coarse_kv[:, :inner].reshape(coarse, heads, HEAD)
    values_far = coarse_kv[:, inner:].reshape(coarse, heads, HEAD)
    scores_win = product('bqhe,bkhe->bhqk', query, keys_win) * scaling
    scores_win = jnp.where((win_mask > 0)[:, None, None, :], scores_win, -jnp.inf)
    scores_far = product('bqhe,mhe->bhqm', query, keys_far) * scaling
    row_max = jnp.maximum(lax.optimization_barrier(jnp.max(scores_win, axis=-1)), lax.optimization_barrier(jnp.max(scores_far, axis=-1)))[..., None]
    exp_win = jnp.exp(scores_win - row_max)
    exp_far = jnp.exp(scores_far - row_max)
    normaliser = lax.optimization_barrier(jnp.sum(exp_win, axis=-1, keepdims=True)) + lax.optimization_barrier(jnp.sum(exp_far, axis=-1, keepdims=True))
    prob_win = exp_win / normaliser
    prob_far = exp_far / normaliser
    weight_win = prob_win.astype(jnp.bfloat16)
    weight_far = prob_far.astype(jnp.bfloat16)
    attended = product('bhqk,bkhe->bqhe', weight_win, values_win) + product('bhqm,mhe->bqhe', weight_far, values_far)
    attended = attended.astype(jnp.bfloat16).reshape(windows, length, inner)
    branch = product('bnd,de->bne', attended, output_proj).astype(jnp.bfloat16)
    output_grad = product('bnd,bne->de', attended, win_cot)
    grad_att = product('bne,de->bnd', win_cot, output_proj).astype(jnp.bfloat16)
    grad_att = grad_att.reshape(windows, length, heads, HEAD)
    grad_prob_win = product('bqhe,bkhe->bhqk', grad_att, values_win)
    grad_prob_far = product('bqhe,mhe->bhqm', grad_att, values_far)
    grad_value_win = product('bhqk,bqhe->bkhe', weight_win, grad_att).astype(jnp.bfloat16)
    grad_value_far = product('bhqm,bqhe->mhe', weight_far, grad_att)
    centre = lax.optimization_barrier(jnp.sum(prob_win * grad_prob_win, axis=-1, keepdims=True)) + lax.optimization_barrier(jnp.sum(prob_far * grad_prob_far, axis=-1, keepdims=True))
    grad_score_win = (prob_win * (grad_prob_win - centre) * scaling).astype(jnp.bfloat16)
    grad_score_far = (prob_far * (grad_prob_far - centre) * scaling).astype(jnp.bfloat16)
    grad_query = product('bhqk,bkhe->bqhe', grad_score_win, keys_win) + product('bhqm,mhe->bqhe', grad_score_far, keys_far)
    grad_query = grad_query.astype(jnp.bfloat16)
    grad_key_win = product('bhqk,bqhe->bkhe', grad_score_win, query).astype(jnp.bfloat16)
    grad_key_far = product('bhqm,bqhe->mhe', grad_score_far, query)
    grad_packed = jnp.stack([grad_query, grad_key_win, grad_value_win], axis=2).reshape(windows, length, 3 * inner)
    input_grad = product('bnd,bne->de', win_tokens, grad_packed)
    token_grad = product('bne,de->bnd', grad_packed, input_proj).astype(jnp.bfloat16)
    coarse_grad = jnp.concatenate([grad_key_far.reshape(coarse, inner), grad_value_far.reshape(coarse, inner)], axis=1)
    return (branch, token_grad, input_grad, output_grad, coarse_grad)

def to_windows(array):
    rest = array.shape[3:]
    grid = array.reshape((NX // WIN, WIN, NY // WIN, WIN, NZ // WIN, WIN) + rest)
    order = (0, 2, 4, 1, 3, 5) + tuple(range(6, 6 + len(rest)))
    grid = jnp.transpose(grid, order)
    return grid.reshape((NX // WIN, NY // WIN * (NZ // WIN), WIN * WIN * WIN) + rest)

def from_windows(array):
    rest = array.shape[3:]
    grid = array.reshape((NX // WIN, NY // WIN, NZ // WIN, WIN, WIN, WIN) + rest)
    order = (0, 3, 1, 4, 2, 5) + tuple(range(6, 6 + len(rest)))
    return jnp.transpose(grid, order).reshape((NX, NY, NZ) + rest)

def reference(tokens, body_mask, cotangent, input_proj, output_proj, coarse_proj):
    inner = HEADS * HEAD
    tokens_wide = tokens.astype(jnp.float32)
    normed, inv_std = normalize(tokens_wide)
    normed_bf = normed.astype(jnp.bfloat16)
    pooled = normed.reshape(NX // POOL, POOL, NY // POOL, POOL, NZ // POOL, POOL, D).mean(axis=(1, 3, 5))
    pooled_bf = pooled.astype(jnp.bfloat16)
    pooled_cols = pooled_bf.reshape(NX // WIN, COARSE, D)
    coarse_kv = jnp.dot(pooled_cols.reshape(-1, D), coarse_proj, preferred_element_type=jnp.float32)
    coarse_kv = coarse_kv.astype(jnp.bfloat16).reshape(NX // WIN, COARSE, 2 * inner)
    axes_all = (0, 1, 2)
    moved = (-SHIFT, -SHIFT, -SHIFT)
    win_tokens = to_windows(jnp.roll(normed_bf, moved, axis=axes_all))
    win_mask = to_windows(jnp.roll(body_mask, moved, axis=axes_all))
    win_cot = to_windows(jnp.roll(cotangent, moved, axis=axes_all))

    def column(running, inputs):
        col_tokens, col_mask, col_cot, column_kv = inputs

        def single(partial_sums, window):
            token_one, mask_one, cot_one = window
            branch, grad_tok, part_input, part_output, part_coarse = window_math(token_one[None], mask_one[None], column_kv, input_proj, output_proj, cot_one[None])
            summed = (partial_sums[0] + part_input, partial_sums[1] + part_output, partial_sums[2] + part_coarse)
            return (summed, (branch[0], grad_tok[0]))
        start = (running[0], running[1], jnp.zeros((COARSE, 2 * inner), jnp.float32))
        finals, stacked = lax.scan(single, start, (col_tokens, col_mask, col_cot))
        return ((finals[0], finals[1]), (stacked[0], stacked[1], finals[2]))
    start_sums = (jnp.zeros((D, 3 * inner), jnp.float32), jnp.zeros((inner, D), jnp.float32))
    sums, results = lax.scan(column, start_sums, (win_tokens, win_mask, win_cot, coarse_kv))
    input_grad, output_grad = sums
    branches, grad_windows, grad_coarse = results
    back = (SHIFT, SHIFT, SHIFT)
    branch_grid = jnp.roll(from_windows(branches), back, axis=axes_all)
    grad_window = jnp.roll(from_windows(grad_windows), back, axis=axes_all)
    block_out = (tokens_wide + branch_grid.astype(jnp.float32)).astype(jnp.bfloat16)
    grad_coarse_bf = grad_coarse.astype(jnp.bfloat16).reshape(-1, 2 * inner)
    coarse_grad = jnp.dot(pooled_cols.reshape(-1, D).T, grad_coarse_bf, preferred_element_type=jnp.float32)
    grad_pooled = jnp.dot(grad_coarse_bf, coarse_proj.T, preferred_element_type=jnp.float32)
    grad_pooled = grad_pooled.reshape(NX // POOL, NY // POOL, NZ // POOL, D)
    spread = jnp.repeat(jnp.repeat(jnp.repeat(grad_pooled, POOL, axis=0), POOL, axis=1), POOL, axis=2)
    grad_normed = grad_window.astype(jnp.float32) + spread / float(POOL * POOL * POOL)
    token_grad = (cotangent.astype(jnp.float32) + norm_backward(normed, inv_std, grad_normed)).astype(jnp.bfloat16)
    return (block_out, token_grad, input_grad, output_grad, coarse_grad)
```

```python
import math

import jax
import jax.numpy as jnp
from jax import lax
from jax.sharding import Mesh
from jax.sharding import PartitionSpec as P

HEAD = 64
GX = ("zh", "x")
GZ = ("zl", "y", "core")
ALL = GX + GZ
bf16 = jnp.bfloat16
f32 = jnp.float32


def product(form, left, right):
    return jnp.einsum(form, left, right, preferred_element_type=f32)


def normalize(values):
    centre = values - jnp.mean(values, axis=-1, keepdims=True)
    inv_std = lax.rsqrt(jnp.mean(centre * centre, axis=-1, keepdims=True) + 1e-05)
    return (centre * inv_std, inv_std)


def norm_backward(normed, inv_std, grad_normed):
    first = jnp.mean(grad_normed, axis=-1, keepdims=True)
    second = jnp.mean(grad_normed * normed, axis=-1, keepdims=True)
    return inv_std * (grad_normed - first - normed * second)


def moved(block, dx, dz):
    nx, nz = lax.axis_size(GX), lax.axis_size(GZ)
    route = [
        (a * nz + c, ((a + dx) % nx) * nz + (c + dz) % nz)
        for a in range(nx)
        for c in range(nz)
    ]
    return lax.ppermute(block, ALL, route)


def quads(a):
    rest = a.shape[3:]
    x, y, z = a.shape[:3]
    a = a.reshape((2, x // 2, y, 2, z // 2) + rest)
    a = jnp.moveaxis(a, 3, 1)
    return a.reshape((2, 2, x * y * z // 4) + rest)


def unquads(a, shape):
    x, y, z = shape
    rest = a.shape[3:]
    a = a.reshape((2, 2, x // 2, y, z // 2) + rest)
    a = jnp.moveaxis(a, 1, 3)
    return a.reshape((x, y, z) + rest)


def window_in(q):
    return jnp.concatenate(
        [q[1, 1], moved(q[1, 0], 0, -1), moved(q[0, 1], -1, 0), moved(q[0, 0], -1, -1)], axis=0
    )


def window_out(w):
    n = w.shape[0] // 4
    own, up, right, both = (w[i * n : (i + 1) * n] for i in range(4))
    return jnp.stack(
        [
            jnp.stack([moved(both, 1, 1), moved(right, 1, 0)]),
            jnp.stack([moved(up, 0, 1), own]),
        ]
    )


def gathered(row, axes):
    n = lax.axis_size(axes)
    return lax.all_to_all(jnp.broadcast_to(row, (n,) + row.shape[1:]), axes, 0, 0, tiled=True)


def window_math(win, mask, kv, w_in, g):
    length = win.shape[0]
    inner = w_in.shape[1] // 3
    heads = inner // HEAD
    coarse = kv.shape[0]
    scaling = 1.0 / math.sqrt(HEAD)
    packed = jnp.dot(win, w_in, preferred_element_type=f32).astype(bf16)
    packed = packed.reshape(length, 3, heads, HEAD)
    query, key_w, val_w = packed[:, 0], packed[:, 1], packed[:, 2]
    far = kv.reshape(coarse, 2, heads, HEAD)
    keys = jnp.concatenate([key_w, far[:, 0]], axis=0)
    vals = jnp.concatenate([val_w, far[:, 1]], axis=0)
    live = jnp.concatenate([mask > 0, jnp.ones((coarse,), bool)])
    scores = product("qhe,khe->hqk", query, keys) * scaling
    scores = jnp.where(live[None, None, :], scores, -jnp.inf)
    e = jnp.exp(scores - jnp.max(scores, axis=-1, keepdims=True))
    prob = e / jnp.sum(e, axis=-1, keepdims=True)
    weight = prob.astype(bf16)
    attended = product("hqk,khe->qhe", weight, vals).astype(bf16).reshape(length, inner)
    g = g.reshape(length, heads, HEAD)
    grad_prob = product("qhe,khe->hqk", g, vals)
    grad_val = product("hqk,qhe->khe", weight, g)
    centre = jnp.sum(prob * grad_prob, axis=-1, keepdims=True)
    grad_score = (prob * (grad_prob - centre) * scaling).astype(bf16)
    grad_query = product("hqk,khe->qhe", grad_score, keys)
    grad_key = product("hqk,qhe->khe", grad_score, query)
    grad_packed = jnp.concatenate(
        [
            grad_query.reshape(length, inner),
            grad_key[:length].reshape(length, inner),
            grad_val[:length].reshape(length, inner),
        ],
        axis=1,
    ).astype(bf16)
    input_part = product("nd,ne->de", win, grad_packed)
    grad_win = product("ne,de->nd", grad_packed, w_in).astype(bf16)
    coarse_part = jnp.concatenate(
        [grad_key[length:].reshape(coarse, inner), grad_val[length:].reshape(coarse, inner)], axis=1
    )
    return attended, grad_win, input_part, coarse_part


def body(tokens, body_mask, cotangent, w_in, w_out, w_coarse):
    cells = tokens.shape[:3]
    size = cells[0] * cells[1] * cells[2]
    features = tokens.shape[3]
    inner = w_out.shape[0]
    devices = lax.axis_size(ALL)
    flat = lax.axis_index(ALL)
    per = features // devices

    tok = quads(tokens)
    win_raw = window_in(tok)
    cot = quads(cotangent)
    g_own = product("abnd,ed->abne", cot, w_out).astype(bf16)
    win_g = window_in(g_own)
    win_mask = window_in(quads(body_mask))

    wide = tok.astype(f32)
    normed, inv_std = normalize(wide)
    pooled_bf = normed.mean(axis=(0, 1, 2))[None].astype(bf16)
    own_kv = jnp.dot(pooled_bf, w_coarse, preferred_element_type=f32).astype(bf16)
    kv = gathered(own_kv, GZ)
    pooled_all = gathered(pooled_bf, ALL)

    win = normalize(win_raw.astype(f32))[0].astype(bf16)
    att, grad_win, input_part, coarse_part = window_math(win, win_mask, kv, w_in, win_g)

    att_own = window_out(att)
    grad_own = window_out(grad_win)
    branch = product("abne,ed->abnd", att_own, w_out).astype(bf16)
    block_out = unquads((wide + branch.astype(f32)).astype(bf16), cells)
    output_part = product("abnd,abne->de", cot, att_own)

    own_coarse = lax.all_to_all(coarse_part.astype(bf16), GZ, 0, 0, tiled=True)
    own_coarse = jnp.sum(own_coarse.astype(f32), axis=0, keepdims=True).astype(bf16)
    grad_all = gathered(own_coarse, ALL)
    grad_pooled = product("me,de->md", own_coarse, w_coarse) / float(size)
    grad_normed = grad_own.astype(f32) + grad_pooled
    token_grad = (cot.astype(f32) + norm_backward(normed, inv_std, grad_normed)).astype(bf16)
    token_grad = unquads(token_grad, cells)

    columns = lax.dynamic_slice_in_dim(pooled_all, flat * per, per, axis=1)
    coarse_grad = product("md,me->de", columns, grad_all)

    parts = jnp.concatenate([input_part, output_part], axis=1)
    parts = parts.reshape(devices // 2, 2, per, 4 * inner)
    core = lax.axis_index("core")
    keep = lax.dynamic_index_in_dim(parts, core, axis=1, keepdims=False)
    send = lax.dynamic_index_in_dim(parts, 1 - core, axis=1, keepdims=False)
    other = lax.ppermute(send.astype(bf16), "core", [(0, 1), (1, 0)])
    half = (keep + other.astype(f32)).astype(bf16)
    got = lax.all_to_all(half, GX + ("zl", "y"), 0, 0)
    summed = jnp.sum(got.astype(f32), axis=0)
    input_grad = summed[:, : 3 * inner]
    output_grad = summed[:, 3 * inner :].T
    return (block_out, token_grad, input_grad, output_grad, coarse_grad)


def solution(mesh):
    fine = Mesh(mesh.devices.reshape(2, 4, 4, 4, 2), ALL)
    grid = P(GX, None, GZ, None)
    return jax.shard_map(
        body,
        mesh=fine,
        in_specs=(grid, P(GX, None, GZ), grid, P(), P(), P()),
        out_specs=(grid, grid, P(ALL, None), P(None, ALL), P(ALL, None)),
        check_vma=False,
    )
```

```python
import functools

import jax
import jax.numpy as jnp
from jax import lax
from jax.experimental import pallas as pl
from jax.experimental.pallas import tpu as pltpu
from jax.sharding import Mesh
from jax.sharding import PartitionSpec as P

HEAD = 64
PAIR = 2 * HEAD
CHUNK = 256
HIDDEN = -1e30
GX = ("zh", "x")
GZ = ("zl", "y", "core")
ALL = GX + GZ
bf16 = jnp.bfloat16
f32 = jnp.float32


def dot(left, right):
    return jnp.dot(left, right, preferred_element_type=f32)


def dot_nt(left, right):
    return lax.dot_general(left, right, (((1,), (1,)), ((), ())), preferred_element_type=f32)


def call(kernel, outs, *args, scratch=(), flops=0, size=0):
    return pl.pallas_call(
        kernel,
        out_shape=[jax.ShapeDtypeStruct(s, d) for s, d in outs],
        scratch_shapes=list(scratch),
        compiler_params=pltpu.CompilerParams(vmem_limit_bytes=40 * 2**20),
        cost_estimate=pl.CostEstimate(flops=flops, bytes_accessed=size, transcendentals=0),
    )(*args)


def normalize(values):
    centre = values - jnp.mean(values, axis=-1, keepdims=True)
    inv_std = lax.rsqrt(jnp.mean(centre * centre, axis=-1, keepdims=True) + 1e-05)
    return centre * inv_std, inv_std


def low_rows(shape):
    return lax.broadcasted_iota(jnp.int32, shape, 1) < shape[1] // 2


def split_z(rows):
    m, z, d = rows.shape[0] // 2, rows.shape[1], rows.shape[2]
    pairs = rows.reshape(m, 2, z, d)
    a, b = pairs[:, 0], pairs[:, 1]
    low = low_rows(a.shape)
    lower = jnp.where(low, a, pltpu.roll(b, z // 2, 1))
    upper = jnp.where(low, pltpu.roll(a, z // 2, 1), b)
    return lower.reshape(m * z, d), upper.reshape(m * z, d)


def join_z(lower, upper):
    m, d = lower.shape[0] // 8, lower.shape[1]
    lower, upper = lower.reshape(m, 8, d), upper.reshape(m, 8, d)
    low = low_rows(lower.shape)
    a = jnp.where(low, lower, pltpu.roll(upper, 4, 1))
    b = jnp.where(low, pltpu.roll(lower, 4, 1), upper)
    return jnp.stack([a, b], axis=1).reshape(2 * m, 8, d)


def x_half(ref, half):
    x, y, z, d = ref.shape
    rows = ref[half * (x // 2) : (half + 1) * (x // 2)].astype(f32)
    return rows.reshape(x // 2 * y, z, d)


def prepare(tok_ref, cot_ref, wo_ref, wc_ref, both_ref, right_ref, up_ref, own_ref, coarse_ref):
    d = tok_ref.shape[3]
    total = jnp.zeros((1, d), f32)
    cells = 1
    for n in tok_ref.shape[:3]:
        cells *= n
    for half, refs in ((0, (both_ref, right_ref)), (1, (up_ref, own_ref))):
        normed, _ = normalize(x_half(tok_ref, half))
        total += jnp.sum(jnp.sum(normed, axis=0), axis=0, keepdims=True)
        for ref, part in zip(refs, split_z(normed)):
            ref[:, :d] = part.astype(bf16)
        for ref, part in zip(refs, split_z(x_half(cot_ref, half))):
            ref[:, d:] = dot_nt(part.astype(bf16), wo_ref[...]).astype(bf16)
    pooled = jnp.broadcast_to((total / cells).astype(bf16), (coarse_ref.shape[0], d))
    coarse_ref[:, :d] = pooled
    coarse_ref[:, d:] = dot(pooled, wc_ref[...]).astype(bf16)


def turn_cot(cot_ref, src_ref, out_ref):
    d = cot_ref.shape[3]
    parts = []
    for half in (0, 1):
        parts += [p.astype(bf16) for p in split_z(x_half(cot_ref, half))]
    perm = picks(src_ref, d)
    n = parts[0].shape[0]
    for i, part in enumerate(parts):
        out_ref[:, i * n : (i + 1) * n] = dot_nt(perm, part).astype(bf16)


def picks(src_ref, d):
    columns = lax.broadcasted_iota(jnp.int32, (d, d), 1)
    return jnp.where(columns == src_ref[...], 1.0, 0.0).astype(bf16)


def head_of(pair, half):
    lanes = lax.broadcasted_iota(jnp.int32, pair.shape, 1)
    return jnp.where((lanes < HEAD) == (half == 0), pair, jnp.zeros_like(pair))


def attend(own_ref, up_ref, right_ref, both_ref, wi_ref, kv_ref, mask_ref,
           a0_ref, a1_ref, a2_ref, a3_ref, q_ref, k_ref, v_ref, m_ref, l_ref, out_ref):
    d, width = wi_ref.shape
    inner = width // 3
    n = own_ref.shape[0]
    tokens = 4 * n
    for i, ref in enumerate((own_ref, up_ref, right_ref, both_ref)):
        packed = dot(ref[:, :d], wi_ref[...])
        rows = slice(i * n, (i + 1) * n)
        q_ref[rows] = packed[:, :inner].astype(bf16) * bf16(0.125)
        k_ref[rows] = packed[:, inner : 2 * inner].astype(bf16)
        v_ref[rows] = packed[:, 2 * inner :].astype(bf16)
    k_ref[tokens:] = kv_ref[:, d : d + inner]
    v_ref[tokens:] = kv_ref[:, d + inner :]
    eye = jnp.where(
        lax.broadcasted_iota(jnp.int32, (PAIR, PAIR), 0)
        == lax.broadcasted_iota(jnp.int32, (PAIR, PAIR), 1), 1.0, 0.0).astype(bf16)
    chunks = tokens // CHUNK
    m_ref[...] = jnp.zeros_like(m_ref)
    l_ref[...] = jnp.zeros_like(l_ref)

    def step(i, _):
        lanes = pl.ds(pl.multiple_of(i // chunks * PAIR, PAIR), PAIR)
        rows = pl.ds(pl.multiple_of(i % chunks * CHUNK, CHUNK), CHUNK)
        keys = k_ref[:, lanes]
        vals_t = dot_nt(eye, v_ref[:, lanes]).astype(bf16)
        query = q_ref[rows, lanes]
        found = []
        for half in range(2):
            s = dot_nt(keys, head_of(query, half)) + mask_ref[...]
            top = jnp.max(s, axis=0, keepdims=True)
            e = jnp.exp(s - top)
            inv = 1.0 / jnp.sum(e, axis=0, keepdims=True)
            weight = (e * inv).astype(bf16)
            found.append(dot(vals_t[half * HEAD : (half + 1) * HEAD], weight))
            m_ref[pl.ds(2 * i + half, 1)] = top
            l_ref[pl.ds(2 * i + half, 1)] = inv
        out_ref[rows, lanes] = jnp.concatenate(found, axis=0).T.astype(bf16)
        return 0

    lax.fori_loop(0, inner // PAIR * chunks, step, 0)
    for i, ref in enumerate((a0_ref, a1_ref, a2_ref, a3_ref)):
        ref[...] = out_ref[i * n : (i + 1) * n]


def attend_back(own_ref, up_ref, right_ref, both_ref, wi_ref, mask_ref, q_ref, k_ref, v_ref, m_ref, l_ref,
                d0_ref, d1_ref, d2_ref, d3_ref, grad_ref, coarse_ref, g_ref, dk_ref, dv_ref):
    d, width = wi_ref.shape
    inner = width // 3
    n = own_ref.shape[0]
    tokens = 4 * n
    for i, ref in enumerate((own_ref, up_ref, right_ref, both_ref)):
        g_ref[i * n : (i + 1) * n] = ref[:, d:]
    eye = jnp.where(
        lax.broadcasted_iota(jnp.int32, (PAIR, PAIR), 0)
        == lax.broadcasted_iota(jnp.int32, (PAIR, PAIR), 1), 1.0, 0.0).astype(bf16)
    chunks = tokens // CHUNK
    dk_ref[...] = jnp.zeros_like(dk_ref)
    dv_ref[...] = jnp.zeros_like(dv_ref)

    def step(i, _):
        lanes = pl.ds(pl.multiple_of(i // chunks * PAIR, PAIR), PAIR)
        rows = pl.ds(pl.multiple_of(i % chunks * CHUNK, CHUNK), CHUNK)
        keys = k_ref[:, lanes]
        vals = v_ref[:, lanes]
        keys_t = dot_nt(eye, keys).astype(bf16)
        found = []
        dv = dv_ref[:, lanes]
        dk = dk_ref[:, lanes]
        for half in range(2):
            query = head_of(q_ref[rows, lanes], half)
            g = head_of(g_ref[rows, lanes], half)
            s = dot_nt(keys, query) + mask_ref[...]
            prob = jnp.exp(s - m_ref[pl.ds(2 * i + half, 1)]) * l_ref[pl.ds(2 * i + half, 1)]
            dv += dot(prob.astype(bf16), g)
            spread = prob * dot_nt(vals, g)
            centre = jnp.sum(spread, axis=0, keepdims=True)
            score = (spread - prob * centre).astype(bf16)
            dk += dot(score, query)
            found.append(dot(keys_t[half * HEAD : (half + 1) * HEAD], score))
        dv_ref[:, lanes] = dv
        dk_ref[:, lanes] = dk
        grad_ref[rows, lanes] = (jnp.concatenate(found, axis=0).T * 0.125).astype(bf16)
        return 0

    lax.fori_loop(0, inner // PAIR * chunks, step, 0)
    grad_ref[:, inner : 2 * inner] = dk_ref[:tokens].astype(bf16)
    grad_ref[:, 2 * inner :] = dv_ref[:tokens].astype(bf16)
    coarse_ref[:, :inner] = dk_ref[tokens:].astype(bf16)
    coarse_ref[:, inner:] = dv_ref[tokens:].astype(bf16)
    for i, ref in enumerate((d0_ref, d1_ref, d2_ref, d3_ref)):
        ref[...] = dot_nt(grad_ref[i * n : (i + 1) * n], wi_ref[...]).astype(bf16)


def weight_grads(own_ref, up_ref, right_ref, both_ref, src_ref, grad_ref, cot_ref,
                 b0_ref, b1_ref, b2_ref, b3_ref, keep_ref, send_ref, turned_ref, att_ref):
    d = src_ref.shape[0]
    n = own_ref.shape[0]
    width = grad_ref.shape[1]
    perm = picks(src_ref, d)
    for i, ref in enumerate((own_ref, up_ref, right_ref, both_ref)):
        turned_ref[:, i * n : (i + 1) * n] = dot_nt(perm, ref[:, :d]).astype(bf16)
    for i, ref in enumerate((b0_ref, b1_ref, b2_ref, b3_ref)):
        att_ref[i * n : (i + 1) * n] = ref[...]
    for ref, rows in ((keep_ref, slice(0, d // 2)), (send_ref, slice(d // 2, d))):
        ref[:, :width] = dot(turned_ref[rows], grad_ref[...]).astype(bf16)
        ref[:, width:] = dot(cot_ref[rows], att_ref[...]).astype(bf16)


def block_result(tok_ref, b0_ref, b1_ref, b2_ref, b3_ref, wo_ref, out_ref):
    x = tok_ref.shape[0]
    for half, refs in ((0, (b0_ref, b1_ref)), (1, (b2_ref, b3_ref))):
        branch = [dot(ref[...], wo_ref[...]).astype(bf16).astype(f32) for ref in refs]
        total = x_half(tok_ref, half) + join_z(*branch)
        out_ref[half * (x // 2) : (half + 1) * (x // 2)] = total.astype(bf16).reshape(
            (x // 2,) + out_ref.shape[1:])


def coarse_total(parts_ref, wc_ref, rows_ref, pooled_ref):
    total = jnp.sum(parts_ref[...].astype(f32), axis=0, keepdims=True).astype(bf16)
    rows_ref[...] = jnp.broadcast_to(total, rows_ref.shape)
    pooled_ref[...] = dot_nt(jnp.broadcast_to(total, (8, total.shape[1])), wc_ref[...])


def token_result(tok_ref, cot_ref, b0_ref, b1_ref, b2_ref, b3_ref, pooled_ref, out_ref):
    x, y, z, d = tok_ref.shape
    pooled = (pooled_ref[0:1] / float(x * y * z))[None]
    for half, refs in ((0, (b0_ref, b1_ref)), (1, (b2_ref, b3_ref))):
        normed, inv_std = normalize(x_half(tok_ref, half))
        grad = join_z(*[ref[...].astype(f32) for ref in refs]) + pooled
        first = jnp.mean(grad, axis=-1, keepdims=True)
        second = jnp.mean(grad * normed, axis=-1, keepdims=True)
        total = x_half(cot_ref, half) + inv_std * (grad - first - normed * second)
        out_ref[half * (x // 2) : (half + 1) * (x // 2)] = total.astype(bf16).reshape(
            (x // 2,) + out_ref.shape[1:])


def moved(block, dx, dz):
    nx, nz = lax.axis_size(GX), lax.axis_size(GZ)
    route = [
        (a * nz + c, ((a + dx) % nx) * nz + (c + dz) % nz)
        for a in range(nx)
        for c in range(nz)
    ]
    return lax.ppermute(block, ALL, route)


def mask_quads(a):
    x, y, z = a.shape
    a = jnp.moveaxis(a.reshape(2, x // 2, y, 2, z // 2), 3, 1)
    return a.reshape(2, 2, 1, x * y * z // 4)


def returned(own, up, right, both):
    return moved(both, 1, 1), moved(right, 1, 0), moved(up, 0, 1), own


def body(tokens, body_mask, cotangent, w_in, w_out, w_coarse):
    x, y, z, d = tokens.shape
    size = x * y * z
    n = size // 4
    inner = w_out.shape[0]
    coarse = lax.axis_size(GZ)
    columns = lax.axis_size(GX)
    devices = columns * coarse
    per = d // devices
    core = lax.axis_index("core")

    quads = mask_quads(body_mask)
    masks = [quads[1, 1], moved(quads[1, 0], 0, -1), moved(quads[0, 1], -1, 0), moved(quads[0, 0], -1, -1)]
    live = jnp.concatenate(masks + [jnp.ones((1, coarse), jnp.int32)], axis=1)
    mask = jnp.where(live > 0, 0.0, HIDDEN).reshape(size + coarse, 1)

    wide = (n, d + inner)
    both, right, up, own, far = call(
        prepare, [(wide, bf16)] * 4 + [((coarse, 2 * d), bf16)], tokens, cotangent, w_out, w_coarse,
        flops=4 * size * d * inner, size=10 * size * d)
    up, right, both = moved(up, 0, -1), moved(right, -1, 0), moved(both, -1, -1)
    far = lax.all_to_all(far, GZ, 0, 0, tiled=True)
    pooled = far[:, :d]

    row = jnp.arange(d, dtype=jnp.int32)
    half = row // (d // 2)
    rest = row % (d // 2)
    src = (rest // per * 2 + (half + core) % 2) * per + rest % per
    src = src.reshape(d, 1)
    (cot_turned,) = call(turn_cot, [((d, size), bf16)], cotangent, src, flops=2 * size * d * d, size=4 * size * d)

    slim = (n, inner)
    a0, a1, a2, a3, q, k, v, top, inv = call(
        attend,
        [(slim, bf16)] * 4
        + [((size, inner), bf16), ((size + coarse, inner), bf16), ((size + coarse, inner), bf16)]
        + [((16, CHUNK), f32)] * 2,
        own, up, right, both, w_in, far, mask,
        scratch=[pltpu.VMEM((size, inner), bf16)], flops=6 * size * d * inner + 8 * size * size * inner, size=8 * size * d)
    b0, b1, b2, b3 = returned(a0, a1, a2, a3)

    d0, d1, d2, d3, grad, coarse_part = call(
        attend_back,
        [((n, d), bf16)] * 4 + [((size, 3 * inner), bf16), ((coarse, 2 * inner), bf16)],
        own, up, right, both, w_in, mask, q, k, v, top, inv,
        scratch=[pltpu.VMEM((size, inner), bf16)] + [pltpu.VMEM((size + coarse, inner), f32)] * 2,
        flops=6 * size * d * inner + 16 * size * size * inner, size=10 * size * d)
    e0, e1, e2, e3 = returned(d0, d1, d2, d3)
    parts = lax.all_to_all(coarse_part, GZ, 0, 0, tiled=True)

    keep, send = call(
        weight_grads, [((d // 2, 4 * inner), bf16)] * 2,
        own, up, right, both, src, grad, cot_turned, b0, b1, b2, b3,
        scratch=[pltpu.VMEM((d, size), bf16), pltpu.VMEM((size, inner), bf16)],
        flops=12 * size * d * inner, size=10 * size * d)
    other = lax.ppermute(send, "core", [(0, 1), (1, 0)])
    chips = devices // 2
    chip_sum = (keep.astype(f32) + other.astype(f32)).astype(bf16).reshape(chips, per, 4 * inner)
    got = lax.all_to_all(chip_sum, GX + ("zl", "y"), 0, 0)

    (block_out,) = call(
        block_result, [(tokens.shape, bf16)], tokens, b0, b1, b2, b3, w_out, flops=2 * size * d * inner, size=6 * size * d)

    rows, grad_pooled = call(
        coarse_total, [((coarse, 2 * inner), bf16), ((8, d), f32)], parts, w_coarse, size=2 * d * d)
    grads_far = lax.all_to_all(rows, GZ, 0, 0, tiled=True)
    picked = lax.dynamic_slice_in_dim(
        pooled.reshape(coarse, columns, d // columns), lax.axis_index(GZ) * per, per, axis=2)
    share = jnp.einsum("mcj,me->cje", picked, grads_far, preferred_element_type=f32)
    coarse_grad = jnp.sum(lax.all_to_all(share, GX, 0, 0), axis=0)

    (token_grad,) = call(
        token_result, [(tokens.shape, bf16)], tokens, cotangent, e0, e1, e2, e3, grad_pooled, size=8 * size * d)

    summed = jnp.sum(got.astype(f32), axis=0)
    input_grad = summed[:, : 3 * inner]
    output_grad = summed[:, 3 * inner :].T
    return (block_out, token_grad, input_grad, output_grad, coarse_grad)


def solution(mesh):
    fine = Mesh(mesh.devices.reshape(2, 4, 4, 4, 2), ALL)
    grid = P(GX, None, GZ, None)
    return jax.shard_map(
        body,
        mesh=fine,
        in_specs=(grid, P(GX, None, GZ), grid, P(), P(), P()),
        out_specs=(grid, grid, P(ALL, None), P(None, ALL), P(ALL, None)),
        check_vma=False,
    )
```

```python
import functools

import jax
import jax.numpy as jnp
from jax import lax
from jax.experimental import pallas as pl
from jax.experimental.pallas import tpu as pltpu
from jax.sharding import Mesh
from jax.sharding import PartitionSpec as P

HEAD = 64
PAIR = 2 * HEAD
CHUNK = 256
HIDDEN = -1e30
GX = ("zh", "x")
GZ = ("zl", "y", "core")
ALL = GX + GZ
bf16 = jnp.bfloat16
f32 = jnp.float32


def dot(left, right):
    return jnp.dot(left, right, preferred_element_type=f32)


def dot_nt(left, right):
    return lax.dot_general(left, right, (((1,), (1,)), ((), ())), preferred_element_type=f32)


def call(kernel, outs, *args, scratch=(), far=(), scalars=(), grant=16):
    return pl.pallas_call(
        kernel,
        out_shape=[jax.ShapeDtypeStruct(s, d) for s, d in outs],
        in_specs=[
            pl.BlockSpec(memory_space=pltpu.HBM if i in far else pltpu.SMEM if i in scalars else pltpu.VMEM) for i in range(len(args))
        ],
        scratch_shapes=list(scratch),
        compiler_params=pltpu.CompilerParams(vmem_limit_bytes=grant * 2**20),
        cost_estimate=pl.CostEstimate(flops=1, bytes_accessed=1, transcendentals=0),
    )(*args)


def normalize(values):
    centre = values - jnp.mean(values, axis=-1, keepdims=True)
    inv_std = lax.rsqrt(jnp.mean(centre * centre, axis=-1, keepdims=True) + 1e-05)
    return centre * inv_std, inv_std


def low_rows(shape):
    return lax.broadcasted_iota(jnp.int32, shape, 1) < shape[1] // 2


def split_z(rows):
    m, z, d = rows.shape[0] // 2, rows.shape[1], rows.shape[2]
    pairs = rows.reshape(m, 2, z, d)
    a, b = pairs[:, 0], pairs[:, 1]
    low = low_rows(a.shape)
    lower = jnp.where(low, a, pltpu.roll(b, z // 2, 1))
    upper = jnp.where(low, pltpu.roll(a, z // 2, 1), b)
    return lower.reshape(m * z, d), upper.reshape(m * z, d)


def join_z(lower, upper):
    m, d = lower.shape[0] // 8, lower.shape[1]
    lower, upper = lower.reshape(m, 8, d), upper.reshape(m, 8, d)
    low = low_rows(lower.shape)
    a = jnp.where(low, lower, pltpu.roll(upper, 4, 1))
    b = jnp.where(low, pltpu.roll(lower, 4, 1), upper)
    return jnp.stack([a, b], axis=1).reshape(2 * m, 8, d)


def x_half(ref, half):
    x, y, z, d = ref.shape
    rows = ref[half * (x // 2) : (half + 1) * (x // 2)].astype(f32)
    return rows.reshape(x // 2 * y, z, d)


def columns_of(mask):
    m, z = mask.shape
    rows = jnp.broadcast_to(mask[:, None, :], (m, z, z))
    shape = (m, z, z)
    same = lax.broadcasted_iota(jnp.int32, shape, 1) == lax.broadcasted_iota(jnp.int32, shape, 2)
    column = jnp.sum(jnp.where(same, rows, 0.0), axis=2, keepdims=True)
    return jnp.broadcast_to(column, (m, z, 128))


def prepare(*refs):
    sources, mask_ref, refs = refs[:4], refs[4], refs[5:]
    outs, held, sems = refs[:5], refs[5:9], refs[9]
    both_ref, right_ref, up_ref, own_ref, coarse_ref = outs
    tok_ref, cot_ref, wo_ref, wc_ref = held
    copies = [pltpu.make_async_copy(a, b, sems.at[i]) for i, (a, b) in enumerate(zip(sources, held))]
    for copy in copies:
        copy.start()
    copies[0].wait()
    inner, d = wo_ref.shape
    total = jnp.zeros((1, d), f32)
    cells = 1
    for n in tok_ref.shape[:3]:
        cells *= n
    halves = ((0, (both_ref, right_ref)), (1, (up_ref, own_ref)))
    for half, refs in halves:
        normed, _ = normalize(x_half(tok_ref, half))
        total += jnp.sum(jnp.sum(normed, axis=0), axis=0, keepdims=True)
        for ref, part in zip(refs, split_z(normed)):
            ref[:, :d] = part.astype(bf16)
        x, y, z = mask_ref.shape
        cells_in = mask_ref[half * (x // 2) : (half + 1) * (x // 2)].astype(f32)
        for ref, part in zip(refs, split_z(columns_of(cells_in.reshape(x // 2 * y, z)))):
            ref[:, d + inner :] = part.astype(bf16)
    copies[1].wait()
    copies[2].wait()
    for half, refs in halves:
        for ref, part in zip(refs, split_z(x_half(cot_ref, half))):
            ref[:, d : d + inner] = dot_nt(part.astype(bf16), wo_ref[...]).astype(bf16)
    copies[3].wait()
    pooled = jnp.broadcast_to((total / cells).astype(bf16), (coarse_ref.shape[0], d))
    coarse_ref[:, :d] = pooled
    coarse_ref[:, d:] = dot(pooled, wc_ref[...]).astype(bf16)


def turn_cot(cot_ref, src_ref, out_ref):
    d = cot_ref.shape[3]
    parts = []
    for half in (0, 1):
        parts += [p.astype(bf16) for p in split_z(x_half(cot_ref, half))]
    perm = picks(src_ref, d)
    n = parts[0].shape[0]
    for i, part in enumerate(parts):
        out_ref[:, i * n : (i + 1) * n] = dot_nt(perm, part).astype(bf16)


def picks(src_ref, d):
    columns = lax.broadcasted_iota(jnp.int32, (d, d), 1)
    return jnp.where(columns == src_ref[...], 1.0, 0.0).astype(bf16)


def head_of(pair, half):
    lanes = lax.broadcasted_iota(jnp.int32, pair.shape, 1)
    return jnp.where((lanes < HEAD) == (half == 0), pair, jnp.zeros_like(pair))


def hide(mask_ref, refs, start):
    n = refs[0].shape[0]
    for i, ref in enumerate(refs):
        seen = ref[:, start:].astype(f32)
        mask_ref[i * n : (i + 1) * n] = jnp.where(seen > 0.5, 0.0, HIDDEN)
    mask_ref[4 * n :] = jnp.zeros((mask_ref.shape[0] - 4 * n, mask_ref.shape[1]), f32)


def attend(own_ref, up_ref, right_ref, both_ref, wi_ref, kv_ref,
           a0_ref, a1_ref, a2_ref, a3_ref, q_ref, k_ref, v_ref, m_ref, l_ref, out_ref, mask_ref):
    d, width = wi_ref.shape
    inner = width // 3
    n = own_ref.shape[0]
    tokens = 4 * n
    for i, ref in enumerate((own_ref, up_ref, right_ref, both_ref)):
        packed = dot(ref[:, :d], wi_ref[...])
        rows = slice(i * n, (i + 1) * n)
        q_ref[rows] = packed[:, :inner].astype(bf16) * bf16(0.125)
        k_ref[rows] = packed[:, inner : 2 * inner].astype(bf16)
        v_ref[rows] = packed[:, 2 * inner :].astype(bf16)
    hide(mask_ref, (own_ref, up_ref, right_ref, both_ref), d + inner)
    k_ref[tokens:] = kv_ref[:, d : d + inner]
    v_ref[tokens:] = kv_ref[:, d + inner :]
    eye = jnp.where(
        lax.broadcasted_iota(jnp.int32, (PAIR, PAIR), 0)
        == lax.broadcasted_iota(jnp.int32, (PAIR, PAIR), 1), 1.0, 0.0).astype(bf16)
    chunks = tokens // CHUNK
    m_ref[...] = jnp.zeros_like(m_ref)
    l_ref[...] = jnp.zeros_like(l_ref)

    def step(i, _):
        lanes = pl.ds(pl.multiple_of(i // chunks * PAIR, PAIR), PAIR)
        rows = pl.ds(pl.multiple_of(i % chunks * CHUNK, CHUNK), CHUNK)
        keys = k_ref[:, lanes]
        vals_t = dot_nt(eye, v_ref[:, lanes]).astype(bf16)
        query = q_ref[rows, lanes]
        found = []
        for half in range(2):
            s = dot_nt(keys, head_of(query, half)) + jnp.concatenate([mask_ref[...]] * 2, axis=1)
            top = jnp.max(s, axis=0, keepdims=True)
            e = jnp.exp(s - top)
            inv = 1.0 / jnp.sum(e, axis=0, keepdims=True)
            weight = (e * inv).astype(bf16)
            found.append(dot(vals_t[half * HEAD : (half + 1) * HEAD], weight))
            m_ref[pl.ds(2 * i + half, 1)] = top
            l_ref[pl.ds(2 * i + half, 1)] = inv
        out_ref[rows, lanes] = jnp.concatenate(found, axis=0).T.astype(bf16)
        return 0

    lax.fori_loop(0, inner // PAIR * chunks, step, 0)
    for i, ref in enumerate((a0_ref, a1_ref, a2_ref, a3_ref)):
        ref[...] = out_ref[i * n : (i + 1) * n]


def attend_back(own_ref, up_ref, right_ref, both_ref, wi_ref, q_ref, k_ref, v_ref, m_ref, l_ref,
                d0_ref, d1_ref, d2_ref, d3_ref, grad_ref, coarse_ref, g_ref, dk_ref, dv_ref, mask_ref):
    d, width = wi_ref.shape
    inner = width // 3
    n = own_ref.shape[0]
    tokens = 4 * n
    for i, ref in enumerate((own_ref, up_ref, right_ref, both_ref)):
        g_ref[i * n : (i + 1) * n] = ref[:, d : d + inner]
    hide(mask_ref, (own_ref, up_ref, right_ref, both_ref), d + inner)
    eye = jnp.where(
        lax.broadcasted_iota(jnp.int32, (PAIR, PAIR), 0)
        == lax.broadcasted_iota(jnp.int32, (PAIR, PAIR), 1), 1.0, 0.0).astype(bf16)
    chunks = tokens // CHUNK
    dk_ref[...] = jnp.zeros_like(dk_ref)
    dv_ref[...] = jnp.zeros_like(dv_ref)

    def step(i, _):
        lanes = pl.ds(pl.multiple_of(i // chunks * PAIR, PAIR), PAIR)
        rows = pl.ds(pl.multiple_of(i % chunks * CHUNK, CHUNK), CHUNK)
        keys = k_ref[:, lanes]
        vals = v_ref[:, lanes]
        keys_t = dot_nt(eye, keys).astype(bf16)
        found = []
        dv = dv_ref[:, lanes]
        dk = dk_ref[:, lanes]
        for half in range(2):
            query = head_of(q_ref[rows, lanes], half)
            g = head_of(g_ref[rows, lanes], half)
            s = dot_nt(keys, query) + jnp.concatenate([mask_ref[...]] * 2, axis=1)
            prob = jnp.exp(s - m_ref[pl.ds(2 * i + half, 1)]) * l_ref[pl.ds(2 * i + half, 1)]
            dv += dot(prob.astype(bf16), g)
            spread = prob * dot_nt(vals, g)
            centre = jnp.sum(spread, axis=0, keepdims=True)
            score = (spread - prob * centre).astype(bf16)
            dk += dot(score, query)
            found.append(dot(keys_t[half * HEAD : (half + 1) * HEAD], score))
        dv_ref[:, lanes] = dv
        dk_ref[:, lanes] = dk
        grad_ref[rows, lanes] = (jnp.concatenate(found, axis=0).T * 0.125).astype(bf16)
        return 0

    lax.fori_loop(0, inner // PAIR * chunks, step, 0)
    grad_ref[:, inner : 2 * inner] = dk_ref[:tokens].astype(bf16)
    grad_ref[:, 2 * inner :] = dv_ref[:tokens].astype(bf16)
    peers = coarse_ref.shape[0]
    part = jnp.concatenate([dk_ref[tokens:].astype(bf16), dv_ref[tokens:].astype(bf16)], axis=1)
    chip = lax.broadcasted_iota(jnp.int32, (peers, peers), 0) // 2 * 2
    token = lax.broadcasted_iota(jnp.int32, (peers, peers), 1)
    for i in range(2):
        pick = jnp.where(token == chip + i, 1.0, 0.0).astype(bf16)
        coarse_ref[:, i * 2 * inner : (i + 1) * 2 * inner] = dot(pick, part).astype(bf16)
    for i, ref in enumerate((d0_ref, d1_ref, d2_ref, d3_ref)):
        ref[...] = dot_nt(grad_ref[i * n : (i + 1) * n], wi_ref[...]).astype(bf16)


def weight_grads(own_ref, up_ref, right_ref, both_ref, src_ref, grad_ref, cot_ref,
                 b0_ref, b1_ref, b2_ref, b3_ref, keep_ref, send_ref, turned_ref, att_ref):
    d = src_ref.shape[0]
    n = own_ref.shape[0]
    width = grad_ref.shape[1]
    perm = picks(src_ref, d)
    for i, ref in enumerate((own_ref, up_ref, right_ref, both_ref)):
        turned_ref[:, i * n : (i + 1) * n] = dot_nt(perm, ref[:, :d]).astype(bf16)
    for i, ref in enumerate((b0_ref, b1_ref, b2_ref, b3_ref)):
        att_ref[i * n : (i + 1) * n] = ref[...]
    for ref, rows in ((keep_ref, slice(0, d // 2)), (send_ref, slice(d // 2, d))):
        ref[:, :width] = dot(turned_ref[rows], grad_ref[...]).astype(bf16)
        ref[:, width:] = dot(cot_ref[rows], att_ref[...]).astype(bf16)


def block_result(tok_ref, b0_ref, b1_ref, b2_ref, b3_ref, wo_ref, out_ref):
    x = tok_ref.shape[0]
    for half, refs in ((0, (b0_ref, b1_ref)), (1, (b2_ref, b3_ref))):
        branch = [dot(ref[...], wo_ref[...]).astype(bf16).astype(f32) for ref in refs]
        total = x_half(tok_ref, half) + join_z(*branch)
        out_ref[half * (x // 2) : (half + 1) * (x // 2)] = total.astype(bf16).reshape(
            (x // 2,) + out_ref.shape[1:])


def coarse_total(parts_ref, wc_ref, core_ref, pair_ref, pooled_ref):
    d = wc_ref.shape[0]
    total = jnp.sum(parts_ref[...].astype(f32), axis=0, keepdims=True).astype(bf16)
    pair_ref[...] = total
    row = jnp.where(core_ref[0, 0] == 0, total[:, :d], total[:, d:])
    pooled_ref[...] = dot_nt(jnp.broadcast_to(row, (8, d)), wc_ref[...])


def assemble(keep_ref, other_ref, pair_ref, picked_ref, out_ref):
    plane, rows, width = out_ref.shape
    rows -= 8
    line = lax.broadcasted_iota(jnp.int32, (8, width), 0)
    lanes = picked_ref.shape[1]
    for i in range(plane):
        part = slice(i * rows, (i + 1) * rows)
        out_ref[i, :rows] = (keep_ref[part].astype(f32) + other_ref[part].astype(f32)).astype(bf16)
        extra = jnp.where(line == 0, pair_ref[...].astype(f32), 0.0)
        out_ref[i, rows:] = extra.astype(bf16)
        seen = jnp.where(line[:, :lanes] == 1, picked_ref[i : i + 1].astype(f32), extra[:, :lanes])
        out_ref[i, rows:, :lanes] = seen.astype(bf16)


def plane_sums(in_ref, out_ref):
    plane, rows, width = in_ref.shape
    rows -= 8
    deep = out_ref.shape[0]
    half = width // 2
    total = jnp.sum(in_ref[:, :rows].astype(f32), axis=0)
    extra = in_ref[:, rows:].astype(f32)
    line = lax.broadcasted_iota(jnp.int32, extra.shape, 1)
    grads = jnp.sum(jnp.where(line == 0, extra, 0.0), axis=1).astype(bf16)
    picked = jnp.sum(jnp.where(line == 1, extra, 0.0), axis=1)[:, :256].astype(bf16)
    coarse = jnp.zeros((128, half), f32)
    for i in range(2):
        coarse += lax.dot_general(
            picked[:, i * 128 : (i + 1) * 128], grads[:, i * half : (i + 1) * half],
            (((0,), (0,)), ((), ())), preferred_element_type=f32)
    step = out_ref.shape[1] // (rows // deep)
    for j in range(rows // deep):
        part = slice(j * deep, (j + 1) * deep)
        out_ref[:, j * step : j * step + width] = total[part].astype(bf16)
        out_ref[:, j * step + width : (j + 1) * step] = coarse[part].astype(bf16)


def token_result(tok_ref, cot_ref, b0_ref, b1_ref, b2_ref, b3_ref, pooled_ref, out_ref):
    x, y, z, d = tok_ref.shape
    pooled = (pooled_ref[0:1] / float(x * y * z))[None]
    for half, refs in ((0, (b0_ref, b1_ref)), (1, (b2_ref, b3_ref))):
        normed, inv_std = normalize(x_half(tok_ref, half))
        grad = join_z(*[ref[...].astype(f32) for ref in refs]) + pooled
        first = jnp.mean(grad, axis=-1, keepdims=True)
        second = jnp.mean(grad * normed, axis=-1, keepdims=True)
        total = x_half(cot_ref, half) + inv_std * (grad - first - normed * second)
        out_ref[half * (x // 2) : (half + 1) * (x // 2)] = total.astype(bf16).reshape(
            (x // 2,) + out_ref.shape[1:])


def moved(block, dx, dz):
    nx, nz = lax.axis_size(GX), lax.axis_size(GZ)
    route = [
        (a * nz + c, ((a + dx) % nx) * nz + (c + dz) % nz)
        for a in range(nx)
        for c in range(nz)
    ]
    return lax.ppermute(block, ALL, route)


def returned(own, up, right, both):
    return moved(both, 1, 1), moved(right, 1, 0), moved(up, 0, 1), own


def body(tokens, body_mask, cotangent, w_in, w_out, w_coarse):
    x, y, z, d = tokens.shape
    size = x * y * z
    n = size // 4
    inner = w_out.shape[0]
    coarse = lax.axis_size(GZ)
    columns = lax.axis_size(GX)
    devices = columns * coarse
    per = d // devices
    core = lax.axis_index("core")

    wide = (n, d + inner + 128)
    both, right, up, own, far = call(
        prepare, [(wide, bf16)] * 4 + [((coarse, 2 * d), bf16)], tokens, cotangent, w_out, w_coarse, body_mask,
        far=range(4),
        grant=60,
        scratch=[pltpu.VMEM(a.shape, bf16) for a in (tokens, cotangent, w_out, w_coarse)] + [pltpu.SemaphoreType.DMA((4,))])
    up, right, both = moved(up, 0, -1), moved(right, -1, 0), moved(both, -1, -1)
    far = lax.all_to_all(far, GZ, 0, 0, tiled=True)

    zh, nx, zl, ny, cores = (lax.axis_size(a) for a in ALL)
    plane, deep = nx * ny, zh * zl
    mine = lax.dynamic_slice_in_dim(far, lax.axis_index(GZ) // cores * cores, cores, axis=0)[:, :d]
    mine = mine.reshape(cores, zh, nx, zl, ny, cores, per)
    mine = lax.dynamic_index_in_dim(mine, core, axis=5, keepdims=False)
    mine = jnp.transpose(mine, (2, 4, 0, 5, 1, 3)).reshape(plane, cores, per * deep)
    picked = jnp.pad(mine, ((0, 0), (0, 0), (0, 128 - per * deep))).reshape(plane, cores * 128)

    row = jnp.arange(d, dtype=jnp.int32)
    half, rest = row // (d // 2), row % (d // 2)
    chip, j, depth = rest // (per * deep), rest % (per * deep) // deep, rest % deep
    device = ((depth // zl * nx + chip // ny) * zl + depth % zl) * ny + chip % ny
    src = ((device * cores + (half + core) % cores) * per + j).reshape(d, 1)
    (cot_turned,) = call(turn_cot, [((d, size), bf16)], cotangent, src)

    slim = (n, inner)
    a0, a1, a2, a3, q, k, v, top, inv = call(
        attend,
        [(slim, bf16)] * 4
        + [((size, inner), bf16), ((size + coarse, inner), bf16), ((size + coarse, inner), bf16)]
        + [((16, CHUNK), f32)] * 2,
        own, up, right, both, w_in, far,
        scratch=[pltpu.VMEM((size, inner), bf16), pltpu.VMEM((size + coarse, 128), f32)])
    b0, b1, b2, b3 = returned(a0, a1, a2, a3)

    d0, d1, d2, d3, grad, coarse_part = call(
        attend_back,
        [((n, d), bf16)] * 4 + [((size, 3 * inner), bf16), ((coarse, 4 * inner), bf16)],
        own, up, right, both, w_in, q, k, v, top, inv,
        scratch=[pltpu.VMEM((size, inner), bf16)] + [pltpu.VMEM((size + coarse, inner), f32)] * 2
        + [pltpu.VMEM((size + coarse, 128), f32)])
    e0, e1, e2, e3 = returned(d0, d1, d2, d3)
    parts = lax.all_to_all(coarse_part, GZ, 0, 0, tiled=True)

    grad, e2 = lax.optimization_barrier((grad, e2))
    keep, send = call(
        weight_grads, [((d // 2, 4 * inner), bf16)] * 2,
        own, up, right, both, src, grad, cot_turned, b0, b1, b2, b3,
        scratch=[pltpu.VMEM((d, size), bf16), pltpu.VMEM((size, inner), bf16)])
    other = lax.ppermute(send, "core", [(0, 1), (1, 0)])
    pair, grad_pooled = call(
        coarse_total, [((1, 4 * inner), bf16), ((8, d), f32)], parts, w_coarse, core.reshape(1, 1), scalars=(2,))

    (packet,) = call(
        assemble, [((plane, per * deep + 8, 4 * inner), bf16)], keep, other, pair, picked)
    packet, e0, e1, e2 = lax.optimization_barrier((packet, e0, e1, e2))
    packet = lax.all_to_all(packet, ("x", "y"), 0, 0, tiled=True)
    (slab,) = call(plane_sums, [((deep, per * 6 * inner), bf16)], packet)
    slab = lax.all_to_all(slab, ("zh", "zl"), 0, 0, tiled=True)

    (block_out,) = call(block_result, [(tokens.shape, bf16)], tokens, b0, b1, b2, b3, w_out)
    (token_grad,) = call(token_result, [(tokens.shape, bf16)], tokens, cotangent, e0, e1, e2, e3, grad_pooled)

    summed = jnp.sum(slab.astype(f32), axis=0).reshape(per, 6 * inner)
    input_grad = summed[:, : 3 * inner]
    output_grad = summed[:, 3 * inner : 4 * inner].T
    coarse_grad = summed[:, 4 * inner :]
    return (block_out, token_grad, input_grad, output_grad, coarse_grad)


def solution(mesh):
    fine = Mesh(mesh.devices.reshape(2, 4, 4, 4, 2), ALL)
    grid = P(GX, None, GZ, None)
    return jax.shard_map(
        body,
        mesh=fine,
        in_specs=(grid, P(GX, None, GZ), grid, P(), P(), P()),
        out_specs=(grid, grid, P(ALL, None), P(None, ALL), P(ALL, None)),
        check_vma=False,
    )
```

```python
import functools

import jax
import jax.numpy as jnp
from jax import lax
from jax.experimental import pallas as pl
from jax.experimental.pallas import tpu as pltpu
from jax.sharding import Mesh
from jax.sharding import PartitionSpec as P

HEAD = 64
PAIR = 2 * HEAD
CHUNK = 256
HIDDEN = -1e30
GX = ("zh", "x")
GZ = ("zl", "y", "core")
ALL = GX + GZ
bf16 = jnp.bfloat16
f32 = jnp.float32


def dot(left, side):
    return jnp.dot(left, side, preferred_element_type=f32)


def dot_nt(left, side):
    return lax.dot_general(left, side, (((1,), (1,)), ((), ())), preferred_element_type=f32)


def call(kernel, outs, *args, scratch=(), far=(), scalars=(), grant=16):
    return pl.pallas_call(
        kernel,
        out_shape=[jax.ShapeDtypeStruct(s, d) for s, d in outs],
        in_specs=[
            pl.BlockSpec(memory_space=pltpu.HBM if i in far else pltpu.SMEM if i in scalars else pltpu.VMEM) for i in range(len(args))
        ],
        scratch_shapes=list(scratch),
        compiler_params=pltpu.CompilerParams(vmem_limit_bytes=grant * 2**20),
        cost_estimate=pl.CostEstimate(flops=1, bytes_accessed=1, transcendentals=0),
    )(*args)


def normalize(values):
    centre = values - jnp.mean(values, axis=-1, keepdims=True)
    inv_std = lax.rsqrt(jnp.mean(centre * centre, axis=-1, keepdims=True) + 1e-05)
    return centre * inv_std, inv_std


def low_rows(shape):
    return lax.broadcasted_iota(jnp.int32, shape, 1) < shape[1] // 2


def split_z(rows):
    m, z, d = rows.shape[0] // 2, rows.shape[1], rows.shape[2]
    pairs = rows.reshape(m, 2, z, d)
    a, b = pairs[:, 0], pairs[:, 1]
    low = low_rows(a.shape)
    lower = jnp.where(low, a, pltpu.roll(b, z // 2, 1))
    upper = jnp.where(low, pltpu.roll(a, z // 2, 1), b)
    return lower.reshape(m * z, d), upper.reshape(m * z, d)


def join_z(lower, upper):
    m, d = lower.shape[0] // 8, lower.shape[1]
    lower, upper = lower.reshape(m, 8, d), upper.reshape(m, 8, d)
    low = low_rows(lower.shape)
    a = jnp.where(low, lower, pltpu.roll(upper, 4, 1))
    b = jnp.where(low, pltpu.roll(lower, 4, 1), upper)
    return jnp.stack([a, b], axis=1).reshape(2 * m, 8, d)


def halves(core_ref, x):
    far = core_ref[0, 0] * (x // 2)
    return far, x // 2 - far


def x_half(ref, start):
    x, y, z, d = ref.shape
    return ref[pl.ds(start, x // 2)].astype(f32).reshape(x // 2 * y, z, d)


def columns_of(mask):
    m, z = mask.shape
    rows = jnp.broadcast_to(mask[:, None, :], (m, z, z))
    shape = (m, z, z)
    same = lax.broadcasted_iota(jnp.int32, shape, 1) == lax.broadcasted_iota(jnp.int32, shape, 2)
    column = jnp.sum(jnp.where(same, rows, 0.0), axis=2, keepdims=True)
    return jnp.broadcast_to(column, (m, z, 128))


def prepare(*refs):
    sources, mask_ref, core_ref, refs = refs[:4], refs[4], refs[5], refs[6:]
    outs, held, sems = refs[:5], refs[5:9], refs[9]
    up_ref, side_ref, both_ref, own_ref, coarse_ref = outs
    tok_ref, cot_ref, wo_ref, wc_ref = held
    copies = [pltpu.make_async_copy(a, b, sems.at[i]) for i, (a, b) in enumerate(zip(sources, held))]
    for copy in copies:
        copy.start()
    copies[0].wait()
    inner, d = wo_ref.shape
    total = jnp.zeros((1, d), f32)
    cells = 1
    for n in tok_ref.shape[:3]:
        cells *= n
    away, home = halves(core_ref, tok_ref.shape[0])
    places = ((away, (up_ref, side_ref)), (home, (both_ref, own_ref)))
    for start, refs in places:
        normed, _ = normalize(x_half(tok_ref, start))
        total += jnp.sum(jnp.sum(normed, axis=0), axis=0, keepdims=True)
        for ref, part in zip(refs, split_z(normed)):
            ref[:, :d] = part.astype(bf16)
        x, y, z = mask_ref.shape
        cells_in = mask_ref[pl.ds(start, x // 2)].astype(f32)
        for ref, part in zip(refs, split_z(columns_of(cells_in.reshape(x // 2 * y, z)))):
            ref[:, d + inner :] = part.astype(bf16)
    copies[1].wait()
    copies[2].wait()
    for start, refs in places:
        for ref, part in zip(refs, split_z(x_half(cot_ref, start))):
            ref[:, d : d + inner] = dot_nt(part.astype(bf16), wo_ref[...]).astype(bf16)
    copies[3].wait()
    pooled = (total / cells).astype(bf16)
    coarse_ref[:, :d] = pooled
    coarse_ref[:, d:] = dot(jnp.broadcast_to(pooled, (8, d)), wc_ref[...])[:1].astype(bf16)


def turn_cot(cot_ref, src_ref, core_ref, out_ref):
    d = cot_ref.shape[3]
    parts = []
    for start in halves(core_ref, cot_ref.shape[0]):
        parts += [p.astype(bf16) for p in split_z(x_half(cot_ref, start))]
    perm = picks(src_ref, d)
    n = parts[0].shape[0]
    for i, part in enumerate(parts):
        out_ref[:, i * n : (i + 1) * n] = dot_nt(perm, part).astype(bf16)


def picks(src_ref, d):
    columns = lax.broadcasted_iota(jnp.int32, (d, d), 1)
    return jnp.where(columns == src_ref[...], 1.0, 0.0).astype(bf16)


def head_of(pair, half):
    lanes = lax.broadcasted_iota(jnp.int32, pair.shape, 1)
    return jnp.where((lanes < HEAD) == (half == 0), pair, jnp.zeros_like(pair))


def hide(mask_ref, refs, start):
    n = refs[0].shape[0]
    for i, ref in enumerate(refs):
        seen = ref[:, start:].astype(f32)
        mask_ref[i * n : (i + 1) * n] = jnp.where(seen > 0.5, 0.0, HIDDEN)
    mask_ref[4 * n :] = jnp.zeros((mask_ref.shape[0] - 4 * n, mask_ref.shape[1]), f32)


def attend(own_ref, up_ref, side_ref, both_ref, wi_ref, kv_ref,
           a0_ref, a1_ref, a2_ref, a3_ref, q_ref, k_ref, v_ref, m_ref, l_ref, out_ref, mask_ref):
    d, width = wi_ref.shape
    inner = width // 3
    n = own_ref.shape[0]
    tokens = 4 * n
    for i, ref in enumerate((own_ref, up_ref, side_ref, both_ref)):
        packed = dot(ref[:, :d], wi_ref[...])
        rows = slice(i * n, (i + 1) * n)
        q_ref[rows] = packed[:, :inner].astype(bf16) * bf16(0.125)
        k_ref[rows] = packed[:, inner : 2 * inner].astype(bf16)
        v_ref[rows] = packed[:, 2 * inner :].astype(bf16)
    hide(mask_ref, (own_ref, up_ref, side_ref, both_ref), d + inner)
    k_ref[tokens:] = kv_ref[:, :inner]
    v_ref[tokens:] = kv_ref[:, inner:]
    eye = jnp.where(
        lax.broadcasted_iota(jnp.int32, (PAIR, PAIR), 0)
        == lax.broadcasted_iota(jnp.int32, (PAIR, PAIR), 1), 1.0, 0.0).astype(bf16)
    chunks = tokens // CHUNK
    m_ref[...] = jnp.zeros_like(m_ref)
    l_ref[...] = jnp.zeros_like(l_ref)

    def step(i, _):
        lanes = pl.ds(pl.multiple_of(i // chunks * PAIR, PAIR), PAIR)
        rows = pl.ds(pl.multiple_of(i % chunks * CHUNK, CHUNK), CHUNK)
        keys = k_ref[:, lanes]
        vals_t = dot_nt(eye, v_ref[:, lanes]).astype(bf16)
        query = q_ref[rows, lanes]
        found = []
        for half in range(2):
            s = dot_nt(keys, head_of(query, half)) + jnp.concatenate([mask_ref[...]] * 2, axis=1)
            top = jnp.max(s, axis=0, keepdims=True)
            e = jnp.exp(s - top)
            inv = 1.0 / jnp.sum(e, axis=0, keepdims=True)
            weight = (e * inv).astype(bf16)
            found.append(dot(vals_t[half * HEAD : (half + 1) * HEAD], weight))
            m_ref[pl.ds(2 * i + half, 1)] = top
            l_ref[pl.ds(2 * i + half, 1)] = inv
        out_ref[rows, lanes] = jnp.concatenate(found, axis=0).T.astype(bf16)
        return 0

    lax.fori_loop(0, inner // PAIR * chunks, step, 0)
    for i, ref in enumerate((a0_ref, a1_ref, a2_ref, a3_ref)):
        ref[...] = out_ref[i * n : (i + 1) * n]


def attend_back(own_ref, up_ref, side_ref, both_ref, wi_ref, q_ref, k_ref, v_ref, m_ref, l_ref,
                d0_ref, d1_ref, d2_ref, d3_ref, grad_ref, coarse_ref, g_ref, dk_ref, dv_ref, mask_ref):
    d, width = wi_ref.shape
    inner = width // 3
    n = own_ref.shape[0]
    tokens = 4 * n
    for i, ref in enumerate((own_ref, up_ref, side_ref, both_ref)):
        g_ref[i * n : (i + 1) * n] = ref[:, d : d + inner]
    hide(mask_ref, (own_ref, up_ref, side_ref, both_ref), d + inner)
    eye = jnp.where(
        lax.broadcasted_iota(jnp.int32, (PAIR, PAIR), 0)
        == lax.broadcasted_iota(jnp.int32, (PAIR, PAIR), 1), 1.0, 0.0).astype(bf16)
    chunks = tokens // CHUNK
    dk_ref[...] = jnp.zeros_like(dk_ref)
    dv_ref[...] = jnp.zeros_like(dv_ref)

    def step(i, _):
        lanes = pl.ds(pl.multiple_of(i // chunks * PAIR, PAIR), PAIR)
        rows = pl.ds(pl.multiple_of(i % chunks * CHUNK, CHUNK), CHUNK)
        keys = k_ref[:, lanes]
        vals = v_ref[:, lanes]
        keys_t = dot_nt(eye, keys).astype(bf16)
        found = []
        dv = dv_ref[:, lanes]
        dk = dk_ref[:, lanes]
        for half in range(2):
            query = head_of(q_ref[rows, lanes], half)
            g = head_of(g_ref[rows, lanes], half)
            s = dot_nt(keys, query) + jnp.concatenate([mask_ref[...]] * 2, axis=1)
            prob = jnp.exp(s - m_ref[pl.ds(2 * i + half, 1)]) * l_ref[pl.ds(2 * i + half, 1)]
            dv += dot(prob.astype(bf16), g)
            spread = prob * dot_nt(vals, g)
            centre = jnp.sum(spread, axis=0, keepdims=True)
            score = (spread - prob * centre).astype(bf16)
            dk += dot(score, query)
            found.append(dot(keys_t[half * HEAD : (half + 1) * HEAD], score))
        dv_ref[:, lanes] = dv
        dk_ref[:, lanes] = dk
        grad_ref[rows, lanes] = (jnp.concatenate(found, axis=0).T * 0.125).astype(bf16)
        return 0

    lax.fori_loop(0, inner // PAIR * chunks, step, 0)
    grad_ref[:, inner : 2 * inner] = dk_ref[:tokens].astype(bf16)
    grad_ref[:, 2 * inner :] = dv_ref[:tokens].astype(bf16)
    peers = coarse_ref.shape[0]
    part = jnp.concatenate([dk_ref[tokens:].astype(bf16), dv_ref[tokens:].astype(bf16)], axis=1)
    chip = lax.broadcasted_iota(jnp.int32, (peers, peers), 0) // 2 * 2
    token = lax.broadcasted_iota(jnp.int32, (peers, peers), 1)
    for i in range(2):
        pick = jnp.where(token == chip + i, 1.0, 0.0).astype(bf16)
        coarse_ref[:, i * 2 * inner : (i + 1) * 2 * inner] = dot(pick, part).astype(bf16)
    for i, ref in enumerate((d0_ref, d1_ref, d2_ref, d3_ref)):
        ref[...] = dot_nt(grad_ref[i * n : (i + 1) * n], wi_ref[...]).astype(bf16)


def weight_grads(own_ref, up_ref, side_ref, both_ref, src_ref, grad_ref, cot_ref,
                 b0_ref, b1_ref, b2_ref, b3_ref, keep_ref, send_ref, turned_ref, att_ref):
    d = src_ref.shape[0]
    n = own_ref.shape[0]
    width = grad_ref.shape[1]
    perm = picks(src_ref, d)
    for i, ref in enumerate((own_ref, up_ref, side_ref, both_ref)):
        turned_ref[:, i * n : (i + 1) * n] = dot_nt(perm, ref[:, :d]).astype(bf16)
    for i, ref in enumerate((b0_ref, b1_ref, b2_ref, b3_ref)):
        att_ref[i * n : (i + 1) * n] = ref[...]
    for ref, rows in ((keep_ref, slice(0, d // 2)), (send_ref, slice(d // 2, d))):
        ref[:, :width] = dot(turned_ref[rows], grad_ref[...]).astype(bf16)
        ref[:, width:] = dot(cot_ref[rows], att_ref[...]).astype(bf16)


def block_result(tok_ref, b0_ref, b1_ref, b2_ref, b3_ref, wo_ref, core_ref, out_ref):
    x = tok_ref.shape[0]
    for start, refs in zip(halves(core_ref, x), ((b0_ref, b1_ref), (b2_ref, b3_ref))):
        branch = [dot(ref[...], wo_ref[...]).astype(bf16).astype(f32) for ref in refs]
        total = x_half(tok_ref, start) + join_z(*branch)
        out_ref[pl.ds(start, x // 2)] = total.astype(bf16).reshape(
            (x // 2,) + out_ref.shape[1:])


def coarse_total(parts_ref, core_ref, pair_ref, here_ref, there_ref):
    d = parts_ref.shape[1] // 2
    parts = parts_ref[...].astype(f32)
    even = lax.broadcasted_iota(jnp.int32, parts.shape, 0) % 2 == 0
    for i, ref in ((0, here_ref), (1, there_ref)):
        total = jnp.sum(jnp.where(even == (i == 0), parts, 0.0), axis=0, keepdims=True)
        pair_ref[pl.ds(i, 1)] = total
        ref[...] = jnp.where(core_ref[0, 0] == 0, total[:, :d], total[:, d:])


def assemble(keep_ref, other_ref, pair_ref, picked_ref, out_ref):
    plane, rows, width = out_ref.shape
    rows -= 8
    line = lax.broadcasted_iota(jnp.int32, (8, width), 0)
    lanes = picked_ref.shape[1]
    for i in range(plane):
        part = slice(i * rows, (i + 1) * rows)
        out_ref[i, :rows] = (keep_ref[part].astype(f32) + other_ref[part].astype(f32)).astype(bf16)
        extra = jnp.where(line == 0, pair_ref[0:1], jnp.where(line == 1, pair_ref[1:2], 0.0))
        out_ref[i, rows:] = extra.astype(bf16)
        seen = jnp.where(line[:, :lanes] == 2, picked_ref[i : i + 1].astype(f32), extra[:, :lanes])
        out_ref[i, rows:, :lanes] = seen.astype(bf16)


def plane_sums(in_ref, out_ref):
    plane, rows, width = in_ref.shape
    rows -= 8
    deep = out_ref.shape[0]
    half = width // 2
    total = jnp.sum(in_ref[:, :rows].astype(f32), axis=0)
    extra = in_ref[:, rows:].astype(f32)
    line = lax.broadcasted_iota(jnp.int32, extra.shape, 1)
    picked = jnp.sum(jnp.where(line == 2, extra, 0.0), axis=1)[:, :512].astype(bf16)
    coarse = jnp.zeros((128, half), f32)
    for i in range(4):
        if i % 2 == 0:
            grads = jnp.sum(jnp.where(line == i // 2, extra, 0.0), axis=1).astype(bf16)
        coarse += lax.dot_general(
            picked[:, i * 128 : (i + 1) * 128], grads[:, i % 2 * half : (i % 2 + 1) * half],
            (((0,), (0,)), ((), ())), preferred_element_type=f32)
    step = out_ref.shape[1] // (rows // deep)
    for j in range(rows // deep):
        part = slice(j * deep, (j + 1) * deep)
        out_ref[:, j * step : j * step + width] = total[part].astype(bf16)
        out_ref[:, j * step + width : (j + 1) * step] = coarse[part].astype(bf16)


def token_result(tok_ref, cot_ref, b0_ref, b1_ref, b2_ref, b3_ref, here_ref, next_ref, wc_ref, core_ref, out_ref):
    x, y, z, d = tok_ref.shape
    coarse = (here_ref[...] + next_ref[...]).astype(bf16)
    pooled = dot_nt(jnp.broadcast_to(coarse, (8, d)), wc_ref[...])[0:1]
    pooled = (pooled / float(x * y * z))[None]
    for start, refs in zip(halves(core_ref, x), ((b0_ref, b1_ref), (b2_ref, b3_ref))):
        normed, inv_std = normalize(x_half(tok_ref, start))
        grad = join_z(*[ref[...].astype(f32) for ref in refs]) + pooled
        first = jnp.mean(grad, axis=-1, keepdims=True)
        second = jnp.mean(grad * normed, axis=-1, keepdims=True)
        total = x_half(cot_ref, start) + inv_std * (grad - first - normed * second)
        out_ref[pl.ds(start, x // 2)] = total.astype(bf16).reshape(
            (x // 2,) + out_ref.shape[1:])


def passed(block, step, back=False):
    nx, nz = lax.axis_size(GX), lax.axis_size(GZ)
    route = []
    for a in range(nx):
        for c in range(nz):
            to_a, to_c = step(a, c)
            route.append((a * nz + c, to_a % nx * nz + to_c % nz))
    if back:
        route = [(b, a) for a, b in route]
    return lax.ppermute(block, ALL, route)


def to_up(a, c):
    return a, c - 1


def to_side(a, c):
    return (a - 1, c) if c % 2 == 0 else (a + 1, c)


def to_both(a, c):
    return (a - 1, c - 1) if c % 2 else (a + 1, c - 1)


def returned(own, up, side, both):
    return passed(up, to_up, True), passed(side, to_side, True), passed(both, to_both, True), own


def body(tokens, body_mask, cotangent, w_in, w_out, w_coarse):
    x, y, z, d = tokens.shape
    size = x * y * z
    n = size // 4
    inner = w_out.shape[0]
    coarse = lax.axis_size(GZ)
    columns = lax.axis_size(GX)
    devices = columns * coarse
    per = d // devices
    core = lax.axis_index("core")

    wide = (n, d + inner + 128)
    place = core.reshape(1, 1)
    up, side, both, own, row = call(
        prepare, [(wide, bf16)] * 4 + [((1, 2 * d), bf16)], tokens, cotangent, w_out, w_coarse, body_mask, place,
        far=range(4),
        scalars=(5,),
        grant=60,
        scratch=[pltpu.VMEM(a.shape, bf16) for a in (tokens, cotangent, w_out, w_coarse)] + [pltpu.SemaphoreType.DMA((4,))])
    before = passed(row, lambda a, c: (a + 1, c))
    up, side, both = passed(up, to_up), passed(side, to_side), passed(both, to_both)

    odd = lax.broadcasted_iota(jnp.int32, (coarse, 1), 0) % 2 == 1
    shared = jnp.broadcast_to(jnp.concatenate([row[:, :d], before[:, :d]], axis=1), (coarse, 2 * d))
    kv = jnp.where(odd, before[:, d:], row[:, d:])
    far = lax.all_to_all(jnp.concatenate([shared, kv], axis=1), GZ, 0, 0, tiled=True)
    kv = far[:, 2 * d :]

    zh, nx, zl, ny, cores = (lax.axis_size(a) for a in ALL)
    plane, deep = nx * ny, zh * zl
    mine = lax.dynamic_slice_in_dim(far, lax.axis_index(GZ) // cores * cores, cores, axis=0)[:, : 2 * d]
    mine = mine.reshape(cores, 2, zh, nx, zl, ny, cores, per)
    mine = lax.dynamic_index_in_dim(mine, core, axis=6, keepdims=False)
    mine = jnp.transpose(mine, (3, 5, 1, 0, 6, 2, 4)).reshape(plane, 2 * cores, per * deep)
    picked = jnp.pad(mine, ((0, 0), (0, 0), (0, 128 - per * deep))).reshape(plane, 2 * cores * 128)

    row = jnp.arange(d, dtype=jnp.int32)
    half, rest = row // (d // 2), row % (d // 2)
    chip, j, depth = rest // (per * deep), rest % (per * deep) // deep, rest % deep
    device = ((depth // zl * nx + chip // ny) * zl + depth % zl) * ny + chip % ny
    src = ((device * cores + (half + core) % cores) * per + j).reshape(d, 1)
    (cot_turned,) = call(turn_cot, [((d, size), bf16)], cotangent, src, place, scalars=(2,))
    kv, cot_turned = lax.optimization_barrier((kv, cot_turned))

    slim = (n, inner)
    a0, a1, a2, a3, q, k, v, top, inv = call(
        attend,
        [(slim, bf16)] * 4
        + [((size, inner), bf16), ((size + coarse, inner), bf16), ((size + coarse, inner), bf16)]
        + [((16, CHUNK), f32)] * 2,
        own, up, side, both, w_in, kv,
        scratch=[pltpu.VMEM((size, inner), bf16), pltpu.VMEM((size + coarse, 128), f32)])
    b0, b1, b2, b3 = returned(a0, a1, a2, a3)

    d0, d1, d2, d3, grad, coarse_part = call(
        attend_back,
        [((n, d), bf16)] * 4 + [((size, 3 * inner), bf16), ((coarse, 4 * inner), bf16)],
        own, up, side, both, w_in, q, k, v, top, inv,
        scratch=[pltpu.VMEM((size, inner), bf16)] + [pltpu.VMEM((size + coarse, inner), f32)] * 2
        + [pltpu.VMEM((size + coarse, 128), f32)])
    e0, e1, e2, e3 = returned(d0, d1, d2, d3)
    parts = lax.all_to_all(coarse_part, GZ, 0, 0, tiled=True)

    grad, parts, e0 = lax.optimization_barrier((grad, parts, e0))
    keep, send = call(
        weight_grads, [((d // 2, 4 * inner), bf16)] * 2,
        own, up, side, both, src, grad, cot_turned, b0, b1, b2, b3,
        scratch=[pltpu.VMEM((d, size), bf16), pltpu.VMEM((size, inner), bf16)])
    other = lax.ppermute(send, "core", [(0, 1), (1, 0)])
    pair, here, there = call(
        coarse_total, [((2, 4 * inner), f32), ((1, d), f32), ((1, d), f32)], parts, place, scalars=(1,))
    later = passed(there, lambda a, c: (a - 1, c))

    (packet,) = call(
        assemble, [((plane, per * deep + 8, 4 * inner), bf16)], keep, other, pair, picked)
    packet, e0, e1, e2 = lax.optimization_barrier((packet, e0, e1, e2))
    packet = lax.all_to_all(packet, ("x", "y"), 0, 0, tiled=True)
    (slab,) = call(plane_sums, [((deep, per * 6 * inner), bf16)], packet)
    slab = lax.all_to_all(slab, ("zh", "zl"), 0, 0, tiled=True)

    (block_out,) = call(block_result, [(tokens.shape, bf16)], tokens, b0, b1, b2, b3, w_out, place, scalars=(6,))
    (token_grad,) = call(token_result, [(tokens.shape, bf16)], tokens, cotangent, e0, e1, e2, e3,
        here, later, w_coarse, place, scalars=(9,))

    summed = jnp.sum(slab.astype(f32), axis=0).reshape(per, 6 * inner)
    input_grad = summed[:, : 3 * inner]
    output_grad = summed[:, 3 * inner : 4 * inner].T
    coarse_grad = summed[:, 4 * inner :]
    return (block_out, token_grad, input_grad, output_grad, coarse_grad)


def solution(mesh):
    fine = Mesh(mesh.devices.reshape(2, 4, 4, 4, 2), ALL)
    grid = P(GX, None, GZ, None)
    return jax.shard_map(
        body,
        mesh=fine,
        in_specs=(grid, P(GX, None, GZ), grid, P(), P(), P()),
        out_specs=(grid, grid, P(ALL, None), P(None, ALL), P(ALL, None)),
        check_vma=False,
    )
```

```python
import functools

import jax
import jax.numpy as jnp
from jax import lax
from jax.experimental import pallas as pl
from jax.experimental.pallas import tpu as pltpu
from jax.sharding import Mesh
from jax.sharding import PartitionSpec as P

HEAD = 64
PAIR = 2 * HEAD
CHUNK = 256
HIDDEN = -1e30
GX = ("zh", "x")
GZ = ("zl", "y", "core")
ALL = GX + GZ
bf16 = jnp.bfloat16
f32 = jnp.float32


def dot(left, side):
    return jnp.dot(left, side, preferred_element_type=f32)


def dot_nt(left, side):
    return lax.dot_general(left, side, (((1,), (1,)), ((), ())), preferred_element_type=f32)


def call(kernel, outs, *args, scratch=(), far=(), scalars=(), grant=16):
    return pl.pallas_call(
        kernel,
        out_shape=[jax.ShapeDtypeStruct(s, d) for s, d in outs],
        in_specs=[
            pl.BlockSpec(memory_space=pltpu.HBM if i in far else pltpu.SMEM if i in scalars else pltpu.VMEM) for i in range(len(args))
        ],
        scratch_shapes=list(scratch),
        compiler_params=pltpu.CompilerParams(vmem_limit_bytes=grant * 2**20),
        cost_estimate=pl.CostEstimate(flops=1, bytes_accessed=1, transcendentals=0),
    )(*args)


def normalize(values):
    centre = values - jnp.mean(values, axis=-1, keepdims=True)
    inv_std = lax.rsqrt(jnp.mean(centre * centre, axis=-1, keepdims=True) + 1e-05)
    return centre * inv_std, inv_std


def low_rows(shape):
    return lax.broadcasted_iota(jnp.int32, shape, 1) < shape[1] // 2


def split_z(rows):
    m, z, d = rows.shape[0] // 2, rows.shape[1], rows.shape[2]
    pairs = rows.reshape(m, 2, z, d)
    a, b = pairs[:, 0], pairs[:, 1]
    low = low_rows(a.shape)
    lower = jnp.where(low, a, pltpu.roll(b, z // 2, 1))
    upper = jnp.where(low, pltpu.roll(a, z // 2, 1), b)
    return lower.reshape(m * z, d), upper.reshape(m * z, d)


def join_z(lower, upper):
    m, d = lower.shape[0] // 8, lower.shape[1]
    lower, upper = lower.reshape(m, 8, d), upper.reshape(m, 8, d)
    low = low_rows(lower.shape)
    a = jnp.where(low, lower, pltpu.roll(upper, 4, 1))
    b = jnp.where(low, pltpu.roll(lower, 4, 1), upper)
    return jnp.stack([a, b], axis=1).reshape(2 * m, 8, d)


def halves(core_ref, x):
    far = core_ref[0, 0] * (x // 2)
    return far, x // 2 - far


def x_half(ref, start):
    x, y, z, d = ref.shape
    return ref[pl.ds(start, x // 2)].astype(f32).reshape(x // 2 * y, z, d)


def columns_of(mask):
    m, z = mask.shape
    rows = jnp.broadcast_to(mask[:, None, :], (m, z, z))
    shape = (m, z, z)
    same = lax.broadcasted_iota(jnp.int32, shape, 1) == lax.broadcasted_iota(jnp.int32, shape, 2)
    column = jnp.sum(jnp.where(same, rows, 0.0), axis=2, keepdims=True)
    return jnp.broadcast_to(column, (m, z, 128))


def prepare(*refs):
    sources, mask_ref, core_ref, refs = refs[:4], refs[4], refs[5], refs[6:]
    outs, held, sems = refs[:5], refs[5:9], refs[9]
    up_ref, side_ref, both_ref, own_ref, coarse_ref = outs
    tok_ref, cot_ref, wo_ref, wc_ref = held
    copies = [pltpu.make_async_copy(a, b, sems.at[i]) for i, (a, b) in enumerate(zip(sources, held))]
    for copy in copies:
        copy.start()
    copies[0].wait()
    inner, d = wo_ref.shape
    total = jnp.zeros((1, d), f32)
    cells = 1
    for n in tok_ref.shape[:3]:
        cells *= n
    away, home = halves(core_ref, tok_ref.shape[0])
    places = ((away, (up_ref, side_ref)), (home, (both_ref, own_ref)))
    for start, refs in places:
        normed, _ = normalize(x_half(tok_ref, start))
        total += jnp.sum(jnp.sum(normed, axis=0), axis=0, keepdims=True)
        for ref, part in zip(refs, split_z(normed)):
            ref[:, :d] = part.astype(bf16)
        x, y, z = mask_ref.shape
        cells_in = mask_ref[pl.ds(start, x // 2)].astype(f32)
        for ref, part in zip(refs, split_z(columns_of(cells_in.reshape(x // 2 * y, z)))):
            ref[:, d + inner :] = part.astype(bf16)
    copies[1].wait()
    copies[2].wait()
    for start, refs in places:
        for ref, part in zip(refs, split_z(x_half(cot_ref, start))):
            ref[:, d : d + inner] = dot_nt(part.astype(bf16), wo_ref[...]).astype(bf16)
    copies[3].wait()
    pooled = (total / cells).astype(bf16)
    coarse_ref[:, :d] = pooled
    coarse_ref[:, d:] = dot(jnp.broadcast_to(pooled, (8, d)), wc_ref[...])[:1].astype(bf16)


def turn_cot(cot_ref, src_ref, here_ref, other_ref, core_ref, out_ref, picked_ref):
    d = cot_ref.shape[3]
    parts = []
    for start in halves(core_ref, cot_ref.shape[0]):
        parts += [p.astype(bf16) for p in split_z(x_half(cot_ref, start))]
    perm = picks(src_ref, d)
    n = parts[0].shape[0]
    for i, part in enumerate(parts):
        out_ref[:, i * n : (i + 1) * n] = dot_nt(perm, part).astype(bf16)
    first = core_ref[0, 0] == 0
    pair = (here_ref[...].astype(f32), other_ref[...].astype(f32))
    pair = (jnp.where(first, pair[0], pair[1]), jnp.where(first, pair[1], pair[0]))
    line = lax.broadcasted_iota(jnp.int32, (8, d), 0)
    rows = jnp.zeros((8, d), f32)
    for i in range(4):
        rows = jnp.where(line == 2 + i, pair[i % 2][:, i // 2 * d : (i // 2 + 1) * d], rows)
    picked_ref[...] = dot_nt(rows.astype(bf16), perm[: d // 2])


def picks(src_ref, d):
    columns = lax.broadcasted_iota(jnp.int32, (d, d), 1)
    return jnp.where(columns == src_ref[...], 1.0, 0.0).astype(bf16)


def head_of(pair, half):
    lanes = lax.broadcasted_iota(jnp.int32, pair.shape, 1)
    return jnp.where((lanes < HEAD) == (half == 0), pair, jnp.zeros_like(pair))


def hide(mask_ref, refs, start):
    n = refs[0].shape[0]
    for i, ref in enumerate(refs):
        seen = ref[:, start:].astype(f32)
        mask_ref[i * n : (i + 1) * n] = jnp.where(seen > 0.5, 0.0, HIDDEN)
    mask_ref[4 * n :] = jnp.zeros((mask_ref.shape[0] - 4 * n, mask_ref.shape[1]), f32)


def attend(own_ref, up_ref, side_ref, both_ref, wi_ref, kv_ref, r0_ref, r1_ref, r2_ref, r3_ref, grad_ref, coarse_ref,
           q_ref, k_ref, v_ref, g_ref, att_ref, dk_ref, dv_ref, mask_ref):
    d, width = wi_ref.shape
    inner = width // 3
    n = own_ref.shape[0]
    tokens = 4 * n
    blocks = (own_ref, up_ref, side_ref, both_ref)
    for i, ref in enumerate(blocks):
        packed = dot(ref[:, :d], wi_ref[...])
        rows = slice(i * n, (i + 1) * n)
        q_ref[rows] = packed[:, :inner].astype(bf16) * bf16(0.125)
        k_ref[rows] = packed[:, inner : 2 * inner].astype(bf16)
        v_ref[rows] = packed[:, 2 * inner :].astype(bf16)
        g_ref[rows] = ref[:, d : d + inner]
    hide(mask_ref, blocks, d + inner)
    k_ref[tokens:] = kv_ref[:, :inner]
    v_ref[tokens:] = kv_ref[:, inner:]
    eye = jnp.where(
        lax.broadcasted_iota(jnp.int32, (PAIR, PAIR), 0)
        == lax.broadcasted_iota(jnp.int32, (PAIR, PAIR), 1), 1.0, 0.0).astype(bf16)
    chunks = tokens // CHUNK
    dk_ref[...] = jnp.zeros_like(dk_ref)
    dv_ref[...] = jnp.zeros_like(dv_ref)

    def step(i, _):
        lanes = pl.ds(pl.multiple_of(i // chunks * PAIR, PAIR), PAIR)
        rows = pl.ds(pl.multiple_of(i % chunks * CHUNK, CHUNK), CHUNK)
        keys = k_ref[:, lanes]
        vals = v_ref[:, lanes]
        keys_t = dot_nt(eye, keys).astype(bf16)
        vals_t = dot_nt(eye, vals).astype(bf16)
        queries = [head_of(q_ref[rows, lanes], half) for half in range(2)]
        gs = [head_of(g_ref[rows, lanes], half) for half in range(2)]
        found = []
        grads = []
        dv = dv_ref[:, lanes]
        dk = dk_ref[:, lanes]
        for half in range(2):
            part = slice(half * HEAD, (half + 1) * HEAD)
            s = dot_nt(keys, queries[half]) + jnp.concatenate([mask_ref[...]] * 2, axis=1)
            e = jnp.exp(s - jnp.max(s, axis=0, keepdims=True))
            prob = e * (1.0 / jnp.sum(e, axis=0, keepdims=True))
            weight = prob.astype(bf16)
            found.append(dot(vals_t[part], weight))
            dv += dot(weight, gs[half])
            spread = prob * dot_nt(vals, gs[half])
            centre = jnp.sum(spread, axis=0, keepdims=True)
            score = (spread - prob * centre).astype(bf16)
            dk += dot(score, queries[half])
            grads.append(dot(keys_t[part], score))
        dv_ref[:, lanes] = dv
        dk_ref[:, lanes] = dk
        att_ref[rows, lanes] = jnp.concatenate(found, axis=0).T.astype(bf16)
        grad_ref[rows, lanes] = (jnp.concatenate(grads, axis=0).T * 0.125).astype(bf16)
        return 0

    lax.fori_loop(0, inner // PAIR * chunks, step, 0)
    grad_ref[:, inner : 2 * inner] = dk_ref[:tokens].astype(bf16)
    grad_ref[:, 2 * inner :] = dv_ref[:tokens].astype(bf16)
    peers = coarse_ref.shape[0]
    part = jnp.concatenate([dk_ref[tokens:].astype(bf16), dv_ref[tokens:].astype(bf16)], axis=1)
    chip = lax.broadcasted_iota(jnp.int32, (peers, peers), 0) // 2 * 2
    token = lax.broadcasted_iota(jnp.int32, (peers, peers), 1)
    for i in range(2):
        pick = jnp.where(token == chip + i, 1.0, 0.0).astype(bf16)
        coarse_ref[:, i * 2 * inner : (i + 1) * 2 * inner] = dot(pick, part).astype(bf16)
    for i, ref in enumerate((r0_ref, r1_ref, r2_ref, r3_ref)):
        rows = slice(i * n, (i + 1) * n)
        ref[:, :d] = dot_nt(grad_ref[rows], wi_ref[...]).astype(bf16)
        ref[:, d:] = att_ref[rows]


def weight_grads(own_ref, up_ref, side_ref, both_ref, src_ref, grad_ref, cot_ref,
                 b0_ref, b1_ref, b2_ref, b3_ref, keep_ref, send_ref, turned_ref, att_ref):
    d = src_ref.shape[0]
    n = own_ref.shape[0]
    width = grad_ref.shape[1]
    perm = picks(src_ref, d)
    for i, ref in enumerate((own_ref, up_ref, side_ref, both_ref)):
        turned_ref[:, i * n : (i + 1) * n] = dot_nt(perm, ref[:, :d]).astype(bf16)
    for i, ref in enumerate((b0_ref, b1_ref, b2_ref, b3_ref)):
        att_ref[i * n : (i + 1) * n] = ref[:, d:]
    for ref, rows in ((keep_ref, slice(0, d // 2)), (send_ref, slice(d // 2, d))):
        ref[:, :width] = dot(turned_ref[rows], grad_ref[...]).astype(bf16)
        ref[:, width:] = dot(cot_ref[rows], att_ref[...]).astype(bf16)


def block_result(tok_ref, b0_ref, b1_ref, b2_ref, b3_ref, wo_ref, core_ref, out_ref):
    x, _, _, d = tok_ref.shape
    for start, refs in zip(halves(core_ref, x), ((b0_ref, b1_ref), (b2_ref, b3_ref))):
        branch = [dot(ref[:, d:], wo_ref[...]).astype(bf16).astype(f32) for ref in refs]
        total = x_half(tok_ref, start) + join_z(*branch)
        out_ref[pl.ds(start, x // 2)] = total.astype(bf16).reshape(
            (x // 2,) + out_ref.shape[1:])


def coarse_total(parts_ref, core_ref, pair_ref, here_ref, there_ref):
    d = parts_ref.shape[1] // 2
    parts = parts_ref[...].astype(f32)
    even = lax.broadcasted_iota(jnp.int32, parts.shape, 0) % 2 == 0
    for i, ref in ((0, here_ref), (1, there_ref)):
        total = jnp.sum(jnp.where(even == (i == 0), parts, 0.0), axis=0, keepdims=True)
        pair_ref[pl.ds(i, 1)] = total
        ref[...] = jnp.where(core_ref[0, 0] == 0, total[:, :d], total[:, d:])


def assemble(keep_ref, other_ref, pair_ref, picked_ref, out_ref):
    plane, rows, width = out_ref.shape
    rows -= 8
    line = lax.broadcasted_iota(jnp.int32, (8, width), 0)
    lanes = picked_ref.shape[1]
    picked = picked_ref[...]
    for i in range(plane):
        part = slice(i * rows, (i + 1) * rows)
        out_ref[i, :rows] = (keep_ref[part].astype(f32) + other_ref[part].astype(f32)).astype(bf16)
        extra = jnp.where(line == 0, pair_ref[0:1], jnp.where(line == 1, pair_ref[1:2], 0.0))
        out_ref[i, rows:] = extra.astype(bf16)
        mine = pltpu.roll(picked, (lanes - i * rows) % lanes, 1)[:, :128]
        out_ref[i, rows:, :128] = jnp.where(line[:, :128] < 2, extra[:, :128], mine).astype(bf16)


def plane_sums(in_ref, out_ref):
    plane, rows, width = in_ref.shape
    rows -= 8
    deep = out_ref.shape[0]
    half = width // 2
    total = jnp.sum(in_ref[:, :rows].astype(f32), axis=0)
    extra = in_ref[:, rows:].astype(f32)
    line = lax.broadcasted_iota(jnp.int32, extra.shape, 1)
    coarse = jnp.zeros((128, half), f32)
    for i in range(4):
        if i % 2 == 0:
            grads = jnp.sum(jnp.where(line == i // 2, extra, 0.0), axis=1).astype(bf16)
        picked = jnp.sum(jnp.where(line[:, :, :128] == 2 + i, extra[:, :, :128], 0.0), axis=1).astype(bf16)
        coarse += lax.dot_general(
            picked, grads[:, i % 2 * half : (i % 2 + 1) * half],
            (((0,), (0,)), ((), ())), preferred_element_type=f32)
    step = out_ref.shape[1] // (rows // deep)
    for j in range(rows // deep):
        part = slice(j * deep, (j + 1) * deep)
        out_ref[:, j * step : j * step + width] = total[part].astype(bf16)
        out_ref[:, j * step + width : (j + 1) * step] = coarse[part].astype(bf16)


def token_result(tok_ref, cot_ref, b0_ref, b1_ref, b2_ref, b3_ref, here_ref, next_ref, wc_ref, core_ref, out_ref):
    x, y, z, d = tok_ref.shape
    coarse = (here_ref[...] + next_ref[...]).astype(bf16)
    pooled = dot_nt(jnp.broadcast_to(coarse, (8, d)), wc_ref[...])[0:1]
    pooled = (pooled / float(x * y * z))[None]
    for start, refs in zip(halves(core_ref, x), ((b0_ref, b1_ref), (b2_ref, b3_ref))):
        normed, inv_std = normalize(x_half(tok_ref, start))
        grad = join_z(*[ref[:, :d].astype(f32) for ref in refs]) + pooled
        first = jnp.mean(grad, axis=-1, keepdims=True)
        second = jnp.mean(grad * normed, axis=-1, keepdims=True)
        total = x_half(cot_ref, start) + inv_std * (grad - first - normed * second)
        out_ref[pl.ds(start, x // 2)] = total.astype(bf16).reshape(
            (x // 2,) + out_ref.shape[1:])


def passed(block, step, back=False):
    nx, nz = lax.axis_size(GX), lax.axis_size(GZ)
    route = []
    for a in range(nx):
        for c in range(nz):
            to_a, to_c = step(a, c)
            route.append((a * nz + c, to_a % nx * nz + to_c % nz))
    if back:
        route = [(b, a) for a, b in route]
    return lax.ppermute(block, ALL, route)


def to_up(a, c):
    return a, c - 1


def to_side(a, c):
    return (a - 1, c) if c % 2 == 0 else (a + 1, c)


def to_both(a, c):
    return (a - 1, c - 1) if c % 2 else (a + 1, c - 1)


def returned(own, up, side, both):
    return passed(up, to_up, True), passed(side, to_side, True), passed(both, to_both, True), own


def body(tokens, body_mask, cotangent, w_in, w_out, w_coarse):
    x, y, z, d = tokens.shape
    size = x * y * z
    n = size // 4
    inner = w_out.shape[0]
    coarse = lax.axis_size(GZ)
    columns = lax.axis_size(GX)
    devices = columns * coarse
    per = d // devices
    core = lax.axis_index("core")

    wide = (n, d + inner + 128)
    place = core.reshape(1, 1)
    up, side, both, own, row = call(
        prepare, [(wide, bf16)] * 4 + [((1, 2 * d), bf16)], tokens, cotangent, w_out, w_coarse, body_mask, place,
        far=range(4),
        scalars=(5,),
        grant=60,
        scratch=[pltpu.VMEM(a.shape, bf16) for a in (tokens, cotangent, w_out, w_coarse)] + [pltpu.SemaphoreType.DMA((4,))])
    before = passed(row, lambda a, c: (a + 1, c))
    up, side, both = passed(up, to_up), passed(side, to_side), passed(both, to_both)

    odd = lax.broadcasted_iota(jnp.int32, (coarse, 1), 0) % 2 == 1
    kv = jnp.where(odd, before[:, d:], row[:, d:])
    shared = jnp.concatenate([row[:, :d], before[:, :d]], axis=1)
    shared, kv = lax.optimization_barrier((shared, kv))
    other = lax.ppermute(shared, "core", [(0, 1), (1, 0)])
    kv = lax.all_to_all(kv, GZ, 0, 0, tiled=True)
    zh, nx, zl, ny, cores = (lax.axis_size(a) for a in ALL)
    plane, deep = nx * ny, zh * zl

    row = jnp.arange(d, dtype=jnp.int32)
    half, rest = row // (d // 2), row % (d // 2)
    chip, j, depth = rest // (per * deep), rest % (per * deep) // deep, rest % deep
    device = ((depth // zl * nx + chip // ny) * zl + depth % zl) * ny + chip % ny
    src = ((device * cores + (half + core) % cores) * per + j).reshape(d, 1)
    cot_turned, picked = call(
        turn_cot, [((d, size), bf16), ((8, d // 2), f32)], cotangent, src, shared, other, place, scalars=(4,))
    kv, cot_turned = lax.optimization_barrier((kv, cot_turned))

    tall = (size + coarse, inner)
    r0, r1, r2, r3, grad, coarse_part = call(
        attend,
        [((n, d + inner), bf16)] * 4 + [((size, 3 * inner), bf16), ((coarse, 4 * inner), bf16)],
        own, up, side, both, w_in, kv,
        grant=24,
        scratch=[pltpu.VMEM(s, bf16) for s in ((size, inner), tall, tall, (size, inner), (size, inner))]
        + [pltpu.VMEM(tall, f32)] * 2 + [pltpu.VMEM((size + coarse, 128), f32)])
    e0, e1, e2, e3 = returned(r0, r1, r2, r3)
    parts = lax.all_to_all(coarse_part, GZ, 0, 0, tiled=True)

    grad, parts, e0, e1, e2 = lax.optimization_barrier((grad, parts, e0, e1, e2))
    keep, send = call(
        weight_grads, [((d // 2, 4 * inner), bf16)] * 2,
        own, up, side, both, src, grad, cot_turned, e0, e1, e2, e3,
        scratch=[pltpu.VMEM((d, size), bf16), pltpu.VMEM((size, inner), bf16)])
    other = lax.ppermute(send, "core", [(0, 1), (1, 0)])
    pair, here, there = call(
        coarse_total, [((2, 4 * inner), f32), ((1, d), f32), ((1, d), f32)], parts, place, scalars=(1,))
    later = passed(there, lambda a, c: (a - 1, c))

    (packet,) = call(
        assemble, [((plane, per * deep + 8, 4 * inner), bf16)], keep, other, pair, picked)
    packet, later = lax.optimization_barrier((packet, later))
    packet = lax.all_to_all(packet, ("x", "y"), 0, 0, tiled=True)
    (slab,) = call(plane_sums, [((deep, per * 6 * inner), bf16)], packet)
    slab = lax.all_to_all(slab, ("zh", "zl"), 0, 0, tiled=True)

    (block_out,) = call(block_result, [(tokens.shape, bf16)], tokens, e0, e1, e2, e3, w_out, place, scalars=(6,))
    (token_grad,) = call(token_result, [(tokens.shape, bf16)], tokens, cotangent, e0, e1, e2, e3,
        here, later, w_coarse, place, scalars=(9,))

    summed = jnp.sum(slab.astype(f32), axis=0).reshape(per, 6 * inner)
    input_grad = summed[:, : 3 * inner]
    output_grad = summed[:, 3 * inner : 4 * inner].T
    coarse_grad = summed[:, 4 * inner :]
    return (block_out, token_grad, input_grad, output_grad, coarse_grad)


def solution(mesh):
    fine = Mesh(mesh.devices.reshape(2, 4, 4, 4, 2), ALL)
    grid = P(GX, None, GZ, None)
    return jax.shard_map(
        body,
        mesh=fine,
        in_specs=(grid, P(GX, None, GZ), grid, P(), P(), P()),
        out_specs=(grid, grid, P(ALL, None), P(None, ALL), P(ALL, None)),
        check_vma=False,
    )
```

```python
import functools

import jax
import jax.numpy as jnp
from jax import lax
from jax.experimental import pallas as pl
from jax.experimental.pallas import tpu as pltpu
from jax.sharding import Mesh
from jax.sharding import PartitionSpec as P

HEAD = 64
PAIR = 2 * HEAD
CHUNK = 512
HIDDEN = -1e30
GX = ("zh", "x")
GZ = ("zl", "y", "core")
ALL = GX + GZ
bf16 = jnp.bfloat16
f32 = jnp.float32


def dot(left, side):
    return jnp.dot(left, side, preferred_element_type=f32)


def dot_nt(left, side):
    return lax.dot_general(left, side, (((1,), (1,)), ((), ())), preferred_element_type=f32)


def call(kernel, outs, *args, scratch=(), far=(), scalars=(), grant=16):
    return pl.pallas_call(
        kernel,
        out_shape=[jax.ShapeDtypeStruct(s, d) for s, d in outs],
        in_specs=[
            pl.BlockSpec(memory_space=pltpu.HBM if i in far else pltpu.SMEM if i in scalars else pltpu.VMEM) for i in range(len(args))
        ],
        scratch_shapes=list(scratch),
        compiler_params=pltpu.CompilerParams(vmem_limit_bytes=grant * 2**20),
        cost_estimate=pl.CostEstimate(flops=1, bytes_accessed=1, transcendentals=0),
    )(*args)


def normalize(values):
    centre = values - jnp.mean(values, axis=-1, keepdims=True)
    inv_std = lax.rsqrt(jnp.mean(centre * centre, axis=-1, keepdims=True) + 1e-05)
    return centre * inv_std, inv_std


def low_rows(shape):
    return lax.broadcasted_iota(jnp.int32, shape, 1) < shape[1] // 2


def split_z(rows):
    m, z, d = rows.shape[0] // 2, rows.shape[1], rows.shape[2]
    pairs = rows.reshape(m, 2, z, d)
    a, b = pairs[:, 0], pairs[:, 1]
    low = low_rows(a.shape)
    lower = jnp.where(low, a, pltpu.roll(b, z // 2, 1))
    upper = jnp.where(low, pltpu.roll(a, z // 2, 1), b)
    return lower.reshape(m * z, d), upper.reshape(m * z, d)


def join_z(lower, upper):
    m, d = lower.shape[0] // 8, lower.shape[1]
    lower, upper = lower.reshape(m, 8, d), upper.reshape(m, 8, d)
    low = low_rows(lower.shape)
    a = jnp.where(low, lower, pltpu.roll(upper, 4, 1))
    b = jnp.where(low, pltpu.roll(lower, 4, 1), upper)
    return jnp.stack([a, b], axis=1).reshape(2 * m, 8, d)


def halves(core_ref, x):
    far = core_ref[0, 0] * (x // 2)
    return far, x // 2 - far


def x_half(ref, start):
    x, y, z, d = ref.shape
    return ref[pl.ds(start, x // 2)].astype(f32).reshape(x // 2 * y, z, d)


def columns_of(mask):
    m, z = mask.shape
    rows = jnp.broadcast_to(mask[:, None, :], (m, z, z))
    shape = (m, z, z)
    same = lax.broadcasted_iota(jnp.int32, shape, 1) == lax.broadcasted_iota(jnp.int32, shape, 2)
    column = jnp.sum(jnp.where(same, rows, 0.0), axis=2, keepdims=True)
    return jnp.broadcast_to(column, (m, z, 128))


def prepare(*refs):
    sources, mask_ref, core_ref, refs = refs[:4], refs[4], refs[5], refs[6:]
    outs, held, sems = refs[:5], refs[5:9], refs[9]
    up_ref, side_ref, both_ref, own_ref, coarse_ref = outs
    tok_ref, cot_ref, wo_ref, wc_ref = held
    copies = [pltpu.make_async_copy(a, b, sems.at[i]) for i, (a, b) in enumerate(zip(sources, held))]
    for copy in copies:
        copy.start()
    copies[0].wait()
    inner, d = wo_ref.shape
    total = jnp.zeros((1, d), f32)
    cells = 1
    for n in tok_ref.shape[:3]:
        cells *= n
    away, home = halves(core_ref, tok_ref.shape[0])
    places = ((away, (up_ref, side_ref)), (home, (both_ref, own_ref)))
    for start, refs in places:
        normed, _ = normalize(x_half(tok_ref, start))
        total += jnp.sum(jnp.sum(normed, axis=0), axis=0, keepdims=True)
        for ref, part in zip(refs, split_z(normed)):
            ref[:, :d] = part.astype(bf16)
        x, y, z = mask_ref.shape
        cells_in = mask_ref[pl.ds(start, x // 2)].astype(f32)
        for ref, part in zip(refs, split_z(columns_of(cells_in.reshape(x // 2 * y, z)))):
            ref[:, d + inner :] = part.astype(bf16)
    copies[1].wait()
    copies[2].wait()
    for start, refs in places:
        for ref, part in zip(refs, split_z(x_half(cot_ref, start))):
            ref[:, d : d + inner] = dot_nt(part.astype(bf16), wo_ref[...]).astype(bf16)
    copies[3].wait()
    pooled = (total / cells).astype(bf16)
    coarse_ref[:, :d] = pooled
    coarse_ref[:, d:] = dot(jnp.broadcast_to(pooled, (8, d)), wc_ref[...])[:1].astype(bf16)


def turn_cot(cot_ref, src_ref, here_ref, other_ref, core_ref, out_ref, picked_ref):
    d = cot_ref.shape[3]
    parts = []
    for start in halves(core_ref, cot_ref.shape[0]):
        parts += [p.astype(bf16) for p in split_z(x_half(cot_ref, start))]
    perm = picks(src_ref, d)
    n = parts[0].shape[0]
    for i, part in enumerate(parts):
        out_ref[:, i * n : (i + 1) * n] = dot_nt(perm, part).astype(bf16)
    first = core_ref[0, 0] == 0
    pair = (here_ref[...].astype(f32), other_ref[...].astype(f32))
    pair = (jnp.where(first, pair[0], pair[1]), jnp.where(first, pair[1], pair[0]))
    line = lax.broadcasted_iota(jnp.int32, (8, d), 0)
    rows = jnp.zeros((8, d), f32)
    for i in range(4):
        rows = jnp.where(line == 2 + i, pair[i % 2][:, i // 2 * d : (i // 2 + 1) * d], rows)
    picked_ref[...] = dot_nt(rows.astype(bf16), perm[: d // 2])


def picks(src_ref, d):
    columns = lax.broadcasted_iota(jnp.int32, (d, d), 1)
    return jnp.where(columns == src_ref[...], 1.0, 0.0).astype(bf16)


def head_of(pair, half):
    lanes = lax.broadcasted_iota(jnp.int32, pair.shape, 1)
    return jnp.where((lanes < HEAD) == (half == 0), pair, jnp.zeros_like(pair))


def hide(mask_ref, refs, start):
    n = refs[0].shape[0]
    for i, ref in enumerate(refs):
        seen = ref[:, start:].astype(f32)
        mask_ref[i * n : (i + 1) * n] = jnp.where(seen > 0.5, 0.0, HIDDEN)
    mask_ref[4 * n :] = jnp.zeros((mask_ref.shape[0] - 4 * n, mask_ref.shape[1]), f32)


def project(own_ref, up_ref, side_ref, both_ref, wi_ref, src_ref, q_ref, k_ref, v_ref, g_ref, mask_ref, turned_ref):
    d, width = wi_ref.shape
    inner = width // 3
    n = own_ref.shape[0]
    blocks = (own_ref, up_ref, side_ref, both_ref)
    perm = picks(src_ref, d)
    for i, ref in enumerate(blocks):
        packed = dot(ref[:, :d], wi_ref[...])
        rows = slice(i * n, (i + 1) * n)
        q_ref[rows] = packed[:, :inner].astype(bf16) * bf16(0.125)
        k_ref[rows] = packed[:, inner : 2 * inner].astype(bf16)
        v_ref[rows] = packed[:, 2 * inner :].astype(bf16)
        g_ref[rows] = ref[:, d : d + inner]
        turned_ref[:, rows] = dot_nt(perm, ref[:, :d]).astype(bf16)
    hide(mask_ref, blocks, d + inner)


def attend(q_ref, kw_ref, vw_ref, g_ref, mask_ref, wi_ref, kv_ref, r0_ref, r1_ref, r2_ref, r3_ref, grad_ref, coarse_ref,
           k_ref, v_ref, att_ref, dk_ref, dv_ref):
    d, width = wi_ref.shape
    inner = width // 3
    tokens = q_ref.shape[0]
    n = tokens // 4
    k_ref[:tokens] = kw_ref[...]
    v_ref[:tokens] = vw_ref[...]
    k_ref[tokens:] = kv_ref[:, :inner]
    v_ref[tokens:] = kv_ref[:, inner:]
    eye = jnp.where(
        lax.broadcasted_iota(jnp.int32, (PAIR, PAIR), 0)
        == lax.broadcasted_iota(jnp.int32, (PAIR, PAIR), 1), 1.0, 0.0).astype(bf16)
    chunks = tokens // CHUNK
    dk_ref[...] = jnp.zeros_like(dk_ref)
    dv_ref[...] = jnp.zeros_like(dv_ref)

    def step(i, _):
        lanes = pl.ds(pl.multiple_of(i // chunks * PAIR, PAIR), PAIR)
        rows = pl.ds(pl.multiple_of(i % chunks * CHUNK, CHUNK), CHUNK)
        keys = k_ref[:, lanes]
        vals = v_ref[:, lanes]
        keys_t = dot_nt(eye, keys).astype(bf16)
        vals_t = dot_nt(eye, vals).astype(bf16)
        queries = [head_of(q_ref[rows, lanes], half) for half in range(2)]
        gs = [head_of(g_ref[rows, lanes], half) for half in range(2)]
        found = []
        grads = []
        dv = dv_ref[:, lanes]
        dk = dk_ref[:, lanes]
        for half in range(2):
            part = slice(half * HEAD, (half + 1) * HEAD)
            s = dot_nt(keys, queries[half]) + jnp.concatenate([mask_ref[...]] * (CHUNK // 128), axis=1)
            e = jnp.exp(s - jnp.max(s, axis=0, keepdims=True))
            prob = e * (1.0 / jnp.sum(e, axis=0, keepdims=True))
            weight = prob.astype(bf16)
            found.append(dot(vals_t[part], weight))
            dv += dot(weight, gs[half])
            spread = prob * dot_nt(vals, gs[half])
            centre = jnp.sum(spread, axis=0, keepdims=True)
            score = (spread - prob * centre).astype(bf16)
            dk += dot(score, queries[half])
            grads.append(dot(keys_t[part], score))
        dv_ref[:, lanes] = dv
        dk_ref[:, lanes] = dk
        att_ref[rows, lanes] = jnp.concatenate(found, axis=0).T.astype(bf16)
        grad_ref[rows, lanes] = (jnp.concatenate(grads, axis=0).T * 0.125).astype(bf16)
        return 0

    lax.fori_loop(0, inner // PAIR * chunks, step, 0)
    grad_ref[:, inner : 2 * inner] = dk_ref[:tokens].astype(bf16)
    grad_ref[:, 2 * inner :] = dv_ref[:tokens].astype(bf16)
    peers = coarse_ref.shape[0]
    part = jnp.concatenate([dk_ref[tokens:].astype(bf16), dv_ref[tokens:].astype(bf16)], axis=1)
    chip = lax.broadcasted_iota(jnp.int32, (peers, peers), 0) // 2 * 2
    token = lax.broadcasted_iota(jnp.int32, (peers, peers), 1)
    for i in range(2):
        pick = jnp.where(token == chip + i, 1.0, 0.0).astype(bf16)
        coarse_ref[:, i * 2 * inner : (i + 1) * 2 * inner] = dot(pick, part).astype(bf16)
    for i, ref in enumerate((r0_ref, r1_ref, r2_ref, r3_ref)):
        rows = slice(i * n, (i + 1) * n)
        ref[:, :d] = dot_nt(grad_ref[rows], wi_ref[...]).astype(bf16)
        ref[:, d:] = att_ref[rows]


def weight_grads(turned_ref, grad_ref, cot_ref, b0_ref, b1_ref, b2_ref, b3_ref, keep_ref, send_ref, att_ref):
    d = turned_ref.shape[0]
    n = b0_ref.shape[0]
    width = grad_ref.shape[1]
    for i, ref in enumerate((b0_ref, b1_ref, b2_ref, b3_ref)):
        att_ref[i * n : (i + 1) * n] = ref[:, d:]
    for ref, rows in ((keep_ref, slice(0, d // 2)), (send_ref, slice(d // 2, d))):
        ref[:, :width] = dot(turned_ref[rows], grad_ref[...]).astype(bf16)
        ref[:, width:] = dot(cot_ref[rows], att_ref[...]).astype(bf16)


def block_result(tok_ref, b0_ref, b1_ref, b2_ref, b3_ref, wo_ref, core_ref, out_ref):
    x, _, _, d = tok_ref.shape
    for start, refs in zip(halves(core_ref, x), ((b0_ref, b1_ref), (b2_ref, b3_ref))):
        branch = [dot(ref[:, d:], wo_ref[...]).astype(bf16).astype(f32) for ref in refs]
        total = x_half(tok_ref, start) + join_z(*branch)
        out_ref[pl.ds(start, x // 2)] = total.astype(bf16).reshape(
            (x // 2,) + out_ref.shape[1:])


def coarse_total(parts_ref, core_ref, pair_ref, here_ref, there_ref):
    d = parts_ref.shape[1] // 2
    parts = parts_ref[...].astype(f32)
    even = lax.broadcasted_iota(jnp.int32, parts.shape, 0) % 2 == 0
    for i, ref in ((0, here_ref), (1, there_ref)):
        total = jnp.sum(jnp.where(even == (i == 0), parts, 0.0), axis=0, keepdims=True)
        pair_ref[pl.ds(i, 1)] = total
        ref[...] = jnp.where(core_ref[0, 0] == 0, total[:, :d], total[:, d:])


def assemble(keep_ref, other_ref, pair_ref, picked_ref, out_ref, pair_rows):
    plane, rows, width = out_ref.shape
    width -= 256
    lanes = picked_ref.shape[1]
    per_row = width // 128
    for i in range(rows):
        at = i % per_row * 128
        pair_rows[i : i + 1] = pair_ref[i // per_row : i // per_row + 1, at : at + 128]
    pairs = pair_rows[...]
    picked = picked_ref[...]
    empty = jnp.zeros((rows - 8, 128), f32)
    for i in range(plane):
        part = slice(i * rows, (i + 1) * rows)
        out_ref[i, :, :width] = (keep_ref[part].astype(f32) + other_ref[part].astype(f32)).astype(bf16)
        mine = pltpu.roll(picked, (lanes - i * rows) % lanes, 1)[:, :128]
        beside = jnp.concatenate([pairs, jnp.concatenate([mine, empty], axis=0)], axis=1)
        out_ref[i, :, width:] = beside.astype(bf16)


def place_of(tile, tiles):
    return tile // tiles, tile % tiles * 128


def plane_sums(in_ref, out_ref, flat_ref):
    plane, rows, width = in_ref.shape
    width -= 256
    deep, lines, lanes = out_ref.shape
    half = width // 2
    total = jnp.sum(in_ref[:, :, :width].astype(f32), axis=0)
    pairs = in_ref[:, :, width : width + 128].astype(f32)
    picked = in_ref[:, :8, width + 128 :].astype(f32)
    line = lax.broadcasted_iota(jnp.int32, picked.shape, 1)

    def row(block, i):
        return jnp.sum(jnp.where(line == i, block, 0.0), axis=1).astype(bf16)

    coarse = jnp.zeros((128, half), f32)
    tiles = half // 128
    for i in range(4):
        grads = [row(pairs[:, q // 8 * 8 : q // 8 * 8 + 8], q % 8) for q in range(i * tiles, (i + 1) * tiles)]
        coarse += lax.dot_general(
            row(picked, 2 + i), jnp.concatenate(grads, axis=1),
            (((0,), (0,)), ((), ())), preferred_element_type=f32)
    flat_ref[...] = jnp.zeros_like(flat_ref)
    tile = 0
    for j in range(rows // deep):
        part = slice(j * deep, (j + 1) * deep)
        for block in (total[part], coarse[part]):
            for at in range(0, block.shape[1], 128):
                r, lane = place_of(tile, lanes // 128)
                flat_ref[lane // 128, pl.ds(r, deep, stride=lines), :] = block[:, at : at + 128]
                tile += 1
    for i in range(lanes // 128):
        out_ref[:, :, i * 128 : (i + 1) * 128] = flat_ref[i].reshape(deep, lines, 128).astype(bf16)


def depth_sums(in_ref, *outs):
    total = jnp.sum(in_ref[...].astype(f32), axis=0)
    tile = 0
    for j in range(outs[0].shape[0]):
        for ref in outs:
            for at in range(0, ref.shape[1], 128):
                r, lane = place_of(tile, total.shape[1] // 128)
                ref[j : j + 1, at : at + 128] = total[r : r + 1, lane : lane + 128]
                tile += 1


def token_result(tok_ref, cot_ref, b0_ref, b1_ref, b2_ref, b3_ref, here_ref, next_ref, wc_ref, core_ref, out_ref):
    x, y, z, d = tok_ref.shape
    coarse = (here_ref[...] + next_ref[...]).astype(bf16)
    pooled = dot_nt(jnp.broadcast_to(coarse, (8, d)), wc_ref[...])[0:1]
    pooled = (pooled / float(x * y * z))[None]
    for start, refs in zip(halves(core_ref, x), ((b0_ref, b1_ref), (b2_ref, b3_ref))):
        normed, inv_std = normalize(x_half(tok_ref, start))
        grad = join_z(*[ref[:, :d].astype(f32) for ref in refs]) + pooled
        first = jnp.mean(grad, axis=-1, keepdims=True)
        second = jnp.mean(grad * normed, axis=-1, keepdims=True)
        total = x_half(cot_ref, start) + inv_std * (grad - first - normed * second)
        out_ref[pl.ds(start, x // 2)] = total.astype(bf16).reshape(
            (x // 2,) + out_ref.shape[1:])


def passed(block, step, back=False):
    nx, nz = lax.axis_size(GX), lax.axis_size(GZ)
    route = []
    for a in range(nx):
        for c in range(nz):
            to_a, to_c = step(a, c)
            route.append((a * nz + c, to_a % nx * nz + to_c % nz))
    if back:
        route = [(b, a) for a, b in route]
    return lax.ppermute(block, ALL, route)


def to_up(a, c):
    return a, c - 1


def to_side(a, c):
    return (a - 1, c) if c % 2 == 0 else (a + 1, c)


def to_both(a, c):
    return (a - 1, c - 1) if c % 2 else (a + 1, c - 1)


def returned(own, up, side, both):
    return passed(up, to_up, True), passed(side, to_side, True), passed(both, to_both, True), own


def body(tokens, body_mask, cotangent, w_in, w_out, w_coarse):
    x, y, z, d = tokens.shape
    size = x * y * z
    n = size // 4
    inner = w_out.shape[0]
    coarse = lax.axis_size(GZ)
    columns = lax.axis_size(GX)
    devices = columns * coarse
    per = d // devices
    core = lax.axis_index("core")

    wide = (n, d + inner + 128)
    place = core.reshape(1, 1)
    up, side, both, own, row = call(
        prepare, [(wide, bf16)] * 4 + [((1, 2 * d), bf16)], tokens, cotangent, w_out, w_coarse, body_mask, place,
        far=range(4),
        scalars=(5,),
        grant=60,
        scratch=[pltpu.VMEM(a.shape, bf16) for a in (tokens, cotangent, w_out, w_coarse)] + [pltpu.SemaphoreType.DMA((4,))])
    before = passed(row, lambda a, c: (a + 1, c))
    up, side, both = passed(up, to_up), passed(side, to_side), passed(both, to_both)

    odd = lax.broadcasted_iota(jnp.int32, (coarse, 1), 0) % 2 == 1
    kv = jnp.where(odd, before[:, d:], row[:, d:])
    shared = jnp.concatenate([row[:, :d], before[:, :d]], axis=1)
    shared, kv = lax.optimization_barrier((shared, kv))
    other = lax.ppermute(shared, "core", [(0, 1), (1, 0)])
    kv = lax.all_to_all(kv, GZ, 0, 0, tiled=True)
    zh, nx, zl, ny, cores = (lax.axis_size(a) for a in ALL)
    plane, deep = nx * ny, zh * zl

    row = jnp.arange(d, dtype=jnp.int32)
    half, rest = row // (d // 2), row % (d // 2)
    chip, j, depth = rest // (per * deep), rest % (per * deep) // deep, rest % deep
    device = ((depth // zl * nx + chip // ny) * zl + depth % zl) * ny + chip % ny
    src = ((device * cores + (half + core) % cores) * per + j).reshape(d, 1)
    cot_turned, picked = call(
        turn_cot, [((d, size), bf16), ((8, d // 2), f32)], cotangent, src, shared, other, place, scalars=(4,))
    kv, cot_turned = lax.optimization_barrier((kv, cot_turned))

    flat, tall = (size, inner), (size + coarse, inner)
    q, k, v, g, mask, win_turned = call(
        project, [(flat, bf16)] * 4 + [((size + coarse, 128), f32), ((d, size), bf16)],
        own, up, side, both, w_in, src)
    r0, r1, r2, r3, grad, coarse_part = call(
        attend,
        [((n, d + inner), bf16)] * 4 + [((size, 3 * inner), bf16), ((coarse, 4 * inner), bf16)],
        q, k, v, g, mask, w_in, kv,
        grant=24,
        scratch=[pltpu.VMEM(s, bf16) for s in (tall, tall, flat)] + [pltpu.VMEM(tall, f32)] * 2)
    e0, e1, e2, e3 = returned(r0, r1, r2, r3)
    parts = lax.all_to_all(coarse_part, GZ, 0, 0, tiled=True)

    grad, parts, e0, e1, e2 = lax.optimization_barrier((grad, parts, e0, e1, e2))
    keep, send = call(
        weight_grads, [((d // 2, 4 * inner), bf16)] * 2,
        win_turned, grad, cot_turned, e0, e1, e2, e3, scratch=[pltpu.VMEM((size, inner), bf16)])
    other = lax.ppermute(send, "core", [(0, 1), (1, 0)])
    pair, here, there = call(
        coarse_total, [((2, 4 * inner), f32), ((1, d), f32), ((1, d), f32)], parts, place, scalars=(1,))
    later = passed(there, lambda a, c: (a - 1, c))

    (packet,) = call(
        assemble, [((plane, per * deep, 4 * inner + 256), bf16)], keep, other, pair, picked,
        scratch=[pltpu.VMEM((per * deep, 128), f32)])
    packet = lax.all_to_all(packet, ("x", "y"), 0, 0, tiled=True)
    tiles = -(-per * 6 * inner // 1024)
    (slab,) = call(
        plane_sums, [((deep, 8, tiles * 128), bf16)], packet, scratch=[pltpu.VMEM((tiles, deep * 8, 128), f32)])
    slab = lax.all_to_all(slab, ("zh", "zl"), 0, 0, tiled=True)

    (block_out,) = call(block_result, [(tokens.shape, bf16)], tokens, e0, e1, e2, e3, w_out, place, scalars=(6,))
    (token_grad,) = call(token_result, [(tokens.shape, bf16)], tokens, cotangent, e0, e1, e2, e3,
        here, later, w_coarse, place, scalars=(9,))

    input_grad, output_grad, coarse_grad = call(
        depth_sums, [((per, 3 * inner), f32), ((per, inner), f32), ((per, 2 * inner), f32)], slab)
    output_grad = output_grad.T
    return (block_out, token_grad, input_grad, output_grad, coarse_grad)


def solution(mesh):
    fine = Mesh(mesh.devices.reshape(2, 4, 4, 4, 2), ALL)
    grid = P(GX, None, GZ, None)
    return jax.shard_map(
        body,
        mesh=fine,
        in_specs=(grid, P(GX, None, GZ), grid, P(), P(), P()),
        out_specs=(grid, grid, P(ALL, None), P(None, ALL), P(ALL, None)),
        check_vma=False,
    )
```

```python
import functools

import jax
import jax.numpy as jnp
from jax import lax
from jax.experimental import pallas as pl
from jax.experimental.pallas import tpu as pltpu
from jax.sharding import Mesh
from jax.sharding import PartitionSpec as P

HEAD = 64
PAIR = 2 * HEAD
CHUNK = 512
HIDDEN = -1e30
GX = ("zh", "x")
GZ = ("zl", "y", "core")
ALL = GX + GZ
bf16 = jnp.bfloat16
f32 = jnp.float32


def dot(left, side):
    return jnp.dot(left, side, preferred_element_type=f32)


def dot_nt(left, side):
    return lax.dot_general(left, side, (((1,), (1,)), ((), ())), preferred_element_type=f32)


def call(kernel, outs, *args, scratch=(), far=(), scalars=(), grant=16):
    return pl.pallas_call(
        kernel,
        out_shape=[jax.ShapeDtypeStruct(s, d) for s, d in outs],
        in_specs=[
            pl.BlockSpec(memory_space=pltpu.HBM if i in far else pltpu.SMEM if i in scalars else pltpu.VMEM) for i in range(len(args))
        ],
        scratch_shapes=list(scratch),
        compiler_params=pltpu.CompilerParams(vmem_limit_bytes=grant * 2**20),
        cost_estimate=pl.CostEstimate(flops=1, bytes_accessed=1, transcendentals=0),
    )(*args)


def normalize(values):
    centre = values - jnp.mean(values, axis=-1, keepdims=True)
    inv_std = lax.rsqrt(jnp.mean(centre * centre, axis=-1, keepdims=True) + 1e-05)
    return centre * inv_std, inv_std


def low_rows(shape):
    return lax.broadcasted_iota(jnp.int32, shape, 1) < shape[1] // 2


def split_z(rows):
    m, z, d = rows.shape[0] // 2, rows.shape[1], rows.shape[2]
    pairs = rows.reshape(m, 2, z, d)
    a, b = pairs[:, 0], pairs[:, 1]
    low = low_rows(a.shape)
    lower = jnp.where(low, a, pltpu.roll(b, z // 2, 1))
    upper = jnp.where(low, pltpu.roll(a, z // 2, 1), b)
    return lower.reshape(m * z, d), upper.reshape(m * z, d)


def join_z(lower, upper):
    m, d = lower.shape[0] // 8, lower.shape[1]
    lower, upper = lower.reshape(m, 8, d), upper.reshape(m, 8, d)
    low = low_rows(lower.shape)
    a = jnp.where(low, lower, pltpu.roll(upper, 4, 1))
    b = jnp.where(low, pltpu.roll(lower, 4, 1), upper)
    return jnp.stack([a, b], axis=1).reshape(2 * m, 8, d)


def halves(core_ref, x):
    far = core_ref[0, 0] * (x // 2)
    return far, x // 2 - far


def x_half(ref, start):
    x, y, z, d = ref.shape
    return ref[pl.ds(start, x // 2)].astype(f32).reshape(x // 2 * y, z, d)


def columns_of(mask):
    m, z = mask.shape
    rows = jnp.broadcast_to(mask[:, None, :], (m, z, z))
    shape = (m, z, z)
    same = lax.broadcasted_iota(jnp.int32, shape, 1) == lax.broadcasted_iota(jnp.int32, shape, 2)
    column = jnp.sum(jnp.where(same, rows, 0.0), axis=2, keepdims=True)
    return jnp.broadcast_to(column, (m, z, 128))


def prepare(*refs):
    sources, mask_ref, core_ref, refs = refs[:4], refs[4], refs[5], refs[6:]
    outs, held, sems = refs[:5], refs[5:9], refs[9]
    up_ref, side_ref, both_ref, own_ref, coarse_ref = outs
    tok_ref, cot_ref, wo_ref, wc_ref = held
    copies = [pltpu.make_async_copy(a, b, sems.at[i]) for i, (a, b) in enumerate(zip(sources, held))]
    for copy in copies:
        copy.start()
    copies[0].wait()
    inner, d = wo_ref.shape
    total = jnp.zeros((1, d), f32)
    cells = 1
    for n in tok_ref.shape[:3]:
        cells *= n
    away, home = halves(core_ref, tok_ref.shape[0])
    places = ((away, (up_ref, side_ref)), (home, (both_ref, own_ref)))
    for start, refs in places:
        normed, _ = normalize(x_half(tok_ref, start))
        total += jnp.sum(jnp.sum(normed, axis=0), axis=0, keepdims=True)
        for ref, part in zip(refs, split_z(normed)):
            ref[:, :d] = part.astype(bf16)
        x, y, z = mask_ref.shape
        cells_in = mask_ref[pl.ds(start, x // 2)].astype(f32)
        for ref, part in zip(refs, split_z(columns_of(cells_in.reshape(x // 2 * y, z)))):
            ref[:, d + inner :] = part.astype(bf16)
    copies[1].wait()
    copies[2].wait()
    for start, refs in places:
        for ref, part in zip(refs, split_z(x_half(cot_ref, start))):
            ref[:, d : d + inner] = dot_nt(part.astype(bf16), wo_ref[...]).astype(bf16)
    copies[3].wait()
    pooled = (total / cells).astype(bf16)
    coarse_ref[:, :d] = pooled
    coarse_ref[:, d:] = dot(jnp.broadcast_to(pooled, (8, d)), wc_ref[...])[:1].astype(bf16)


def turn_cot(cot_ref, src_ref, here_ref, other_ref, core_ref, out_ref, picked_ref):
    d = cot_ref.shape[3]
    parts = []
    for start in halves(core_ref, cot_ref.shape[0]):
        parts += [p.astype(bf16) for p in split_z(x_half(cot_ref, start))]
    perm = picks(src_ref, d)
    n = parts[0].shape[0]
    for i, part in enumerate(parts):
        out_ref[:, i * n : (i + 1) * n] = dot_nt(perm, part).astype(bf16)
    first = core_ref[0, 0] == 0
    pair = (here_ref[...].astype(f32), other_ref[...].astype(f32))
    pair = (jnp.where(first, pair[0], pair[1]), jnp.where(first, pair[1], pair[0]))
    line = lax.broadcasted_iota(jnp.int32, (8, d), 0)
    rows = jnp.zeros((8, d), f32)
    for i in range(4):
        rows = jnp.where(line == 2 + i, pair[i % 2][:, i // 2 * d : (i // 2 + 1) * d], rows)
    picked_ref[...] = dot_nt(rows.astype(bf16), perm[: d // 2])


def picks(src_ref, d):
    columns = lax.broadcasted_iota(jnp.int32, (d, d), 1)
    return jnp.where(columns == src_ref[...], 1.0, 0.0).astype(bf16)


def head_of(pair, half):
    lanes = lax.broadcasted_iota(jnp.int32, pair.shape, 1)
    return jnp.where((lanes < HEAD) == (half == 0), pair, jnp.zeros_like(pair))


def hide(mask_ref, refs, start):
    n = refs[0].shape[0]
    for i, ref in enumerate(refs):
        seen = ref[:, start:].astype(f32)
        mask_ref[i * n : (i + 1) * n] = jnp.where(seen > 0.5, 0.0, HIDDEN)
    mask_ref[4 * n :] = jnp.zeros((mask_ref.shape[0] - 4 * n, mask_ref.shape[1]), f32)


def project(own_ref, up_ref, side_ref, both_ref, wi_ref, src_ref, q_ref, k_ref, v_ref, g_ref, mask_ref, turned_ref):
    d, width = wi_ref.shape
    inner = width // 3
    n = own_ref.shape[0]
    blocks = (own_ref, up_ref, side_ref, both_ref)
    perm = picks(src_ref, d)
    for i, ref in enumerate(blocks):
        packed = dot(ref[:, :d], wi_ref[...])
        rows = slice(i * n, (i + 1) * n)
        q_ref[rows] = packed[:, :inner].astype(bf16) * bf16(0.125)
        k_ref[rows] = packed[:, inner : 2 * inner].astype(bf16)
        v_ref[rows] = packed[:, 2 * inner :].astype(bf16)
        g_ref[rows] = ref[:, d : d + inner]
        turned_ref[:, rows] = dot_nt(perm, ref[:, :d]).astype(bf16)
    hide(mask_ref, blocks, d + inner)


def attend(q_ref, kw_ref, vw_ref, g_ref, mask_ref, wi_ref, kv_ref, turned_ref,
           r0_ref, r1_ref, r2_ref, r3_ref, keep_ref, send_ref, coarse_ref,
           k_ref, v_ref, att_ref, grad_ref, dk_ref, dv_ref):
    d, width = wi_ref.shape
    inner = width // 3
    tokens = q_ref.shape[0]
    n = tokens // 4
    k_ref[:tokens] = kw_ref[...]
    v_ref[:tokens] = vw_ref[...]
    k_ref[tokens:] = kv_ref[:, :inner]
    v_ref[tokens:] = kv_ref[:, inner:]
    eye = jnp.where(
        lax.broadcasted_iota(jnp.int32, (PAIR, PAIR), 0)
        == lax.broadcasted_iota(jnp.int32, (PAIR, PAIR), 1), 1.0, 0.0).astype(bf16)
    chunks = tokens // CHUNK
    dk_ref[...] = jnp.zeros_like(dk_ref)
    dv_ref[...] = jnp.zeros_like(dv_ref)

    def step(i, _):
        lanes = pl.ds(pl.multiple_of(i // chunks * PAIR, PAIR), PAIR)
        rows = pl.ds(pl.multiple_of(i % chunks * CHUNK, CHUNK), CHUNK)
        keys = k_ref[:, lanes]
        vals = v_ref[:, lanes]
        keys_t = dot_nt(eye, keys).astype(bf16)
        vals_t = dot_nt(eye, vals).astype(bf16)
        queries = [head_of(q_ref[rows, lanes], half) for half in range(2)]
        gs = [head_of(g_ref[rows, lanes], half) for half in range(2)]
        found = []
        grads = []
        dv = dv_ref[:, lanes]
        dk = dk_ref[:, lanes]
        for half in range(2):
            part = slice(half * HEAD, (half + 1) * HEAD)
            s = dot_nt(keys, queries[half]) + jnp.concatenate([mask_ref[...]] * (CHUNK // 128), axis=1)
            e = jnp.exp(s - jnp.max(s, axis=0, keepdims=True))
            prob = e * (1.0 / jnp.sum(e, axis=0, keepdims=True))
            weight = prob.astype(bf16)
            found.append(dot(vals_t[part], weight))
            dv += dot(weight, gs[half])
            spread = prob * dot_nt(vals, gs[half])
            centre = jnp.sum(spread, axis=0, keepdims=True)
            score = (spread - prob * centre).astype(bf16)
            dk += dot(score, queries[half])
            grads.append(dot(keys_t[part], score))
        dv_ref[:, lanes] = dv
        dk_ref[:, lanes] = dk
        att_ref[rows, lanes] = jnp.concatenate(found, axis=0).T.astype(bf16)
        grad_ref[rows, lanes] = (jnp.concatenate(grads, axis=0).T * 0.125).astype(bf16)
        return 0

    lax.fori_loop(0, inner // PAIR * chunks, step, 0)
    grad_ref[:, inner : 2 * inner] = dk_ref[:tokens].astype(bf16)
    grad_ref[:, 2 * inner :] = dv_ref[:tokens].astype(bf16)
    peers = coarse_ref.shape[0]
    part = jnp.concatenate([dk_ref[tokens:].astype(bf16), dv_ref[tokens:].astype(bf16)], axis=1)
    chip = lax.broadcasted_iota(jnp.int32, (peers, peers), 0) // 2 * 2
    token = lax.broadcasted_iota(jnp.int32, (peers, peers), 1)
    for i in range(2):
        pick = jnp.where(token == chip + i, 1.0, 0.0).astype(bf16)
        coarse_ref[:, i * 2 * inner : (i + 1) * 2 * inner] = dot(pick, part).astype(bf16)
    for i, ref in enumerate((r0_ref, r1_ref, r2_ref, r3_ref)):
        rows = slice(i * n, (i + 1) * n)
        ref[:, :d] = dot_nt(grad_ref[rows], wi_ref[...]).astype(bf16)
        ref[:, d:] = att_ref[rows]
    for ref, rows in ((keep_ref, slice(0, d // 2)), (send_ref, slice(d // 2, d))):
        ref[...] = dot(turned_ref[rows], grad_ref[...]).astype(bf16)


def output_grads(cot_ref, b0_ref, b1_ref, b2_ref, b3_ref, keep_ref, send_ref, att_ref):
    d = cot_ref.shape[0]
    n = b0_ref.shape[0]
    for i, ref in enumerate((b0_ref, b1_ref, b2_ref, b3_ref)):
        att_ref[i * n : (i + 1) * n] = ref[:, d:]
    for ref, rows in ((keep_ref, slice(0, d // 2)), (send_ref, slice(d // 2, d))):
        ref[...] = dot(cot_ref[rows], att_ref[...]).astype(bf16)


def block_result(tok_ref, b0_ref, b1_ref, b2_ref, b3_ref, wo_ref, core_ref, out_ref):
    x, _, _, d = tok_ref.shape
    for start, refs in zip(halves(core_ref, x), ((b0_ref, b1_ref), (b2_ref, b3_ref))):
        branch = [dot(ref[:, d:], wo_ref[...]).astype(bf16).astype(f32) for ref in refs]
        total = x_half(tok_ref, start) + join_z(*branch)
        out_ref[pl.ds(start, x // 2)] = total.astype(bf16).reshape(
            (x // 2,) + out_ref.shape[1:])


def coarse_total(parts_ref, core_ref, pair_ref, here_ref, there_ref):
    d = parts_ref.shape[1] // 2
    parts = parts_ref[...].astype(f32)
    even = lax.broadcasted_iota(jnp.int32, parts.shape, 0) % 2 == 0
    for i, ref in ((0, here_ref), (1, there_ref)):
        total = jnp.sum(jnp.where(even == (i == 0), parts, 0.0), axis=0, keepdims=True)
        pair_ref[pl.ds(i, 1)] = total
        ref[...] = jnp.where(core_ref[0, 0] == 0, total[:, :d], total[:, d:])


def assemble(keep_ref, other_ref, out_keep_ref, out_other_ref, pair_ref, picked_ref, out_ref, pair_rows):
    plane, rows, width = out_ref.shape
    width -= 256
    lanes = picked_ref.shape[1]
    per_row = width // 128
    for i in range(rows):
        at = i % per_row * 128
        pair_rows[i : i + 1] = pair_ref[i // per_row : i // per_row + 1, at : at + 128]
    pairs = pair_rows[...]
    picked = picked_ref[...]
    empty = jnp.zeros((rows - 8, 128), f32)
    for i in range(plane):
        part = slice(i * rows, (i + 1) * rows)
        split = keep_ref.shape[1]
        out_ref[i, :, :split] = (keep_ref[part].astype(f32) + other_ref[part].astype(f32)).astype(bf16)
        out_ref[i, :, split:width] = (out_keep_ref[part].astype(f32) + out_other_ref[part].astype(f32)).astype(bf16)
        mine = pltpu.roll(picked, (lanes - i * rows) % lanes, 1)[:, :128]
        beside = jnp.concatenate([pairs, jnp.concatenate([mine, empty], axis=0)], axis=1)
        out_ref[i, :, width:] = beside.astype(bf16)


def place_of(tile, tiles):
    return tile // tiles, tile % tiles * 128


def plane_sums(in_ref, out_ref, flat_ref):
    plane, rows, width = in_ref.shape
    width -= 256
    deep, lines, lanes = out_ref.shape
    half = width // 2
    total = jnp.sum(in_ref[:, :, :width].astype(f32), axis=0)
    pairs = in_ref[:, :, width : width + 128].astype(f32)
    picked = in_ref[:, :8, width + 128 :].astype(f32)
    line = lax.broadcasted_iota(jnp.int32, picked.shape, 1)

    def row(block, i):
        return jnp.sum(jnp.where(line == i, block, 0.0), axis=1).astype(bf16)

    coarse = jnp.zeros((128, half), f32)
    tiles = half // 128
    for i in range(4):
        grads = [row(pairs[:, q // 8 * 8 : q // 8 * 8 + 8], q % 8) for q in range(i * tiles, (i + 1) * tiles)]
        coarse += lax.dot_general(
            row(picked, 2 + i), jnp.concatenate(grads, axis=1),
            (((0,), (0,)), ((), ())), preferred_element_type=f32)
    flat_ref[...] = jnp.zeros_like(flat_ref)
    tile = 0
    for j in range(rows // deep):
        part = slice(j * deep, (j + 1) * deep)
        for block in (total[part], coarse[part]):
            for at in range(0, block.shape[1], 128):
                r, lane = place_of(tile, lanes // 128)
                flat_ref[lane // 128, pl.ds(r, deep, stride=lines), :] = block[:, at : at + 128]
                tile += 1
    for i in range(lanes // 128):
        out_ref[:, :, i * 128 : (i + 1) * 128] = flat_ref[i].reshape(deep, lines, 128).astype(bf16)


def depth_sums(in_ref, *outs):
    total = jnp.sum(in_ref[...].astype(f32), axis=0)
    tile = 0
    for j in range(outs[0].shape[0]):
        for ref in outs:
            for at in range(0, ref.shape[1], 128):
                r, lane = place_of(tile, total.shape[1] // 128)
                ref[j : j + 1, at : at + 128] = total[r : r + 1, lane : lane + 128]
                tile += 1


def token_result(tok_ref, cot_ref, b0_ref, b1_ref, b2_ref, b3_ref, here_ref, next_ref, wc_ref, core_ref, out_ref):
    x, y, z, d = tok_ref.shape
    coarse = (here_ref[...] + next_ref[...]).astype(bf16)
    pooled = dot_nt(jnp.broadcast_to(coarse, (8, d)), wc_ref[...])[0:1]
    pooled = (pooled / float(x * y * z))[None]
    for start, refs in zip(halves(core_ref, x), ((b0_ref, b1_ref), (b2_ref, b3_ref))):
        normed, inv_std = normalize(x_half(tok_ref, start))
        grad = join_z(*[ref[:, :d].astype(f32) for ref in refs]) + pooled
        first = jnp.mean(grad, axis=-1, keepdims=True)
        second = jnp.mean(grad * normed, axis=-1, keepdims=True)
        total = x_half(cot_ref, start) + inv_std * (grad - first - normed * second)
        out_ref[pl.ds(start, x // 2)] = total.astype(bf16).reshape(
            (x // 2,) + out_ref.shape[1:])


def passed(block, step, back=False):
    nx, nz = lax.axis_size(GX), lax.axis_size(GZ)
    route = []
    for a in range(nx):
        for c in range(nz):
            to_a, to_c = step(a, c)
            route.append((a * nz + c, to_a % nx * nz + to_c % nz))
    if back:
        route = [(b, a) for a, b in route]
    return lax.ppermute(block, ALL, route)


def to_up(a, c):
    return a, c - 1


def to_side(a, c):
    return (a - 1, c) if c % 2 == 0 else (a + 1, c)


def to_both(a, c):
    return (a - 1, c - 1) if c % 2 else (a + 1, c - 1)


def returned(own, up, side, both):
    return passed(up, to_up, True), passed(side, to_side, True), passed(both, to_both, True), own


def body(tokens, body_mask, cotangent, w_in, w_out, w_coarse):
    x, y, z, d = tokens.shape
    size = x * y * z
    n = size // 4
    inner = w_out.shape[0]
    coarse = lax.axis_size(GZ)
    columns = lax.axis_size(GX)
    devices = columns * coarse
    per = d // devices
    core = lax.axis_index("core")

    wide = (n, d + inner + 128)
    place = core.reshape(1, 1)
    up, side, both, own, row = call(
        prepare, [(wide, bf16)] * 4 + [((1, 2 * d), bf16)], tokens, cotangent, w_out, w_coarse, body_mask, place,
        far=range(4),
        scalars=(5,),
        grant=60,
        scratch=[pltpu.VMEM(a.shape, bf16) for a in (tokens, cotangent, w_out, w_coarse)] + [pltpu.SemaphoreType.DMA((4,))])
    before = passed(row, lambda a, c: (a + 1, c))
    up, side, both = passed(up, to_up), passed(side, to_side), passed(both, to_both)

    odd = lax.broadcasted_iota(jnp.int32, (coarse, 1), 0) % 2 == 1
    kv = jnp.where(odd, before[:, d:], row[:, d:])
    shared = jnp.concatenate([row[:, :d], before[:, :d]], axis=1)
    shared, kv = lax.optimization_barrier((shared, kv))
    other = lax.ppermute(shared, "core", [(0, 1), (1, 0)])
    kv = lax.all_to_all(kv, GZ, 0, 0, tiled=True)
    zh, nx, zl, ny, cores = (lax.axis_size(a) for a in ALL)
    plane, deep = nx * ny, zh * zl

    row = jnp.arange(d, dtype=jnp.int32)
    half, rest = row // (d // 2), row % (d // 2)
    chip, j, depth = rest // (per * deep), rest % (per * deep) // deep, rest % deep
    device = ((depth // zl * nx + chip // ny) * zl + depth % zl) * ny + chip % ny
    src = ((device * cores + (half + core) % cores) * per + j).reshape(d, 1)
    cot_turned, picked = call(
        turn_cot, [((d, size), bf16), ((8, d // 2), f32)], cotangent, src, shared, other, place, scalars=(4,))
    kv, cot_turned = lax.optimization_barrier((kv, cot_turned))

    flat, tall = (size, inner), (size + coarse, inner)
    q, k, v, g, mask, win_turned = call(
        project, [(flat, bf16)] * 4 + [((size + coarse, 128), f32), ((d, size), bf16)],
        own, up, side, both, w_in, src)
    r0, r1, r2, r3, keep, send, coarse_part = call(
        attend,
        [((n, d + inner), bf16)] * 4 + [((d // 2, 3 * inner), bf16)] * 2 + [((coarse, 4 * inner), bf16)],
        q, k, v, g, mask, w_in, kv, win_turned,
        grant=16,
        scratch=[pltpu.VMEM(s, bf16) for s in (tall, tall, flat, (size, 3 * inner))] + [pltpu.VMEM(tall, f32)] * 2)
    e0, e1, e2, e3 = returned(r0, r1, r2, r3)
    parts = lax.all_to_all(coarse_part, GZ, 0, 0, tiled=True)

    swap = [(0, 1), (1, 0)]
    other = lax.ppermute(send, "core", swap)
    cot_turned, parts, other, e0, e1, e2 = lax.optimization_barrier((cot_turned, parts, other, e0, e1, e2))
    out_keep, out_send = call(
        output_grads, [((d // 2, inner), bf16)] * 2,
        cot_turned, e0, e1, e2, e3, scratch=[pltpu.VMEM((size, inner), bf16)])
    out_other = lax.ppermute(out_send, "core", swap)
    pair, here, there = call(
        coarse_total, [((2, 4 * inner), f32), ((1, d), f32), ((1, d), f32)], parts, place, scalars=(1,))
    later = passed(there, lambda a, c: (a - 1, c))

    (packet,) = call(
        assemble, [((plane, per * deep, 4 * inner + 256), bf16)], keep, other, out_keep, out_other, pair, picked,
        scratch=[pltpu.VMEM((per * deep, 128), f32)])
    packet = lax.all_to_all(packet, ("x", "y"), 0, 0, tiled=True)
    (block_out,) = call(block_result, [(tokens.shape, bf16)], tokens, e0, e1, e2, e3, w_out, place, scalars=(6,))
    (token_grad,) = call(token_result, [(tokens.shape, bf16)], tokens, cotangent, e0, e1, e2, e3,
        here, later, w_coarse, place, scalars=(9,))
    packet, block_out, token_grad = lax.optimization_barrier((packet, block_out, token_grad))
    tiles = -(-per * 6 * inner // 1024)
    (slab,) = call(
        plane_sums, [((deep, 8, tiles * 128), bf16)], packet, scratch=[pltpu.VMEM((tiles, deep * 8, 128), f32)])
    slab = lax.all_to_all(slab, ("zh", "zl"), 0, 0, tiled=True)

    input_grad, output_grad, coarse_grad = call(
        depth_sums, [((per, 3 * inner), f32), ((per, inner), f32), ((per, 2 * inner), f32)], slab)
    output_grad = output_grad.T
    return (block_out, token_grad, input_grad, output_grad, coarse_grad)


def solution(mesh):
    fine = Mesh(mesh.devices.reshape(2, 4, 4, 4, 2), ALL)
    grid = P(GX, None, GZ, None)
    return jax.shard_map(
        body,
        mesh=fine,
        in_specs=(grid, P(GX, None, GZ), grid, P(), P(), P()),
        out_specs=(grid, grid, P(ALL, None), P(None, ALL), P(ALL, None)),
        check_vma=False,
    )
```

```python
import functools

import jax
import jax.numpy as jnp
from jax import lax
from jax.experimental import pallas as pl
from jax.experimental.pallas import tpu as pltpu
from jax.sharding import Mesh
from jax.sharding import PartitionSpec as P

HEAD = 64
PAIR = 2 * HEAD
CHUNK = 512
HIDDEN = -1e30
GX = ("zh", "x")
GZ = ("zl", "y", "core")
ALL = GX + GZ
bf16 = jnp.bfloat16
f32 = jnp.float32


def dot(left, side):
    return jnp.dot(left, side, preferred_element_type=f32)


def dot_nt(left, side):
    return lax.dot_general(left, side, (((1,), (1,)), ((), ())), preferred_element_type=f32)


def call(kernel, outs, *args, scratch=(), far=(), scalars=(), grant=16):
    return pl.pallas_call(
        kernel,
        out_shape=[jax.ShapeDtypeStruct(s, d) for s, d in outs],
        in_specs=[
            pl.BlockSpec(memory_space=pltpu.HBM if i in far else pltpu.SMEM if i in scalars else pltpu.VMEM) for i in range(len(args))
        ],
        scratch_shapes=list(scratch),
        compiler_params=pltpu.CompilerParams(vmem_limit_bytes=grant * 2**20),
        cost_estimate=pl.CostEstimate(flops=1, bytes_accessed=1, transcendentals=0),
    )(*args)


def normalize(values):
    centre = values - jnp.mean(values, axis=-1, keepdims=True)
    inv_std = lax.rsqrt(jnp.mean(centre * centre, axis=-1, keepdims=True) + 1e-05)
    return centre * inv_std, inv_std


def low_rows(shape):
    return lax.broadcasted_iota(jnp.int32, shape, 1) < shape[1] // 2


def split_z(rows):
    m, z, d = rows.shape[0] // 2, rows.shape[1], rows.shape[2]
    pairs = rows.reshape(m, 2, z, d)
    a, b = pairs[:, 0], pairs[:, 1]
    low = low_rows(a.shape)
    lower = jnp.where(low, a, pltpu.roll(b, z // 2, 1))
    upper = jnp.where(low, pltpu.roll(a, z // 2, 1), b)
    return lower.reshape(m * z, d), upper.reshape(m * z, d)


def join_z(lower, upper):
    m, d = lower.shape[0] // 8, lower.shape[1]
    lower, upper = lower.reshape(m, 8, d), upper.reshape(m, 8, d)
    low = low_rows(lower.shape)
    a = jnp.where(low, lower, pltpu.roll(upper, 4, 1))
    b = jnp.where(low, pltpu.roll(lower, 4, 1), upper)
    return jnp.stack([a, b], axis=1).reshape(2 * m, 8, d)


def halves(core_ref, x):
    far = core_ref[0, 0] * (x // 2)
    return far, x // 2 - far


def x_half(ref, start):
    x, y, z, d = ref.shape
    return ref[pl.ds(start, x // 2)].astype(f32).reshape(x // 2 * y, z, d)


def columns_of(mask):
    m, z = mask.shape
    rows = jnp.broadcast_to(mask[:, None, :], (m, z, z))
    shape = (m, z, z)
    same = lax.broadcasted_iota(jnp.int32, shape, 1) == lax.broadcasted_iota(jnp.int32, shape, 2)
    column = jnp.sum(jnp.where(same, rows, 0.0), axis=2, keepdims=True)
    return jnp.broadcast_to(column, (m, z, 128))


def prepare(*refs):
    sources, mask_ref, core_ref, refs = refs[:4], refs[4], refs[5], refs[6:]
    outs, held, sems = refs[:5], refs[5:9], refs[9]
    up_ref, side_ref, both_ref, own_ref, coarse_ref = outs
    tok_ref, cot_ref, wo_ref, wc_ref = held
    copies = [pltpu.make_async_copy(a, b, sems.at[i]) for i, (a, b) in enumerate(zip(sources, held))]
    for copy in copies:
        copy.start()
    copies[0].wait()
    inner, d = wo_ref.shape
    total = jnp.zeros((1, d), f32)
    cells = 1
    for n in tok_ref.shape[:3]:
        cells *= n
    away, home = halves(core_ref, tok_ref.shape[0])
    places = ((away, (up_ref, side_ref)), (home, (both_ref, own_ref)))
    for start, refs in places:
        normed, _ = normalize(x_half(tok_ref, start))
        total += jnp.sum(jnp.sum(normed, axis=0), axis=0, keepdims=True)
        for ref, part in zip(refs, split_z(normed)):
            ref[:, :d] = part.astype(bf16)
        x, y, z = mask_ref.shape
        cells_in = mask_ref[pl.ds(start, x // 2)].astype(f32)
        for ref, part in zip(refs, split_z(columns_of(cells_in.reshape(x // 2 * y, z)))):
            ref[:, d + inner :] = part.astype(bf16)
    copies[1].wait()
    copies[2].wait()
    for start, refs in places:
        for ref, part in zip(refs, split_z(x_half(cot_ref, start))):
            ref[:, d : d + inner] = dot_nt(part.astype(bf16), wo_ref[...]).astype(bf16)
    copies[3].wait()
    pooled = (total / cells).astype(bf16)
    coarse_ref[:, :d] = pooled
    coarse_ref[:, d:] = dot(jnp.broadcast_to(pooled, (8, d)), wc_ref[...])[:1].astype(bf16)


def turn_cot(cot_ref, src_ref, here_ref, other_ref, core_ref, out_ref, picked_ref):
    d = cot_ref.shape[3]
    parts = []
    for start in halves(core_ref, cot_ref.shape[0]):
        parts += [p.astype(bf16) for p in split_z(x_half(cot_ref, start))]
    perm = picks(src_ref, d)
    n = parts[0].shape[0]
    for i, part in enumerate(parts):
        out_ref[:, i * n : (i + 1) * n] = dot_nt(perm, part).astype(bf16)
    first = core_ref[0, 0] == 0
    pair = (here_ref[...].astype(f32), other_ref[...].astype(f32))
    pair = (jnp.where(first, pair[0], pair[1]), jnp.where(first, pair[1], pair[0]))
    line = lax.broadcasted_iota(jnp.int32, (8, d), 0)
    rows = jnp.zeros((8, d), f32)
    for i in range(4):
        rows = jnp.where(line == 2 + i, pair[i % 2][:, i // 2 * d : (i // 2 + 1) * d], rows)
    picked_ref[...] = dot_nt(rows.astype(bf16), perm[: d // 2])


def picks(src_ref, d):
    columns = lax.broadcasted_iota(jnp.int32, (d, d), 1)
    return jnp.where(columns == src_ref[...], 1.0, 0.0).astype(bf16)


def head_of(pair, half):
    lanes = lax.broadcasted_iota(jnp.int32, pair.shape, 1)
    return jnp.where((lanes < HEAD) == (half == 0), pair, jnp.zeros_like(pair))


def hide(mask_ref, refs, start):
    n = refs[0].shape[0]
    for i, ref in enumerate(refs):
        seen = ref[:, start:].astype(f32)
        mask_ref[i * n : (i + 1) * n] = jnp.where(seen > 0.5, 0.0, HIDDEN)
    mask_ref[4 * n :] = jnp.zeros((mask_ref.shape[0] - 4 * n, mask_ref.shape[1]), f32)


def project(own_ref, up_ref, side_ref, both_ref, wi_ref, src_ref, q_ref, k_ref, v_ref, g_ref, mask_ref, turned_ref):
    d, width = wi_ref.shape
    inner = width // 3
    n = own_ref.shape[0]
    blocks = (own_ref, up_ref, side_ref, both_ref)
    perm = picks(src_ref, d)
    for i, ref in enumerate(blocks):
        packed = dot(ref[:, :d], wi_ref[...])
        rows = slice(i * n, (i + 1) * n)
        q_ref[rows] = packed[:, :inner].astype(bf16) * bf16(0.125)
        k_ref[rows] = packed[:, inner : 2 * inner].astype(bf16)
        v_ref[rows] = packed[:, 2 * inner :].astype(bf16)
        g_ref[rows] = ref[:, d : d + inner]
        turned_ref[:, rows] = dot_nt(perm, ref[:, :d]).astype(bf16)
    hide(mask_ref, blocks, d + inner)


def attend(q_ref, kw_ref, vw_ref, g_ref, mask_ref, wi_ref, kv_ref, turned_ref,
           r0_ref, r1_ref, r2_ref, r3_ref, keep_ref, send_ref, coarse_ref,
           k_ref, v_ref, att_ref, grad_ref, dk_ref, dv_ref):
    d, width = wi_ref.shape
    inner = width // 3
    tokens = q_ref.shape[0]
    n = tokens // 4
    k_ref[:tokens] = kw_ref[...]
    v_ref[:tokens] = vw_ref[...]
    k_ref[tokens:] = kv_ref[:, :inner]
    v_ref[tokens:] = kv_ref[:, inner:]
    eye = jnp.where(
        lax.broadcasted_iota(jnp.int32, (PAIR, PAIR), 0)
        == lax.broadcasted_iota(jnp.int32, (PAIR, PAIR), 1), 1.0, 0.0).astype(bf16)
    chunks = tokens // CHUNK
    dk_ref[...] = jnp.zeros_like(dk_ref)
    dv_ref[...] = jnp.zeros_like(dv_ref)

    def step(i, _):
        lanes = pl.ds(pl.multiple_of(i // chunks * PAIR, PAIR), PAIR)
        rows = pl.ds(pl.multiple_of(i % chunks * CHUNK, CHUNK), CHUNK)
        keys = k_ref[:, lanes]
        vals = v_ref[:, lanes]
        keys_t = dot_nt(eye, keys).astype(bf16)
        vals_t = dot_nt(eye, vals).astype(bf16)
        queries = [head_of(q_ref[rows, lanes], half) for half in range(2)]
        gs = [head_of(g_ref[rows, lanes], half) for half in range(2)]
        found = []
        grads = []
        dv = dv_ref[:, lanes]
        dk = dk_ref[:, lanes]
        for half in range(2):
            part = slice(half * HEAD, (half + 1) * HEAD)
            s = dot_nt(keys, queries[half]) + jnp.concatenate([mask_ref[...]] * (CHUNK // 128), axis=1)
            e = jnp.exp(s - jnp.max(s, axis=0, keepdims=True))
            prob = e * (1.0 / jnp.sum(e, axis=0, keepdims=True))
            weight = prob.astype(bf16)
            found.append(dot(vals_t[part], weight))
            dv += dot(weight, gs[half])
            spread = prob * dot_nt(vals, gs[half])
            centre = jnp.sum(spread, axis=0, keepdims=True)
            score = (spread - prob * centre).astype(bf16)
            dk += dot(score, queries[half])
            grads.append(dot(keys_t[part], score))
        dv_ref[:, lanes] = dv
        dk_ref[:, lanes] = dk
        att_ref[rows, lanes] = jnp.concatenate(found, axis=0).T.astype(bf16)
        grad_ref[rows, lanes] = (jnp.concatenate(grads, axis=0).T * 0.125).astype(bf16)
        return 0

    lax.fori_loop(0, inner // PAIR * chunks, step, 0, unroll=True)
    grad_ref[:, inner : 2 * inner] = dk_ref[:tokens].astype(bf16)
    grad_ref[:, 2 * inner :] = dv_ref[:tokens].astype(bf16)
    peers = coarse_ref.shape[0]
    part = jnp.concatenate([dk_ref[tokens:].astype(bf16), dv_ref[tokens:].astype(bf16)], axis=1)
    chip = lax.broadcasted_iota(jnp.int32, (peers, peers), 0) // 2 * 2
    token = lax.broadcasted_iota(jnp.int32, (peers, peers), 1)
    for i in range(2):
        pick = jnp.where(token == chip + i, 1.0, 0.0).astype(bf16)
        coarse_ref[:, i * 2 * inner : (i + 1) * 2 * inner] = dot(pick, part).astype(bf16)
    for i, ref in enumerate((r0_ref, r1_ref, r2_ref, r3_ref)):
        rows = slice(i * n, (i + 1) * n)
        ref[:, :d] = dot_nt(grad_ref[rows], wi_ref[...]).astype(bf16)
        ref[:, d:] = att_ref[rows]
    for ref, rows in ((keep_ref, slice(0, d // 2)), (send_ref, slice(d // 2, d))):
        ref[...] = dot(turned_ref[rows], grad_ref[...]).astype(bf16)


def output_grads(cot_ref, b0_ref, b1_ref, b2_ref, b3_ref, keep_ref, send_ref, att_ref):
    d = cot_ref.shape[0]
    n = b0_ref.shape[0]
    for i, ref in enumerate((b0_ref, b1_ref, b2_ref, b3_ref)):
        att_ref[i * n : (i + 1) * n] = ref[:, d:]
    for ref, rows in ((keep_ref, slice(0, d // 2)), (send_ref, slice(d // 2, d))):
        ref[...] = dot(cot_ref[rows], att_ref[...]).astype(bf16)


def block_result(tok_ref, b0_ref, b1_ref, b2_ref, b3_ref, wo_ref, core_ref, out_ref):
    x, _, _, d = tok_ref.shape
    for start, refs in zip(halves(core_ref, x), ((b0_ref, b1_ref), (b2_ref, b3_ref))):
        branch = [dot(ref[:, d:], wo_ref[...]).astype(bf16).astype(f32) for ref in refs]
        total = x_half(tok_ref, start) + join_z(*branch)
        out_ref[pl.ds(start, x // 2)] = total.astype(bf16).reshape(
            (x // 2,) + out_ref.shape[1:])


def coarse_total(parts_ref, core_ref, pair_ref, here_ref, there_ref):
    d = parts_ref.shape[1] // 2
    parts = parts_ref[...].astype(f32)
    even = lax.broadcasted_iota(jnp.int32, parts.shape, 0) % 2 == 0
    for i, ref in ((0, here_ref), (1, there_ref)):
        total = jnp.sum(jnp.where(even == (i == 0), parts, 0.0), axis=0, keepdims=True)
        pair_ref[pl.ds(i, 1)] = total
        ref[...] = jnp.where(core_ref[0, 0] == 0, total[:, :d], total[:, d:])


def assemble(keep_ref, other_ref, out_keep_ref, out_other_ref, pair_ref, picked_ref, out_ref, pair_rows):
    plane, rows, width = out_ref.shape
    width -= 256
    lanes = picked_ref.shape[1]
    per_row = width // 128
    for i in range(rows):
        at = i % per_row * 128
        pair_rows[i : i + 1] = pair_ref[i // per_row : i // per_row + 1, at : at + 128]
    pairs = pair_rows[...]
    picked = picked_ref[...]
    empty = jnp.zeros((rows - 8, 128), f32)
    for i in range(plane):
        part = slice(i * rows, (i + 1) * rows)
        split = keep_ref.shape[1]
        out_ref[i, :, :split] = (keep_ref[part].astype(f32) + other_ref[part].astype(f32)).astype(bf16)
        out_ref[i, :, split:width] = (out_keep_ref[part].astype(f32) + out_other_ref[part].astype(f32)).astype(bf16)
        mine = pltpu.roll(picked, (lanes - i * rows) % lanes, 1)[:, :128]
        beside = jnp.concatenate([pairs, jnp.concatenate([mine, empty], axis=0)], axis=1)
        out_ref[i, :, width:] = beside.astype(bf16)


def place_of(tile, tiles):
    return tile // tiles, tile % tiles * 128


def plane_sums(in_ref, out_ref, flat_ref):
    plane, rows, width = in_ref.shape
    width -= 256
    deep, lines, lanes = out_ref.shape
    half = width // 2
    total = jnp.sum(in_ref[:, :, :width].astype(f32), axis=0)
    pairs = in_ref[:, :, width : width + 128].astype(f32)
    picked = in_ref[:, :8, width + 128 :].astype(f32)
    line = lax.broadcasted_iota(jnp.int32, picked.shape, 1)

    def row(block, i):
        return jnp.sum(jnp.where(line == i, block, 0.0), axis=1).astype(bf16)

    coarse = jnp.zeros((128, half), f32)
    tiles = half // 128
    for i in range(4):
        grads = [row(pairs[:, q // 8 * 8 : q // 8 * 8 + 8], q % 8) for q in range(i * tiles, (i + 1) * tiles)]
        coarse += lax.dot_general(
            row(picked, 2 + i), jnp.concatenate(grads, axis=1),
            (((0,), (0,)), ((), ())), preferred_element_type=f32)
    flat_ref[...] = jnp.zeros_like(flat_ref)
    tile = 0
    for j in range(rows // deep):
        part = slice(j * deep, (j + 1) * deep)
        for block in (total[part], coarse[part]):
            for at in range(0, block.shape[1], 128):
                r, lane = place_of(tile, lanes // 128)
                flat_ref[lane // 128, pl.ds(r, deep, stride=lines), :] = block[:, at : at + 128]
                tile += 1
    for i in range(lanes // 128):
        out_ref[:, :, i * 128 : (i + 1) * 128] = flat_ref[i].reshape(deep, lines, 128).astype(bf16)


def depth_sums(in_ref, *outs):
    total = jnp.sum(in_ref[...].astype(f32), axis=0)
    tile = 0
    for j in range(outs[0].shape[0]):
        for ref in outs:
            for at in range(0, ref.shape[1], 128):
                r, lane = place_of(tile, total.shape[1] // 128)
                ref[j : j + 1, at : at + 128] = total[r : r + 1, lane : lane + 128]
                tile += 1


def token_result(tok_ref, cot_ref, b0_ref, b1_ref, b2_ref, b3_ref, here_ref, next_ref, wc_ref, core_ref, out_ref):
    x, y, z, d = tok_ref.shape
    coarse = (here_ref[...] + next_ref[...]).astype(bf16)
    pooled = dot_nt(jnp.broadcast_to(coarse, (8, d)), wc_ref[...])[0:1]
    pooled = (pooled / float(x * y * z))[None]
    for start, refs in zip(halves(core_ref, x), ((b0_ref, b1_ref), (b2_ref, b3_ref))):
        normed, inv_std = normalize(x_half(tok_ref, start))
        grad = join_z(*[ref[:, :d].astype(f32) for ref in refs]) + pooled
        first = jnp.mean(grad, axis=-1, keepdims=True)
        second = jnp.mean(grad * normed, axis=-1, keepdims=True)
        total = x_half(cot_ref, start) + inv_std * (grad - first - normed * second)
        out_ref[pl.ds(start, x // 2)] = total.astype(bf16).reshape(
            (x // 2,) + out_ref.shape[1:])


def passed(block, step, back=False):
    nx, nz = lax.axis_size(GX), lax.axis_size(GZ)
    route = []
    for a in range(nx):
        for c in range(nz):
            to_a, to_c = step(a, c)
            route.append((a * nz + c, to_a % nx * nz + to_c % nz))
    if back:
        route = [(b, a) for a, b in route]
    return lax.ppermute(block, ALL, route)


def to_up(a, c):
    return a, c - 1


def to_side(a, c):
    return (a - 1, c) if c % 2 == 0 else (a + 1, c)


def to_both(a, c):
    return (a - 1, c - 1) if c % 2 else (a + 1, c - 1)


def returned(own, up, side, both):
    return passed(up, to_up, True), passed(side, to_side, True), passed(both, to_both, True), own


def body(tokens, body_mask, cotangent, w_in, w_out, w_coarse):
    x, y, z, d = tokens.shape
    size = x * y * z
    n = size // 4
    inner = w_out.shape[0]
    coarse = lax.axis_size(GZ)
    columns = lax.axis_size(GX)
    devices = columns * coarse
    per = d // devices
    core = lax.axis_index("core")

    wide = (n, d + inner + 128)
    place = core.reshape(1, 1)
    up, side, both, own, row = call(
        prepare, [(wide, bf16)] * 4 + [((1, 2 * d), bf16)], tokens, cotangent, w_out, w_coarse, body_mask, place,
        far=range(4),
        scalars=(5,),
        grant=60,
        scratch=[pltpu.VMEM(a.shape, bf16) for a in (tokens, cotangent, w_out, w_coarse)] + [pltpu.SemaphoreType.DMA((4,))])
    before = passed(row, lambda a, c: (a + 1, c))
    up, side, both = passed(up, to_up), passed(side, to_side), passed(both, to_both)

    odd = lax.broadcasted_iota(jnp.int32, (coarse, 1), 0) % 2 == 1
    kv = jnp.where(odd, before[:, d:], row[:, d:])
    shared = jnp.concatenate([row[:, :d], before[:, :d]], axis=1)
    shared, kv = lax.optimization_barrier((shared, kv))
    other = lax.ppermute(shared, "core", [(0, 1), (1, 0)])
    kv = lax.all_to_all(kv, GZ, 0, 0, tiled=True)
    zh, nx, zl, ny, cores = (lax.axis_size(a) for a in ALL)
    plane, deep = nx * ny, zh * zl

    row = jnp.arange(d, dtype=jnp.int32)
    half, rest = row // (d // 2), row % (d // 2)
    chip, j, depth = rest // (per * deep), rest % (per * deep) // deep, rest % deep
    device = ((depth // zl * nx + chip // ny) * zl + depth % zl) * ny + chip % ny
    src = ((device * cores + (half + core) % cores) * per + j).reshape(d, 1)
    cot_turned, picked = call(
        turn_cot, [((d, size), bf16), ((8, d // 2), f32)], cotangent, src, shared, other, place, scalars=(4,))
    kv, cot_turned = lax.optimization_barrier((kv, cot_turned))

    flat, tall = (size, inner), (size + coarse, inner)
    q, k, v, g, mask, win_turned = call(
        project, [(flat, bf16)] * 4 + [((size + coarse, 128), f32), ((d, size), bf16)],
        own, up, side, both, w_in, src)
    r0, r1, r2, r3, keep, send, coarse_part = call(
        attend,
        [((n, d + inner), bf16)] * 4 + [((d // 2, 3 * inner), bf16)] * 2 + [((coarse, 4 * inner), bf16)],
        q, k, v, g, mask, w_in, kv, win_turned,
        grant=16,
        scratch=[pltpu.VMEM(s, bf16) for s in (tall, tall, flat, (size, 3 * inner))] + [pltpu.VMEM(tall, f32)] * 2)
    e0, e1, e2, e3 = returned(r0, r1, r2, r3)
    parts = lax.all_to_all(coarse_part, GZ, 0, 0, tiled=True)

    swap = [(0, 1), (1, 0)]
    other = lax.ppermute(send, "core", swap)
    cot_turned, parts, other, e0, e1, e2 = lax.optimization_barrier((cot_turned, parts, other, e0, e1, e2))
    out_keep, out_send = call(
        output_grads, [((d // 2, inner), bf16)] * 2,
        cot_turned, e0, e1, e2, e3, scratch=[pltpu.VMEM((size, inner), bf16)])
    out_other = lax.ppermute(out_send, "core", swap)
    pair, here, there = call(
        coarse_total, [((2, 4 * inner), f32), ((1, d), f32), ((1, d), f32)], parts, place, scalars=(1,))
    later = passed(there, lambda a, c: (a - 1, c))

    (packet,) = call(
        assemble, [((plane, per * deep, 4 * inner + 256), bf16)], keep, other, out_keep, out_other, pair, picked,
        scratch=[pltpu.VMEM((per * deep, 128), f32)])
    packet = lax.all_to_all(packet, ("x", "y"), 0, 0, tiled=True)
    (block_out,) = call(block_result, [(tokens.shape, bf16)], tokens, e0, e1, e2, e3, w_out, place, scalars=(6,))
    (token_grad,) = call(token_result, [(tokens.shape, bf16)], tokens, cotangent, e0, e1, e2, e3,
        here, later, w_coarse, place, scalars=(9,))
    packet, block_out, token_grad = lax.optimization_barrier((packet, block_out, token_grad))
    tiles = -(-per * 6 * inner // 1024)
    (slab,) = call(
        plane_sums, [((deep, 8, tiles * 128), bf16)], packet, scratch=[pltpu.VMEM((tiles, deep * 8, 128), f32)])
    slab = lax.all_to_all(slab, ("zh", "zl"), 0, 0, tiled=True)

    input_grad, output_grad, coarse_grad = call(
        depth_sums, [((per, 3 * inner), f32), ((per, inner), f32), ((per, 2 * inner), f32)], slab)
    output_grad = output_grad.T
    return (block_out, token_grad, input_grad, output_grad, coarse_grad)


def solution(mesh):
    fine = Mesh(mesh.devices.reshape(2, 4, 4, 4, 2), ALL)
    grid = P(GX, None, GZ, None)
    return jax.shard_map(
        body,
        mesh=fine,
        in_specs=(grid, P(GX, None, GZ), grid, P(), P(), P()),
        out_specs=(grid, grid, P(ALL, None), P(None, ALL), P(ALL, None)),
        check_vma=False,
    )
```

```python
import functools

import jax
import jax.numpy as jnp
from jax import lax
from jax.experimental import pallas as pl
from jax.experimental.pallas import tpu as pltpu
from jax.sharding import Mesh
from jax.sharding import PartitionSpec as P

HEAD = 64
PAIR = 2 * HEAD
CHUNK = 512
HIDDEN = -1e30
GX = ("zh", "x")
GZ = ("zl", "y", "core")
ALL = GX + GZ
bf16 = jnp.bfloat16
f32 = jnp.float32


def dot(left, side):
    return jnp.dot(left, side, preferred_element_type=f32)


def dot_nt(left, side):
    return lax.dot_general(left, side, (((1,), (1,)), ((), ())), preferred_element_type=f32)


def call(kernel, outs, *args, scratch=(), far=(), scalars=(), grant=16):
    return pl.pallas_call(
        kernel,
        out_shape=[jax.ShapeDtypeStruct(s, d) for s, d in outs],
        in_specs=[
            pl.BlockSpec(memory_space=pltpu.HBM if i in far else pltpu.SMEM if i in scalars else pltpu.VMEM) for i in range(len(args))
        ],
        scratch_shapes=list(scratch),
        compiler_params=pltpu.CompilerParams(vmem_limit_bytes=grant * 2**20),
        cost_estimate=pl.CostEstimate(flops=1, bytes_accessed=1, transcendentals=0),
    )(*args)


def normalize(values):
    centre = values - jnp.mean(values, axis=-1, keepdims=True)
    inv_std = lax.rsqrt(jnp.mean(centre * centre, axis=-1, keepdims=True) + 1e-05)
    return centre * inv_std, inv_std


def low_rows(shape):
    return lax.broadcasted_iota(jnp.int32, shape, 1) < shape[1] // 2


def split_z(rows):
    m, z, d = rows.shape[0] // 2, rows.shape[1], rows.shape[2]
    pairs = rows.reshape(m, 2, z, d)
    a, b = pairs[:, 0], pairs[:, 1]
    low = low_rows(a.shape)
    lower = jnp.where(low, a, pltpu.roll(b, z // 2, 1))
    upper = jnp.where(low, pltpu.roll(a, z // 2, 1), b)
    return lower.reshape(m * z, d), upper.reshape(m * z, d)


def join_z(lower, upper):
    m, d = lower.shape[0] // 8, lower.shape[1]
    lower, upper = lower.reshape(m, 8, d), upper.reshape(m, 8, d)
    low = low_rows(lower.shape)
    a = jnp.where(low, lower, pltpu.roll(upper, 4, 1))
    b = jnp.where(low, pltpu.roll(lower, 4, 1), upper)
    return jnp.stack([a, b], axis=1).reshape(2 * m, 8, d)


def halves(core_ref, x):
    far = core_ref[0, 0] * (x // 2)
    return far, x // 2 - far


def x_half(ref, start):
    x, y, z, d = ref.shape
    return ref[pl.ds(start, x // 2)].astype(f32).reshape(x // 2 * y, z, d)


def columns_of(mask):
    m, z = mask.shape
    rows = jnp.broadcast_to(mask[:, None, :], (m, z, z))
    shape = (m, z, z)
    same = lax.broadcasted_iota(jnp.int32, shape, 1) == lax.broadcasted_iota(jnp.int32, shape, 2)
    column = jnp.sum(jnp.where(same, rows, 0.0), axis=2, keepdims=True)
    return jnp.broadcast_to(column, (m, z, 128))


def prepare(*refs):
    sources, mask_ref, core_ref, refs = refs[:4], refs[4], refs[5], refs[6:]
    outs, held, sems = refs[:5], refs[5:9], refs[9]
    up_ref, side_ref, both_ref, own_ref, coarse_ref = outs
    tok_ref, cot_ref, wo_ref, wc_ref = held
    copies = [pltpu.make_async_copy(a, b, sems.at[i]) for i, (a, b) in enumerate(zip(sources, held))]
    for copy in copies:
        copy.start()
    copies[0].wait()
    inner, d = wo_ref.shape
    total = jnp.zeros((1, d), f32)
    cells = 1
    for n in tok_ref.shape[:3]:
        cells *= n
    away, home = halves(core_ref, tok_ref.shape[0])
    places = ((away, (up_ref, side_ref)), (home, (both_ref, own_ref)))
    for start, refs in places:
        normed, _ = normalize(x_half(tok_ref, start))
        total += jnp.sum(jnp.sum(normed, axis=0), axis=0, keepdims=True)
        for ref, part in zip(refs, split_z(normed)):
            ref[:, :d] = part.astype(bf16)
        x, y, z = mask_ref.shape
        cells_in = mask_ref[pl.ds(start, x // 2)].astype(f32)
        for ref, part in zip(refs, split_z(columns_of(cells_in.reshape(x // 2 * y, z)))):
            ref[:, d + inner :] = part.astype(bf16)
    copies[1].wait()
    copies[2].wait()
    for start, refs in places:
        for ref, part in zip(refs, split_z(x_half(cot_ref, start))):
            ref[:, d : d + inner] = dot_nt(part.astype(bf16), wo_ref[...]).astype(bf16)
    copies[3].wait()
    pooled = (total / cells).astype(bf16)
    coarse_ref[:, :d] = pooled
    coarse_ref[:, d:] = dot(jnp.broadcast_to(pooled, (8, d)), wc_ref[...])[:1].astype(bf16)


def turn_cot(cot_ref, src_ref, here_ref, other_ref, core_ref, out_ref, picked_ref):
    d = cot_ref.shape[3]
    parts = []
    for start in halves(core_ref, cot_ref.shape[0]):
        parts += [p.astype(bf16) for p in split_z(x_half(cot_ref, start))]
    perm = picks(src_ref, d)
    n = parts[0].shape[0]
    for i, part in enumerate(parts):
        out_ref[:, i * n : (i + 1) * n] = dot_nt(perm, part).astype(bf16)
    first = core_ref[0, 0] == 0
    pair = (here_ref[...].astype(f32), other_ref[...].astype(f32))
    pair = (jnp.where(first, pair[0], pair[1]), jnp.where(first, pair[1], pair[0]))
    line = lax.broadcasted_iota(jnp.int32, (8, d), 0)
    rows = jnp.zeros((8, d), f32)
    for i in range(4):
        rows = jnp.where(line == 2 + i, pair[i % 2][:, i // 2 * d : (i // 2 + 1) * d], rows)
    picked_ref[...] = dot_nt(rows.astype(bf16), perm[: d // 2])


def picks(src_ref, d):
    columns = lax.broadcasted_iota(jnp.int32, (d, d), 1)
    return jnp.where(columns == src_ref[...], 1.0, 0.0).astype(bf16)


def head_of(pair, half):
    lanes = lax.broadcasted_iota(jnp.int32, pair.shape, 1)
    return jnp.where((lanes < HEAD) == (half == 0), pair, jnp.zeros_like(pair))


def hide(mask_ref, refs, start):
    n = refs[0].shape[0]
    for i, ref in enumerate(refs):
        seen = ref[:, start:].astype(f32)
        mask_ref[i * n : (i + 1) * n] = jnp.where(seen > 0.5, 0.0, HIDDEN)
    mask_ref[4 * n :] = jnp.zeros((mask_ref.shape[0] - 4 * n, mask_ref.shape[1]), f32)


def project(own_ref, up_ref, side_ref, both_ref, wi_ref, src_ref, q_ref, k_ref, v_ref, g_ref, mask_ref, turned_ref):
    d, width = wi_ref.shape
    inner = width // 3
    n = own_ref.shape[0]
    blocks = (own_ref, up_ref, side_ref, both_ref)
    perm = picks(src_ref, d)
    for i, ref in enumerate(blocks):
        packed = dot(ref[:, :d], wi_ref[...])
        rows = slice(i * n, (i + 1) * n)
        q_ref[rows] = packed[:, :inner].astype(bf16) * bf16(0.125)
        k_ref[rows] = packed[:, inner : 2 * inner].astype(bf16)
        v_ref[rows] = packed[:, 2 * inner :].astype(bf16)
        g_ref[rows] = ref[:, d : d + inner]
        turned_ref[:, rows] = dot_nt(perm, ref[:, :d]).astype(bf16)
    hide(mask_ref, blocks, d + inner)


def attend(q_ref, kw_ref, vw_ref, g_ref, mask_ref, wi_ref, kv_ref, turned_ref,
           r0_ref, r1_ref, r2_ref, r3_ref, keep_ref, send_ref, coarse_ref,
           k_ref, v_ref, att_ref, grad_ref, dk_ref, dv_ref):
    d, width = wi_ref.shape
    inner = width // 3
    tokens = q_ref.shape[0]
    n = tokens // 4
    k_ref[:tokens] = kw_ref[...]
    v_ref[:tokens] = vw_ref[...]
    k_ref[tokens:] = kv_ref[:, :inner]
    v_ref[tokens:] = kv_ref[:, inner:]
    eye = jnp.where(
        lax.broadcasted_iota(jnp.int32, (PAIR, PAIR), 0)
        == lax.broadcasted_iota(jnp.int32, (PAIR, PAIR), 1), 1.0, 0.0).astype(bf16)
    chunks = tokens // CHUNK
    dk_ref[...] = jnp.zeros_like(dk_ref)
    dv_ref[...] = jnp.zeros_like(dv_ref)

    def step(i, _):
        lanes = pl.ds(pl.multiple_of(i // chunks * PAIR, PAIR), PAIR)
        rows = pl.ds(pl.multiple_of(i % chunks * CHUNK, CHUNK), CHUNK)
        keys = k_ref[:, lanes]
        vals = v_ref[:, lanes]
        keys_t = dot_nt(eye, keys).astype(bf16)
        vals_t = dot_nt(eye, vals).astype(bf16)
        queries = [head_of(q_ref[rows, lanes], half) for half in range(2)]
        gs = [head_of(g_ref[rows, lanes], half) for half in range(2)]
        found = []
        grads = []
        dv = dv_ref[:, lanes]
        dk = dk_ref[:, lanes]
        for half in range(2):
            part = slice(half * HEAD, (half + 1) * HEAD)
            s = dot_nt(keys, queries[half]) + jnp.concatenate([mask_ref[...]] * (CHUNK // 128), axis=1)
            e = jnp.exp(s - jnp.max(s, axis=0, keepdims=True))
            prob = e * (1.0 / jnp.sum(e, axis=0, keepdims=True))
            weight = prob.astype(bf16)
            found.append(dot(vals_t[part], weight))
            dv += dot(weight, gs[half])
            spread = prob * dot_nt(vals, gs[half])
            centre = jnp.sum(spread, axis=0, keepdims=True)
            score = (spread - prob * centre).astype(bf16)
            dk += dot(score, queries[half])
            grads.append(dot(keys_t[part], score))
        dv_ref[:, lanes] = dv
        dk_ref[:, lanes] = dk
        att_ref[rows, lanes] = jnp.concatenate(found, axis=0).T.astype(bf16)
        grad_ref[rows, lanes] = (jnp.concatenate(grads, axis=0).T * 0.125).astype(bf16)
        return 0

    lax.fori_loop(0, inner // PAIR * chunks, step, 0, unroll=True)
    grad_ref[:, inner : 2 * inner] = dk_ref[:tokens].astype(bf16)
    grad_ref[:, 2 * inner :] = dv_ref[:tokens].astype(bf16)
    peers = coarse_ref.shape[0]
    part = jnp.concatenate([dk_ref[tokens:].astype(bf16), dv_ref[tokens:].astype(bf16)], axis=1)
    chip = lax.broadcasted_iota(jnp.int32, (peers, peers), 0) // 2 * 2
    token = lax.broadcasted_iota(jnp.int32, (peers, peers), 1)
    for i in range(2):
        pick = jnp.where(token == chip + i, 1.0, 0.0).astype(bf16)
        coarse_ref[:, i * 2 * inner : (i + 1) * 2 * inner] = dot(pick, part).astype(bf16)
    for i, ref in enumerate((r0_ref, r1_ref, r2_ref, r3_ref)):
        rows = slice(i * n, (i + 1) * n)
        ref[:, :d] = dot_nt(grad_ref[rows], wi_ref[...]).astype(bf16)
        ref[:, d:] = att_ref[rows]
    for ref, rows in ((keep_ref, slice(0, d // 2)), (send_ref, slice(d // 2, d))):
        ref[...] = dot(turned_ref[rows], grad_ref[...]).astype(bf16)


def output_grads(cot_ref, b0_ref, b1_ref, b2_ref, b3_ref, keep_ref, send_ref, att_ref):
    d = cot_ref.shape[0]
    n = b0_ref.shape[0]
    for i, ref in enumerate((b0_ref, b1_ref, b2_ref, b3_ref)):
        att_ref[i * n : (i + 1) * n] = ref[:, d:]
    for ref, rows in ((keep_ref, slice(0, d // 2)), (send_ref, slice(d // 2, d))):
        ref[...] = dot(cot_ref[rows], att_ref[...]).astype(bf16)


def block_result(tok_ref, b0_ref, b1_ref, b2_ref, b3_ref, wo_ref, core_ref, out_ref):
    x, _, _, d = tok_ref.shape
    for start, refs in zip(halves(core_ref, x), ((b0_ref, b1_ref), (b2_ref, b3_ref))):
        branch = [dot(ref[:, d:], wo_ref[...]).astype(bf16).astype(f32) for ref in refs]
        total = x_half(tok_ref, start) + join_z(*branch)
        out_ref[pl.ds(start, x // 2)] = total.astype(bf16).reshape(
            (x // 2,) + out_ref.shape[1:])


def coarse_total(parts_ref, core_ref, pair_ref, here_ref, there_ref):
    d = parts_ref.shape[1] // 2
    parts = parts_ref[...].astype(f32)
    even = lax.broadcasted_iota(jnp.int32, parts.shape, 0) % 2 == 0
    for i, ref in ((0, here_ref), (1, there_ref)):
        total = jnp.sum(jnp.where(even == (i == 0), parts, 0.0), axis=0, keepdims=True)
        pair_ref[pl.ds(i, 1)] = total
        ref[...] = jnp.where(core_ref[0, 0] == 0, total[:, :d], total[:, d:])


def assemble(keep_ref, other_ref, out_keep_ref, out_other_ref, pair_ref, picked_ref, out_ref, pair_rows):
    plane, rows, width = out_ref.shape
    width -= 256
    lanes = picked_ref.shape[1]
    per_row = width // 128
    for i in range(rows):
        at = i % per_row * 128
        pair_rows[i : i + 1] = pair_ref[i // per_row : i // per_row + 1, at : at + 128]
    pairs = pair_rows[...]
    picked = picked_ref[...]
    empty = jnp.zeros((rows - 8, 128), f32)
    for i in range(plane):
        part = slice(i * rows, (i + 1) * rows)
        split = keep_ref.shape[1]
        out_ref[i, :, :split] = (keep_ref[part].astype(f32) + other_ref[part].astype(f32)).astype(bf16)
        out_ref[i, :, split:width] = (out_keep_ref[part].astype(f32) + out_other_ref[part].astype(f32)).astype(bf16)
        mine = pltpu.roll(picked, (lanes - i * rows) % lanes, 1)[:, :128]
        beside = jnp.concatenate([pairs, jnp.concatenate([mine, empty], axis=0)], axis=1)
        out_ref[i, :, width:] = beside.astype(bf16)


def place_of(tile, tiles):
    return tile // tiles, tile % tiles * 128


def plane_sums(in_ref, out_ref, flat_ref):
    plane, rows, width = in_ref.shape
    width -= 256
    deep, lines, lanes = out_ref.shape
    half = width // 2
    total = jnp.sum(in_ref[:, :, :width].astype(f32), axis=0)
    pairs = in_ref[:, :, width : width + 128].astype(f32)
    picked = in_ref[:, :8, width + 128 :].astype(f32)
    line = lax.broadcasted_iota(jnp.int32, picked.shape, 1)

    def row(block, i):
        return jnp.sum(jnp.where(line == i, block, 0.0), axis=1).astype(bf16)

    coarse = jnp.zeros((128, half), f32)
    tiles = half // 128
    for i in range(4):
        grads = [row(pairs[:, q // 8 * 8 : q // 8 * 8 + 8], q % 8) for q in range(i * tiles, (i + 1) * tiles)]
        coarse += lax.dot_general(
            row(picked, 2 + i), jnp.concatenate(grads, axis=1),
            (((0,), (0,)), ((), ())), preferred_element_type=f32)
    flat_ref[...] = jnp.zeros_like(flat_ref)
    tile = 0
    for j in range(rows // deep):
        part = slice(j * deep, (j + 1) * deep)
        for block in (total[part], coarse[part]):
            for at in range(0, block.shape[1], 128):
                r, lane = place_of(tile, lanes // 128)
                flat_ref[lane // 128, pl.ds(r, deep, stride=lines), :] = block[:, at : at + 128]
                tile += 1
    for i in range(lanes // 128):
        out_ref[:, :, i * 128 : (i + 1) * 128] = flat_ref[i].reshape(deep, lines, 128).astype(bf16)


def depth_sums(in_ref, *outs):
    total = jnp.sum(in_ref[...].astype(f32), axis=0)
    tile = 0
    for j in range(outs[0].shape[0]):
        for ref in outs:
            for at in range(0, ref.shape[1], 128):
                r, lane = place_of(tile, total.shape[1] // 128)
                ref[j : j + 1, at : at + 128] = total[r : r + 1, lane : lane + 128]
                tile += 1


def token_result(tok_ref, cot_ref, b0_ref, b1_ref, b2_ref, b3_ref, here_ref, next_ref, wc_ref, core_ref, out_ref):
    x, y, z, d = tok_ref.shape
    coarse = (here_ref[...] + next_ref[...]).astype(bf16)
    pooled = dot_nt(jnp.broadcast_to(coarse, (8, d)), wc_ref[...])[0:1]
    pooled = (pooled / float(x * y * z))[None]
    for start, refs in zip(halves(core_ref, x), ((b0_ref, b1_ref), (b2_ref, b3_ref))):
        normed, inv_std = normalize(x_half(tok_ref, start))
        grad = join_z(*[ref[:, :d].astype(f32) for ref in refs]) + pooled
        first = jnp.mean(grad, axis=-1, keepdims=True)
        second = jnp.mean(grad * normed, axis=-1, keepdims=True)
        total = x_half(cot_ref, start) + inv_std * (grad - first - normed * second)
        out_ref[pl.ds(start, x // 2)] = total.astype(bf16).reshape(
            (x // 2,) + out_ref.shape[1:])


def passed(block, step, back=False):
    nx, nz = lax.axis_size(GX), lax.axis_size(GZ)
    route = []
    for a in range(nx):
        for c in range(nz):
            to_a, to_c = step(a, c)
            route.append((a * nz + c, to_a % nx * nz + to_c % nz))
    if back:
        route = [(b, a) for a, b in route]
    return lax.ppermute(block, ALL, route)


def to_up(a, c):
    return a, c - 1


def to_side(a, c):
    return (a - 1, c) if c % 2 == 0 else (a + 1, c)


def to_both(a, c):
    return (a - 1, c - 1) if c % 2 else (a + 1, c - 1)


def returned(own, up, side, both):
    side, both = passed(side, to_side, True), passed(both, to_both, True)
    return passed(up, to_up, True), side, both, own


def body(tokens, body_mask, cotangent, w_in, w_out, w_coarse):
    x, y, z, d = tokens.shape
    size = x * y * z
    n = size // 4
    inner = w_out.shape[0]
    coarse = lax.axis_size(GZ)
    columns = lax.axis_size(GX)
    devices = columns * coarse
    per = d // devices
    core = lax.axis_index("core")

    wide = (n, d + inner + 128)
    place = core.reshape(1, 1)
    up, side, both, own, row = call(
        prepare, [(wide, bf16)] * 4 + [((1, 2 * d), bf16)], tokens, cotangent, w_out, w_coarse, body_mask, place,
        far=range(4),
        scalars=(5,),
        grant=60,
        scratch=[pltpu.VMEM(a.shape, bf16) for a in (tokens, cotangent, w_out, w_coarse)] + [pltpu.SemaphoreType.DMA((4,))])
    before = passed(row, lambda a, c: (a + 1, c))
    side, both, up = passed(side, to_side), passed(both, to_both), passed(up, to_up)

    odd = lax.broadcasted_iota(jnp.int32, (coarse, 1), 0) % 2 == 1
    kv = jnp.where(odd, before[:, d:], row[:, d:])
    shared = jnp.concatenate([row[:, :d], before[:, :d]], axis=1)
    shared, kv = lax.optimization_barrier((shared, kv))
    other = lax.ppermute(shared, "core", [(0, 1), (1, 0)])
    kv = lax.all_to_all(kv, GZ, 0, 0, tiled=True)
    zh, nx, zl, ny, cores = (lax.axis_size(a) for a in ALL)
    plane, deep = nx * ny, zh * zl

    row = jnp.arange(d, dtype=jnp.int32)
    half, rest = row // (d // 2), row % (d // 2)
    chip, j, depth = rest // (per * deep), rest % (per * deep) // deep, rest % deep
    device = ((depth // zl * nx + chip // ny) * zl + depth % zl) * ny + chip % ny
    src = ((device * cores + (half + core) % cores) * per + j).reshape(d, 1)
    cot_turned, picked = call(
        turn_cot, [((d, size), bf16), ((8, d // 2), f32)], cotangent, src, shared, other, place, scalars=(4,))
    kv, cot_turned = lax.optimization_barrier((kv, cot_turned))

    flat, tall = (size, inner), (size + coarse, inner)
    q, k, v, g, mask, win_turned = call(
        project, [(flat, bf16)] * 4 + [((size + coarse, 128), f32), ((d, size), bf16)],
        own, up, side, both, w_in, src)
    r0, r1, r2, r3, keep, send, coarse_part = call(
        attend,
        [((n, d + inner), bf16)] * 4 + [((d // 2, 3 * inner), bf16)] * 2 + [((coarse, 4 * inner), bf16)],
        q, k, v, g, mask, w_in, kv, win_turned,
        grant=16,
        scratch=[pltpu.VMEM(s, bf16) for s in (tall, tall, flat, (size, 3 * inner))] + [pltpu.VMEM(tall, f32)] * 2)
    e0, e1, e2, e3 = returned(r0, r1, r2, r3)
    parts = lax.all_to_all(coarse_part, GZ, 0, 0, tiled=True)

    swap = [(0, 1), (1, 0)]
    other = lax.ppermute(send, "core", swap)
    cot_turned, parts, other, e0, e1, e2 = lax.optimization_barrier((cot_turned, parts, other, e0, e1, e2))
    out_keep, out_send = call(
        output_grads, [((d // 2, inner), bf16)] * 2,
        cot_turned, e0, e1, e2, e3, scratch=[pltpu.VMEM((size, inner), bf16)])
    out_other = lax.ppermute(out_send, "core", swap)
    pair, here, there = call(
        coarse_total, [((2, 4 * inner), f32), ((1, d), f32), ((1, d), f32)], parts, place, scalars=(1,))
    later = passed(there, lambda a, c: (a - 1, c))

    (packet,) = call(
        assemble, [((plane, per * deep, 4 * inner + 256), bf16)], keep, other, out_keep, out_other, pair, picked,
        scratch=[pltpu.VMEM((per * deep, 128), f32)])
    packet = lax.all_to_all(packet, ("x", "y"), 0, 0, tiled=True)
    (block_out,) = call(block_result, [(tokens.shape, bf16)], tokens, e0, e1, e2, e3, w_out, place, scalars=(6,))
    (token_grad,) = call(token_result, [(tokens.shape, bf16)], tokens, cotangent, e0, e1, e2, e3,
        here, later, w_coarse, place, scalars=(9,))
    packet, block_out, token_grad = lax.optimization_barrier((packet, block_out, token_grad))
    tiles = -(-per * 6 * inner // 1024)
    (slab,) = call(
        plane_sums, [((deep, 8, tiles * 128), bf16)], packet, scratch=[pltpu.VMEM((tiles, deep * 8, 128), f32)])
    slab = lax.all_to_all(slab, ("zh", "zl"), 0, 0, tiled=True)

    input_grad, output_grad, coarse_grad = call(
        depth_sums, [((per, 3 * inner), f32), ((per, inner), f32), ((per, 2 * inner), f32)], slab)
    output_grad = output_grad.T
    return (block_out, token_grad, input_grad, output_grad, coarse_grad)


def solution(mesh):
    fine = Mesh(mesh.devices.reshape(2, 4, 4, 4, 2), ALL)
    grid = P(GX, None, GZ, None)
    return jax.shard_map(
        body,
        mesh=fine,
        in_specs=(grid, P(GX, None, GZ), grid, P(), P(), P()),
        out_specs=(grid, grid, P(ALL, None), P(None, ALL), P(ALL, None)),
        check_vma=False,
    )
```
